32 devices in a mesh: dp: 8 (over z, x), rep: 4 (over y, core).
Axes of the slice: x: 2, y: 2, z: 4, core: 2. Of those that a mesh axis runs over, the one named last changes fastest.
Arguments:
- tokens: bfloat16 [32, 320, 1024], P(('dp', 'rep')), may hold values from -6 to 6
- cotangent: bfloat16 [32, 320, 1024], P(('dp', 'rep')), may hold values from -6 to 6
- lengths: int32 [32], P(('dp', 'rep')), may hold values from 1 to 320, 7680 in all
- norm_gain: float32 [1024], replicated, may hold values from 0.5 to 1.5
- in_weight: bfloat16 [1024, 4096], replicated, may hold values from -0.1875 to 0.1875
- conv_weight: float32 [4, 2048], replicated, may hold values from -3 to 3
- conv_bias: float32 [2048], replicated, may hold values from -3 to 3
- xproj_weight: bfloat16 [2048, 96], replicated, may hold values from -0.125 to 0.125
- dt_weight: bfloat16 [64, 2048], replicated, may hold values from -0.75 to 0.75
- dt_bias: float32 [2048], replicated, may hold values from -4.5 to -1.5
- decay_log: float32 [16, 2048], replicated, may hold values from 0 to 2.5
- skip_gain: float32 [2048], replicated, may hold values from 0.5 to 1.5
- out_weight: bfloat16 [2048, 1024], replicated, may hold values from -0.25 to 0.25
Outputs:
- mixed: bfloat16 [32, 320, 1024], P(('dp', 'rep'))
- grad_tokens: float32 [32, 320, 1024], P(('dp', 'rep'))
- grad_norm_gain: float32 [1024], replicated
- grad_in_weight: float32 [1024, 4096], replicated
- grad_conv_weight: float32 [4, 2048], replicated
- grad_conv_bias: float32 [2048], replicated
- grad_xproj_weight: float32 [2048, 96], replicated
- grad_dt_weight: float32 [64, 2048], replicated
- grad_dt_bias: float32 [2048], replicated
- grad_decay_log: float32 [16, 2048], replicated
- grad_skip_gain: float32 [2048], replicated
- grad_out_weight: float32 [2048, 1024], replicated
The draws below stay inside these ranges and needn't reach their ends.
Inputs may be any that keep to these rules, and one draw needn't show every extreme that they name: `lengths`: live length of each slot; the largest is exactly 320.
All inputs are finite; a program needn't handle non-finite values. No bound on the sum of `lengths` on one device may be relied on, other than what follows from the above.
Results may differ from the reference program's by a relative error of at most 0.012.
Values sent between devices are 32-bit elements; how exact they have to be, the bound alone decides.
No kernel may reach another device: no remote copies, remote signals or barrier semaphores. Data moves between devices by JAX's collectives and lax.ppermute only.
A program may use at most 256 MiB of HBM per device.

```python
import math
import jax
import jax.numpy as jnp
import numpy as np
from jax import lax

D = 1024
INNER = 2048
STATE = 16
RANK = 64
CONV = 4
BLOCK = 64
SLOT_LEN = 320
SLOTS = 32


def shard_levels(rng, extent, cuts, smallest, largest):
    factor_of = 1.0
    for dim, parts in cuts:
        draws = jax.random.uniform(jax.random.fold_in(jax.random.fold_in(rng, 6), dim), (parts,), jnp.float32, smallest / len(cuts), largest / len(cuts))
        factor_of = factor_of * jnp.repeat(jnp.exp(draws), extent[dim] // parts).reshape((-1,) + (1,) * (len(extent) - 1 - dim))
    return factor_of


def profile(number_of, total, bound, slope):
    loads = [(1 << 20) // math.isqrt(standing ** slope) + 1 for standing in range(2, number_of + 1)]
    rest, given = total - bound - (number_of - 1), [1] * (number_of - 1)
    while rest > 0:
        free = [i for i in range(number_of - 1) if given[i] < bound]
        mass, remaining = sum([loads[i] for i in free]), rest
        for i in free:
            extra = min(bound - given[i], max(1, remaining * loads[i] // mass), rest)
            given[i] = given[i] + extra
            rest = rest - extra
    return np.array([bound] + given)


def uneven(stream_key, number_of, total, bound, slope):
    if number_of == 2:
        one = jax.random.randint(stream_key, (), max(1, total - bound), min(bound, total - 1) + 1)
        return jnp.stack([one, total - one])
    sizes = jnp.asarray(profile(number_of, total, bound, slope), jnp.int32)
    twos = (number_of - 1) // 2
    source_of, receiver = sizes[1:1 + 2 * twos:2], sizes[2:2 + 2 * twos:2]
    slack = jnp.minimum(source_of - 1, bound - receiver)
    shifted = jax.random.randint(jax.random.fold_in(stream_key, 1), (twos,), 0, 1 << 20) % (slack + 1)
    sizes = sizes.at[1:1 + 2 * twos:2].set(source_of - shifted).at[2:2 + 2 * twos:2].set(receiver + shifted)
    return sizes[jax.random.permutation(jax.random.fold_in(stream_key, 2), number_of)]


def noise(own_key, shape, spread, most, cuts=(), dtype=jnp.bfloat16):
    values = jax.random.normal(own_key, shape, jnp.float32) * spread
    if len(cuts) > 0:
        values = shard_levels(own_key, shape, cuts, -0.22, 0.18) * values
    return jnp.clip(values, min=-most, max=most).astype(dtype)


def setup_inputs(seed: int = 0) -> dict:
    arg_keys = jax.random.split(jax.random.key(seed), 14)
    tokens = noise(arg_keys[0], (SLOTS, SLOT_LEN, D), 1.0, 6.0, ((0, 32),))
    cotangent = noise(arg_keys[1], (SLOTS, SLOT_LEN, D), 1.0, 6.0, ((0, 32),))
    lengths = uneven(arg_keys[2], SLOTS, SLOTS * SLOT_LEN * 3 // 4, SLOT_LEN, 2).astype(jnp.int32)
    norm_gain = jnp.clip(1.0 + 0.1 * jax.random.normal(arg_keys[3], (D,), jnp.float32), 0.5, 1.5)
    in_weight = noise(arg_keys[4], (D, 2 * INNER), D ** -0.5, 0.1875)
    conv_weight = noise(arg_keys[5], (CONV, INNER), CONV ** -0.5, 3.0, (), jnp.float32)
    conv_bias = noise(arg_keys[6], (INNER,), 0.5, 3.0, (), jnp.float32)
    xproj_weight = noise(arg_keys[7], (INNER, RANK + 2 * STATE), INNER ** -0.5, 0.125)
    dt_weight = noise(arg_keys[8], (RANK, INNER), RANK ** -0.5, 0.75)
    dt_bias = jnp.clip(jax.random.uniform(arg_keys[9], (INNER,), jnp.float32, -4.5, -1.5), -4.5, -1.5)
    decay_log = jnp.clip(jax.random.uniform(arg_keys[10], (STATE, INNER), jnp.float32, 0.0, 2.5), 0.0, 2.5)
    skip_gain = jnp.clip(jax.random.uniform(arg_keys[11], (INNER,), jnp.float32, 0.5, 1.5), 0.5, 1.5)
    out_weight = noise(arg_keys[12], (INNER, D), (INNER // 4) ** -0.5, 0.25)
    return {"tokens": tokens, "cotangent": cotangent, "lengths": lengths, "norm_gain": norm_gain, "in_weight": in_weight, "conv_weight": conv_weight, "conv_bias": conv_bias, "xproj_weight": xproj_weight, "dt_weight": dt_weight, "dt_bias": dt_bias, "decay_log": decay_log, "skip_gain": skip_gain, "out_weight": out_weight}


@jax.custom_vjp
def low(v):
    return lax.optimization_barrier(v.astype(jnp.bfloat16)).astype(jnp.float32)

@jax.custom_vjp
def low_back(v):
    return v

def low_keep(v):
    return (low(v), None)

def low_pass(kept, grad):
    return (grad,)

def back_keep(v):
    return (v, None)

def back_low(kept, grad):
    return (low(grad),)
low.defvjp(low_keep, low_pass)
low_back.defvjp(back_keep, back_low)
epsilon = 1e-05
highest = lax.Precision.HIGHEST

def matmul(left, right):
    return jnp.dot(left, right, precision=highest, preferred_element_type=jnp.float32)

def combine_pairs(earlier, later):
    return (earlier[0] * later[0], later[0] * earlier[1] + later[1])

def scan_block(carried, delta_blk, inputs_blk, write_blk, read_blk, decay_rates):
    factors = jnp.exp(delta_blk[:, None, :] * decay_rates[None, :, :])
    drives = (delta_blk * inputs_blk)[:, None, :] * write_blk[:, :, None]
    first_row = drives[:1] + factors[:1] * carried[None]
    drives = jnp.concatenate([first_row, drives[1:]], axis=0)
    totals = lax.associative_scan(combine_pairs, (factors, drives), axis=0)[1]
    outputs = lax.optimization_barrier(jnp.sum(totals * read_blk[:, :, None], axis=1))
    return (totals[-1], outputs)

def selective_scan(step_size, inputs, write_coef, read_coef, decay_rates):
    length = step_size.shape[0]
    count = length // BLOCK
    blocked = tuple((member.reshape(count, BLOCK, member.shape[1]) for member in (step_size, inputs, write_coef, read_coef)))

    def one_block(carried, pieces):
        return scan_block(carried, pieces[0], pieces[1], pieces[2], pieces[3], decay_rates)
    start = jnp.zeros((STATE, step_size.shape[1]), jnp.float32)
    final_state, outputs = lax.scan(jax.checkpoint(one_block), start, blocked)
    return outputs.reshape(length, step_size.shape[1])

def layer(token_row, mask_row, params):
    norm_gain, in_weight, conv_weight, conv_bias, xproj_weight, dt_weight, dt_bias, decay_log, skip_gain, out_weight = params
    length = token_row.shape[0]
    mean_square = lax.optimization_barrier(jnp.mean(token_row * token_row, axis=1, keepdims=True))
    normed = low(token_row * lax.rsqrt(mean_square + epsilon) * norm_gain)
    projected = low_back(matmul(normed, in_weight))
    inner = projected[:, :INNER]
    gate_pre = projected[:, INNER:]
    padded = jnp.concatenate([jnp.zeros((CONV - 1, INNER), jnp.float32), inner], axis=0)
    conv_out = conv_bias + sum((conv_weight[offset] * padded[offset:offset + length] for offset in range(CONV)))
    activated = low(jax.nn.silu(conv_out))
    mixed_proj = low_back(matmul(activated, xproj_weight))
    delta_in = low(mixed_proj[:, :RANK])
    write_coef = mixed_proj[:, RANK:RANK + STATE]
    read_coef = mixed_proj[:, RANK + STATE:]
    delta_lin = low_back(matmul(delta_in, dt_weight))
    step_size = jax.nn.softplus(delta_lin + dt_bias)
    decay_rates = -jnp.exp(decay_log)
    summed = selective_scan(step_size, activated, write_coef, read_coef, decay_rates) + skip_gain * activated
    branch = low(summed * jax.nn.silu(gate_pre))
    return token_row + mask_row * matmul(branch, out_weight)

def reference(tokens, cotangent, lengths, norm_gain, in_weight, conv_weight, conv_bias, xproj_weight, dt_weight, dt_bias, decay_log, skip_gain, out_weight):
    weights = tuple((member.astype(jnp.float32) for member in (norm_gain, in_weight, conv_weight, conv_bias, xproj_weight, dt_weight, dt_bias, decay_log, skip_gain, out_weight)))
    positions = jnp.arange(SLOT_LEN)
    zeros = tuple((jnp.zeros(member.shape, jnp.float32) for member in weights))

    def per_slot(totals, slot):
        token_row, cotangent_row, length_row = slot
        mask_row = (positions < length_row).astype(jnp.float32)[:, None]

        def forward(row_input, params):
            return layer(row_input, mask_row, params)
        output, pullback = jax.vjp(forward, token_row.astype(jnp.float32), weights)
        grad_row, grad_params = pullback(cotangent_row.astype(jnp.float32))
        totals = jax.tree.map(jnp.add, totals, grad_params)
        return (totals, (output.astype(jnp.bfloat16), grad_row))
    totals, outputs = lax.scan(per_slot, zeros, (tokens, cotangent, lengths))
    mixed, grad_tokens = outputs
    return (mixed, grad_tokens, totals[0], totals[1], totals[2], totals[3], totals[4], totals[5], totals[6], totals[7], totals[8], totals[9])
```

```python
import functools
import math
import jax
import jax.numpy as jnp
from jax import lax
from jax.experimental import pallas as pl
from jax.experimental.pallas import tpu as pltpu
from jax.sharding import PartitionSpec as P

F32 = jnp.float32
BF16 = jnp.bfloat16
EPS = 1e-05
LANES = 128
SUB = 8
WIDE = 1024
SEG = 16
VMEM = 60 * 1024 * 1024
LOG2E = math.log2(math.e)
CHEAP = pl.CostEstimate(flops=0, bytes_accessed=0, transcendentals=0)


def dot(a, b, dims=((1,), (0,))):
    return lax.dot_general(a, b, (dims, ((), ())), preferred_element_type=F32)


def shifted(value, rows):
    if rows == 0:
        return value
    length = value.shape[0]
    index = lax.broadcasted_iota(jnp.int32, value.shape, 0)
    moved = pltpu.roll(value, rows % length, 0)
    keep = index >= rows if rows > 0 else index < length + rows
    return jnp.where(keep, moved, 0.0)


def conv_of(inner, cw_ref, cb_ref):
    taps = cw_ref.shape[0]
    total = cb_ref[...] + cw_ref[taps - 1 : taps, :] * inner
    for k in range(taps - 1):
        total = total + cw_ref[k : k + 1, :] * shifted(inner, taps - 1 - k)
    return total


def front_kernel(
    len_ref, tok_ref, cot_ref, gain_ref, w_ref, cw_ref, cb_ref, xp_ref,
    normed_ref, send_ref, og_ref, inner_ref, act_ref, mp_ref,
):
    @pl.when(pl.program_id(0) == 0)
    def _():
        x = tok_ref[...].astype(F32)
        inv = lax.rsqrt(jnp.mean(x * x, axis=1, keepdims=True) + EPS)
        normed = (x * inv * gain_ref[...]).astype(BF16)
        normed_ref[...] = normed
        low = x.shape[1] // 2
        send_ref[...] = jnp.where(len_ref[1] == 0, normed[:, low:], normed[:, :low]).astype(F32)
        row = lax.broadcasted_iota(jnp.int32, x.shape, 0)
        og_ref[...] = jnp.where(row < len_ref[0], cot_ref[...].astype(F32), 0.0)
        mp_ref[...] = jnp.zeros_like(mp_ref)

    inner = dot(normed_ref[...], w_ref[...])
    inner_ref[...] = inner
    conv = conv_of(inner, cw_ref, cb_ref)
    act = (conv * jax.nn.sigmoid(conv)).astype(BF16)
    act_ref[...] = act
    mp_ref[...] += dot(act, xp_ref[...], ((1,), (1,)))


def front(tokens, cot, lengths, gain, in_weight, cw, cb, xproj):
    length, model = tokens.shape
    width = cw.shape[1]
    cols = xproj.shape[0]
    blk = 256
    whole = lambda shape: pl.BlockSpec(shape, lambda j: (0, 0))
    part = lambda rows: pl.BlockSpec((rows, blk), lambda j: (0, j))
    return pl.pallas_call(
        front_kernel,
        grid=(width // blk,),
        in_specs=[
            pl.BlockSpec(memory_space=pltpu.SMEM),
            whole((length, model)), whole((length, model)), whole((1, model)),
            part(model), part(cw.shape[0]), part(1),
            part(cols),
        ],
        out_specs=[
            whole((length, model)), whole((length, model // 2)), whole((length, model)),
            part(length), part(length), whole((length, cols)),
        ],
        out_shape=[
            jax.ShapeDtypeStruct((length, model), BF16),
            jax.ShapeDtypeStruct((length, model // 2), F32),
            jax.ShapeDtypeStruct((length, model), F32),
            jax.ShapeDtypeStruct((length, width), F32),
            jax.ShapeDtypeStruct((length, width), BF16),
            jax.ShapeDtypeStruct((length, cols), F32),
        ],
        compiler_params=pltpu.CompilerParams(vmem_limit_bytes=VMEM),
        cost_estimate=CHEAP,
        name="front",
    )(lengths, tokens, cot, gain, in_weight, cw, cb, xproj)


def splat_rows(length, count):
    return -(-length // LANES) * count * LANES


def fill_splats(mp_ref, splat_ref, first, count):
    length, cols = mp_ref.shape
    for g in range(-(-length // LANES)):
        size = min(LANES, length - g * LANES)
        rows = mp_ref[pl.ds(g * LANES, size), :]
        rows = jnp.concatenate([rows, jnp.zeros((size, LANES - cols), F32)], axis=1)
        if size < LANES:
            rows = jnp.concatenate([rows, jnp.zeros((LANES - size, LANES), F32)], axis=0)
        turned = rows.T
        for n in range(count):
            line = jnp.broadcast_to(turned[first + n : first + n + 1, :], (LANES, LANES))
            splat_ref[pl.ds((g * count + n) * LANES, size), :] = line.T[:size]


def splat(splat_ref, tb, count, n, s):
    per = LANES // SUB
    row = tb // per * (count * LANES) + tb % per * SUB + (n * LANES + s)
    return jnp.broadcast_to(splat_ref[pl.ds(row, 1), :], (SUB, LANES))


def tile_rows(tb, s):
    return pl.ds(pl.multiple_of(tb * SUB * SUB, SUB * SUB) + s, SUB, stride=SUB)


def put_tiles(ref, j, value):
    for tb in range(value.shape[0] // SUB):
        ref[pl.ds(tb * SUB * SUB + j * SUB, SUB), :] = value[tb * SUB : (tb + 1) * SUB, :]


def get_tiles(ref, j, length):
    return jnp.concatenate(
        [ref[pl.ds(tb * SUB * SUB + j * SUB, SUB), :] for tb in range(length // SUB)], axis=0
    )


def scan_kernel(
    core_ref, mp_ref, normed_ref, og_ref, act_ref, wg_ref, wo_ref, dtw_ref, dtb_ref, dlog_ref, skip_ref,
    branch_ref, send_ref, ggp_ref, gs_ref, step_ref, mark_ref,
    splat_ref, u_ref, y_ref, a_ref, gate_ref, gb_ref,
):
    length = mp_ref.shape[0]
    rank = dtw_ref.shape[0]
    states = a_ref.shape[0]
    both = 2 * states
    fill_splats(mp_ref, splat_ref, rank, both)
    a_ref[...] = -jnp.exp(dlog_ref[...]) * LOG2E
    delta_in = mp_ref[:, :rank].astype(BF16)
    for j in range(WIDE // LANES):
        cols = pl.ds(j * LANES, LANES)
        pre = dot(delta_in, dtw_ref[:, cols]) + dtb_ref[:, cols]
        step = jnp.maximum(pre, 0.0) + jnp.log1p(jnp.exp(-jnp.abs(pre)))
        put_tiles(step_ref, j, step)
        put_tiles(u_ref, j, step * act_ref[:, cols].astype(F32))

    def body(tb, carry):
        h = list(carry)
        @pl.when(tb % (SEG // SUB) == 0)
        def _():
            base = pl.multiple_of((tb // (SEG // SUB)) * states * SUB, states * SUB)
            for n in range(states):
                mark_ref[pl.ds(base + n * SUB, SUB), :] = h[n]
        for s in range(SUB):
            step = step_ref[tile_rows(tb, s), :]
            u = u_ref[tile_rows(tb, s), :]
            y = None
            for n in range(states):
                f = jnp.exp2(step * a_ref[n])
                h[n] = f * h[n] + u * splat(splat_ref, tb, both, n, s)
                q = h[n] * splat(splat_ref, tb, both, states + n, s)
                y = q if y is None else y + q
            y_ref[tile_rows(tb, s), :] = y
        return tuple(h)

    zero = jnp.zeros((SUB, LANES), F32)
    lax.fori_loop(0, length // SUB, body, (zero,) * states)

    og = og_ref[...].astype(BF16)
    for k in range(WIDE // 256):
        cols = pl.ds(k * 256, 256)
        gate_ref[:, cols] = dot(normed_ref[...], wg_ref[:, cols])
        gb_ref[:, cols] = dot(og, wo_ref[cols, :], ((1,), (1,)))
    for j in range(WIDE // LANES):
        cols = pl.ds(j * LANES, LANES)
        gate = gate_ref[:, cols]
        gb = gb_ref[:, cols]
        summed = get_tiles(y_ref, j, length) + skip_ref[:, cols] * act_ref[:, cols].astype(F32)
        sig = jax.nn.sigmoid(gate)
        gate_act = gate * sig
        branch = (summed * gate_act).astype(BF16)
        branch_ref[:, cols] = branch
        into = pl.ds(j * LANES % (WIDE // 2), LANES)

        @pl.when((core_ref[0] == 0) == (j * LANES >= WIDE // 2))
        def _():
            send_ref[:, into] = branch.astype(F32)
        put_tiles(gs_ref, j, gb * gate_act)
        ggp_ref[:, cols] = gb * summed * (sig * (1.0 + gate * (1.0 - sig)))


def scan(block, core, mp, normed, og, act, in_weight, out_weight, dtw, dtb, dlog, skip):
    length, model = normed.shape
    width = act.shape[1]
    rank = dtw.shape[0]
    states = dlog.shape[0]
    count = width // WIDE
    whole = lambda shape: pl.BlockSpec(shape, lambda i: (0,) * len(shape))
    col = lambda rows, at: pl.BlockSpec((rows, WIDE), lambda i: (0, at))
    tiles = jax.ShapeDtypeStruct((length * SUB, LANES), F32)
    marks = (length // SEG) * states * SUB
    flat = jax.ShapeDtypeStruct((length, WIDE), F32)
    return pl.pallas_call(
        scan_kernel,
        grid=(1,),
        in_specs=[
            pl.BlockSpec(memory_space=pltpu.SMEM), whole(mp.shape), whole(normed.shape), whole(og.shape), col(length, block),
            col(model, count + block), pl.BlockSpec((WIDE, model), lambda i: (block, 0)),
            col(rank, block), col(1, block),
            pl.BlockSpec((states, SUB, LANES), lambda i: (0, block, 0)), col(1, block),
        ],
        out_specs=[whole(flat.shape), whole((length, WIDE // 2)), whole(flat.shape), whole(tiles.shape), whole(tiles.shape), whole((marks, LANES))],
        out_shape=[jax.ShapeDtypeStruct(flat.shape, BF16), jax.ShapeDtypeStruct((length, WIDE // 2), F32), flat, tiles, tiles, jax.ShapeDtypeStruct((marks, LANES), F32)],
        scratch_shapes=[
            pltpu.VMEM((splat_rows(length, 2 * states), LANES), F32),
            pltpu.VMEM((length * SUB, LANES), F32),
            pltpu.VMEM((length * SUB, LANES), F32),
            pltpu.VMEM((states, SUB, LANES), F32),
            pltpu.VMEM((length, WIDE), F32),
            pltpu.VMEM((length, WIDE), F32),
        ],
        compiler_params=pltpu.CompilerParams(vmem_limit_bytes=VMEM),
        cost_estimate=CHEAP,
        name=f"scan{block}",
    )(core, mp, normed, og, act, in_weight, out_weight, dtw, dtb, dlog, skip)


def back_kernel(
    mp_ref, act_ref, step_ref, gs_ref, mark_ref, dtw_ref, dlog_ref,
    gact_ref, glin_ref, gdelta_ref, gdtw_ref, gwr_ref, gdlog_ref, rows_ref,
    splat_ref, act_t_ref, gd_ref, gu_ref, a_ref, f_ref, h_ref, carry_ref, turn_ref, part_ref,
):
    length = mp_ref.shape[0]
    rank = dtw_ref.shape[0]
    states = a_ref.shape[0]
    both = 2 * states
    fill_splats(mp_ref, splat_ref, rank, both)
    rate = -jnp.exp(dlog_ref[...])
    a_ref[...] = rate
    for j in range(WIDE // LANES):
        put_tiles(act_t_ref, j, act_ref[:, pl.ds(j * LANES, LANES)].astype(F32))
    per = SEG // SUB

    groups = states // SUB
    carry_ref[...] = jnp.zeros_like(carry_ref)

    def segment(i, _):
        seg = length // SEG - 1 - i
        for q in range(groups):
            mine = range(q * SUB, (q + 1) * SUB)
            rates = [a_ref[n] for n in mine]
            base = pl.multiple_of(seg * states * SUB, states * SUB)
            start = [mark_ref[pl.ds(base + n * SUB, SUB), :] for n in mine]
            for j in range(SUB):
                h_ref[0, j] = start[j]

            def again(k, hs):
                hs = list(hs)
                tb = seg * per + k
                for s in range(SUB):
                    step = step_ref[tile_rows(tb, s), :]
                    u = step * act_t_ref[tile_rows(tb, s), :]
                    step2 = step * LOG2E
                    for j, n in enumerate(mine):
                        f = jnp.exp2(step2 * rates[j])
                        f_ref[k * SUB + s, j] = f
                        hs[j] = f * hs[j] + u * splat(splat_ref, tb, both, n, s)
                        h_ref[k * SUB + s + 1, j] = hs[j]
                return tuple(hs)

            last = lax.fori_loop(0, per, again, tuple(start))

            def reverse(k2, carry):
                dhs, gas, now = (list(c) for c in carry)
                k = per - 1 - k2
                tb = seg * per + k
                for s in reversed(range(SUB)):
                    g = gs_ref[tile_rows(tb, s), :]
                    step = step_ref[tile_rows(tb, s), :]
                    u = step * act_t_ref[tile_rows(tb, s), :]
                    gd = gu = None
                    ws, rs = [], []
                    for j, n in enumerate(mine):
                        dh = dhs[j] + g * splat(splat_ref, tb, both, states + n, s)
                        before = h_ref[k * SUB + s, j]
                        rs.append(now[j] * g)
                        ws.append(dh * u)
                        t = dh * splat(splat_ref, tb, both, n, s)
                        gu = t if gu is None else gu + t
                        dhs[j] = dh * f_ref[k * SUB + s, j]
                        ga = dhs[j] * before
                        t = ga * rates[j]
                        gd = t if gd is None else gd + t
                        gas[j] = gas[j] + ga * step
                        now[j] = before
                    if q == 0:
                        gd_ref[tile_rows(tb, s), :] = gd
                        gu_ref[tile_rows(tb, s), :] = gu
                    else:
                        gd_ref[tile_rows(tb, s), :] = gd_ref[tile_rows(tb, s), :] + gd
                        gu_ref[tile_rows(tb, s), :] = gu_ref[tile_rows(tb, s), :] + gu
                    for slot, values in ((0, ws), (1, rs)):
                        at = (s * 2 + slot) * SUB * SUB
                        for j in range(SUB):
                            turn_ref[pl.ds(at + j * SUB, SUB), :] = values[j]
                        total = turn_ref[pl.ds(at, SUB, stride=SUB), :]
                        for j in range(1, SUB):
                            total = total + turn_ref[pl.ds(at + j, SUB, stride=SUB), :]
                        row = tb * (both * SUB) + (slot * states + q * SUB) * SUB + s
                        part_ref[pl.ds(row, SUB, stride=SUB), :] = total
                return (tuple(dhs), tuple(gas), tuple(now))

            begin = (
                tuple(carry_ref[0, n] for n in mine), tuple(carry_ref[1, n] for n in mine), last
            )
            dhs, gas, _ = lax.fori_loop(0, per, reverse, begin)
            for j, n in enumerate(mine):
                carry_ref[0, n] = dhs[j]
                carry_ref[1, n] = gas[j]
        return 0

    lax.fori_loop(0, length // SEG, segment, 0)
    for n in range(states):
        gdlog_ref[n] = carry_ref[1, n] * rate[n]

    row = lax.broadcasted_iota(jnp.int32, (2 * LANES, LANES), 0)
    lane = lax.broadcasted_iota(jnp.int32, (2 * LANES, LANES), 1)
    gwr = None
    for n in range(0, both, 2):
        pieces = []
        for k in range(2):
            pieces.append(jnp.concatenate(
                [part_ref[pl.ds((tb * both + n + k) * SUB, SUB), :] for tb in range(length // SUB)], axis=0
            ).astype(BF16))
        into = jnp.where(lane == rank + n + row // LANES, 1.0, 0.0).astype(BF16)
        term = dot(jnp.concatenate(pieces, axis=1), into)
        gwr = term if gwr is None else gwr + term
    gwr_ref[...] = gwr

    for j in range(WIDE // LANES):
        cols = pl.ds(j * LANES, LANES)
        act = act_ref[:, cols].astype(F32)
        step = get_tiles(step_ref, j, length)
        gs = get_tiles(gs_ref, j, length)
        gu = get_tiles(gu_ref, j, length)
        gstep = get_tiles(gd_ref, j, length) + gu * act
        gpre = gstep * (1.0 - jnp.exp(-step))
        glin_ref[:, cols] = gpre.astype(BF16)
        rows_ref[0:1, cols] = jnp.sum(gpre, axis=0, keepdims=True)
        rows_ref[1:2, cols] = jnp.sum(gs * act, axis=0, keepdims=True)
        gact_ref[:, cols] = gu * step
    delta_in = mp_ref[:, :rank].astype(BF16)
    gdtw_ref[...] = dot(delta_in, glin_ref[...], ((0,), (0,)))
    gdelta_ref[...] = dot(glin_ref[...], dtw_ref[...], ((1,), (1,)))


def back(block, mp, act, step, gs, marks, dtw, dlog):
    length = act.shape[0]
    rank = dtw.shape[0]
    states = dlog.shape[0]
    whole = lambda shape: pl.BlockSpec(shape, lambda i: (0,) * len(shape))
    col = lambda rows, at: pl.BlockSpec((rows, WIDE), lambda i: (0, at))
    flat = jax.ShapeDtypeStruct((length, WIDE), F32)
    outs = [
        flat,
        jax.ShapeDtypeStruct((length, WIDE), BF16),
        jax.ShapeDtypeStruct((length, rank), F32),
        jax.ShapeDtypeStruct((rank, WIDE), F32),
        jax.ShapeDtypeStruct((length, LANES), F32),
        jax.ShapeDtypeStruct((states, SUB, LANES), F32),
        jax.ShapeDtypeStruct((2, WIDE), F32),
    ]
    tiles = pltpu.VMEM((length * SUB, LANES), F32)
    return pl.pallas_call(
        back_kernel,
        grid=(1,),
        in_specs=[
            whole(mp.shape), col(length, block), whole(step.shape), whole(gs.shape), whole(marks.shape),
            col(rank, block), pl.BlockSpec((states, SUB, LANES), lambda i: (0, block, 0)),
        ],
        out_specs=[whole(o.shape) for o in outs],
        out_shape=outs,
        scratch_shapes=[
            pltpu.VMEM((splat_rows(length, 2 * states), LANES), F32),
            tiles, tiles, tiles,
            pltpu.VMEM((states, SUB, LANES), F32),
            pltpu.VMEM((SEG, SUB, SUB, LANES), F32),
            pltpu.VMEM((SEG + 1, SUB, SUB, LANES), F32),
            pltpu.VMEM((2, states, SUB, LANES), F32),
            pltpu.VMEM((2 * SUB * SUB * SUB, LANES), F32),
            pltpu.VMEM((length * 2 * states, LANES), F32),
        ],
        compiler_params=pltpu.CompilerParams(vmem_limit_bytes=VMEM),
        cost_estimate=CHEAP,
        name=f"back{block}",
    )(mp, act, step, gs, marks, dtw, dlog)


def post_kernel(
    gmix_ref, gs_ref, gact_ref, act_ref, inner_ref, xp_ref, cw_ref, cb_ref, skip_ref, gdtw_ref, gdlog_ref, two_ref,
    gi_ref, small_ref,
):
    length = act_ref.shape[0]
    taps = cw_ref.shape[0]
    share = dot(gmix_ref[...], xp_ref[...])
    sizes = [xp_ref.shape[0], gdtw_ref.shape[0], gdlog_ref.shape[0], two_ref.shape[0]]
    ends = [sum(sizes[: i + 1]) for i in range(4)]
    small_ref[: ends[0], :] = dot(gmix_ref[...], act_ref[...], ((0,), (0,)))
    small_ref[ends[0] : ends[1], :] = gdtw_ref[...]
    small_ref[ends[1] : ends[2], :] = gdlog_ref[...]
    small_ref[ends[2] : ends[3], :] = two_ref[...]
    small_ref[ends[3] + taps + 1 :, :] = jnp.zeros((small_ref.shape[0] - ends[3] - taps - 1, WIDE), F32)
    for j in range(WIDE // LANES):
        cols = pl.ds(j * LANES, LANES)
        inner = inner_ref[:, cols]
        cw = cw_ref[:, cols]
        conv = conv_of(inner, cw, cb_ref[:, cols])
        sig = jax.nn.sigmoid(conv)
        gact = (
            get_tiles(gs_ref, j, length) * skip_ref[:, cols]
            + gact_ref[:, cols]
            + share[:, j * LANES : (j + 1) * LANES]
        )
        gconv = gact * (sig * (1.0 + conv * (1.0 - sig)))
        at = ends[3]
        small_ref[at + taps : at + taps + 1, cols] = jnp.sum(gconv, axis=0, keepdims=True)
        total = None
        for k in range(taps):
            small_ref[at + k : at + k + 1, cols] = jnp.sum(
                gconv * shifted(inner, taps - 1 - k), axis=0, keepdims=True
            )
            term = cw[k : k + 1, :] * shifted(gconv, k + 1 - taps)
            total = term if total is None else total + term
        gi_ref[:, cols] = total


def post(block, lines, gmix, gs, gact, act, inner, xproj, cw, cb, skip, gdtw, gdlog, two):
    length = act.shape[0]
    cols = xproj.shape[0]
    taps = cw.shape[0]
    whole = lambda shape: pl.BlockSpec(shape, lambda i: (0,) * len(shape))
    col = lambda rows, at: pl.BlockSpec((rows, WIDE), lambda i: (0, at))
    outs = [jax.ShapeDtypeStruct((length, WIDE), F32), jax.ShapeDtypeStruct((lines, WIDE), F32)]
    return pl.pallas_call(
        post_kernel,
        grid=(1,),
        in_specs=[
            whole(gmix.shape), whole(gs.shape), whole(gact.shape), col(length, block), col(length, block),
            col(cols, block), col(taps, block), col(1, block), col(1, block),
            whole(gdtw.shape), whole(gdlog.shape), whole(two.shape),
        ],
        out_specs=[whole(o.shape) for o in outs],
        out_shape=outs,
        compiler_params=pltpu.CompilerParams(vmem_limit_bytes=VMEM),
        cost_estimate=CHEAP,
        name=f"post{block}",
    )(gmix, gs, gact, act, inner, xproj, cw, cb, skip, gdtw, gdlog, two)


def outer(core, own, other, rows, small=()):
    length = own[0][0].shape[0]
    low, cols = own[0][0].shape[1] // 2, own[0][1].shape[1]
    per = 2
    blk = low // per
    ins, specs = [], []
    for c in range(2):
        at = lambda i, c=c: jnp.clip(i - c * per, 0, per - 1)
        ins += [own[c][0], other[c][0], own[c][1], other[c][1]]
        specs += [
            pl.BlockSpec((length, blk), lambda i, ix, at=at: (0, ix[0] * per + at(i))),
            pl.BlockSpec((length, blk), lambda i, ix, at=at: (0, at(i))),
            pl.BlockSpec((length, cols), lambda i, ix: (0, 0)),
            pl.BlockSpec((length, cols), lambda i, ix: (0, 0)),
        ]
    ins += list(small)
    specs += [pl.BlockSpec(v.shape, lambda i, ix: (0, 0)) for v in small]
    rest = rows - 2 * low
    total = 2 * low + (rest > 0) * blk * -(-rest // blk)

    def body(ix, *refs):
        out = refs[-1]
        step = pl.program_id(0)
        for c in range(2):
            @pl.when((step >= c * per) & (step < (c + 1) * per))
            def _():
                l, lo, r, ro = [ref[...].astype(BF16) for ref in refs[4 * c : 4 * c + 4]]
                out[...] = dot(l, r, ((0,), (0,))) + dot(lo, ro, ((0,), (0,)))

        @pl.when(step >= 2 * per)
        def _():
            out[...] = jnp.zeros_like(out)
            if small:
                a, b, got = refs[8:11]
                out[: got.shape[0], :] = jnp.where(ix[0] == 0, a[...], b[...]) + got[...]

    return pl.pallas_call(
        body,
        out_shape=jax.ShapeDtypeStruct((rows, cols), F32),
        grid_spec=pltpu.PrefetchScalarGridSpec(
            num_scalar_prefetch=1, grid=(total // blk,), in_specs=specs,
            out_specs=pl.BlockSpec((blk, cols), lambda i, ix: (i, 0)),
        ),
        compiler_params=pltpu.CompilerParams(vmem_limit_bytes=VMEM),
        cost_estimate=CHEAP,
        name="outer",
    )(core, *ins)


def blank(shape):
    return pl.pallas_call(
        lambda ref: None, out_shape=jax.ShapeDtypeStruct(shape, F32),
        out_specs=pl.BlockSpec(memory_space=pltpu.HBM), name="blank",
        compiler_params=pltpu.CompilerParams(vmem_limit_bytes=VMEM), cost_estimate=CHEAP,
    )()


def put(targets, pieces, spans, flags):
    arrays = [p[0] for p in pieces]
    n = len(targets)
    sems = max(len(spans(p[1], h)) for p in pieces for h in range(2))

    def body(flag_ref, *refs):
        values = refs[n : n + len(arrays)]
        outs, sem = refs[n + len(arrays) : -1], refs[-1]

        def copies(k, h):
            _, chunk, _, at = pieces[k]
            made = []
            for q, (first, rows, target, row, per, col) in enumerate(spans(chunk, h)):
                to = outs[target].at[
                    pl.ds(pl.multiple_of(flag_ref[at] * per + row, SUB), rows), pl.ds(col, arrays[k].shape[1])
                ]
                made.append(pltpu.make_async_copy(values[k].at[pl.ds(first, rows), :], to, sem.at[k * sems + q]))
            return made

        for act in ("start", "wait"):
            for k in range(len(arrays)):
                for h in range(2):
                    @pl.when(flag_ref[pieces[k][2]] == h)
                    def _():
                        for copy in copies(k, h):
                            getattr(copy, act)()

    return pl.pallas_call(
        body,
        out_shape=[jax.ShapeDtypeStruct(t.shape, F32) for t in targets],
        grid_spec=pltpu.PrefetchScalarGridSpec(
            num_scalar_prefetch=1, grid=(1,),
            in_specs=[pl.BlockSpec(memory_space=pltpu.HBM)] * n
            + [pl.BlockSpec(a.shape, lambda i, ix: (0, 0)) for a in arrays],
            out_specs=[pl.BlockSpec(memory_space=pltpu.HBM)] * n,
            scratch_shapes=[pltpu.SemaphoreType.DMA((len(arrays) * sems,))],
        ),
        input_output_aliases={1 + k: k for k in range(n)},
        compiler_params=pltpu.CompilerParams(vmem_limit_bytes=VMEM),
        cost_estimate=CHEAP,
        name="put",
    )(flags, *targets, *arrays)


def bits_of(axis):
    return lax.axis_size(axis).bit_length() - 1


def bit(step):
    return (lax.axis_index(step[0]) >> step[1]) & 1


def swap(value, step):
    axis, place = step
    size = lax.axis_size(axis)
    return lax.ppermute(value, axis, [(i, i ^ (1 << place)) for i in range(size)])


CORE = ("rep", 0)


def orders():
    x, y, z = ("dp", 0), ("rep", 1), ("dp", 1)
    rest = [("dp", b) for b in range(2, bits_of("dp"))] + [("rep", b) for b in range(2, bits_of("rep"))]
    return [[x, y, z] + rest, [y, z, x] + rest, [z, x, y] + rest]


def fits(rows):
    unit = 3 << len(orders()[0])
    return -(-rows // unit) * unit


def slab(value, start, rows):
    return lax.dynamic_slice_in_dim(value, start, rows, 0)


class Order:
    def __init__(self):
        self.last = None

    def tie(self, *values):
        if self.last is None:
            return values
        return lax.optimization_barrier((values, self.last))[0]

    def done(self, value):
        self.last = value


class Reduced:
    def __init__(self, order):
        self.order = order
        self.steps = orders()
        self.count = len(self.steps[0])
        self.k = -1
        self.share = None

    def same(self, k):
        return self.steps[0][k] == self.steps[1][k]

    def send(self, k, values):
        if self.same(k):
            got = swap(jnp.concatenate(values), self.steps[0][k])
            size = values[0].shape[0]
            return [lax.slice_in_dim(got, c * size, (c + 1) * size) for c in range(3)]
        return [swap(v, s[k]) for v, s in zip(values, self.steps)]

    def begin(self, whole):
        rows = whole.shape[0] // 3
        self.kept = [(whole, c * rows, rows) for c in range(3)]
        self.got = None
        self.fold()

    def fold(self):
        k = self.k + 1
        if self.got is None:
            terms = [[v] for v in self.kept]
        else:
            arrays = self.order.tie([v[0] for v in self.kept], self.got)
            terms = [
                [(a, start, rows), (g, 0, rows)]
                for a, (_, start, rows), g in zip(arrays[0], self.kept, arrays[1])
            ]

        def part(term, i, halves):
            values = []
            for value, start, rows in term:
                size = rows // halves
                values.append(slab(value, start + i * size, size))
            return sum(values[1:], values[0])

        if k == self.count:
            self.share = [part(t, 0, 1) for t in terms]
            self.order.done(self.share[0])
            self.got = self.send(k - 1, self.share)
            self.k = k - 1
            return
        index = [bit(s[k]) for s in self.steps]
        sends = [part(t, 1 - i, 2) for t, i in zip(terms, index)]
        self.order.done(sends)
        if self.got is None:
            self.kept = [(v, start + i * (rows // 2), rows // 2) for (v, start, rows), i in zip(self.kept, index)]
            got = self.send(k, sends)
        else:
            got = self.send(k, sends)
            tied = self.order.tie([[v[0] for v in t] for t in terms])[0]
            keeps = [
                part([(a, start, rows) for a, (_, start, rows) in zip(arr, t)], i, 2)
                for arr, t, i in zip(tied, terms, index)
            ]
            self.order.done(keeps)
            self.kept = [(v, 0, v.shape[0]) for v in keeps]
        self.got = got
        self.k = k

    def finish(self):
        while self.share is None:
            self.fold()
        while self.k > 3:
            self.widen()

    def widen(self):
        k = self.k
        share, got = self.order.tie(self.share, self.got)
        wide = []
        for v, g, s in zip(share, got, self.steps):
            first = bit(s[k]) == 0
            wide.append(jnp.where(first, jnp.concatenate([v, g]), jnp.concatenate([g, v])))
        self.share = wide
        self.order.done(wide)
        self.k = k - 1
        self.got = self.send(k - 1, wide)
        if k == 1:
            self.across = [swap(v, CORE) for v in wide]

    def own(self):
        return [(v, c, c, 6) for c, v in enumerate(self.share)] + [(v, c, c, 7) for c, v in enumerate(self.across)]

    def arrived(self):
        return [(v, c, 3 + c, 6) for c, v in enumerate(self.got)] + [(swap(v, CORE), c, 3 + c, 7) for c, v in enumerate(self.got)]

    def flags(self):
        mine = [bit(s[0]) for s in self.steps]
        core = bit(CORE)
        return jnp.stack(mine + [1 - i for i in mine] + [core, 1 - core]).astype(jnp.int32)


def spans_of(total, parts):
    size = total // 6

    def spans(chunk, h):
        low = (2 * chunk + h) * size
        found, start = [], 0
        for rows, target, row, col in parts:
            a, b = max(low, start), min(low + size, start + rows)
            if a < b and target is not None:
                found.append((a - low, b - a, target, row + a - start, rows, col))
            start += rows
        return found

    return spans


SEQUENCE = (
    "front", "scan0", "out0", "scan1", "out1", "p0.f", "back0", "p0.f", "p1.f", "back1", "p0.f", "p1.f", "mix", "post0",
    "post1", "p0.e", "p1.f", "out2", "p1.e", "p0.w", "p1.w", "p2.f", "p0.w", "p1.w", "p2.f", "p0.w", "gn", "p2.f",
    "p1.w", "p0.own", "p2.e", "p0.got", "p1.own", "p2.w", "p1.got", "p2.w", "mixed", "p2.w", "p2.own", "p2.got",
)


def shards(
    tokens, cotangent, lengths, norm_gain, in_weight, conv_weight, conv_bias, xproj_weight,
    dt_weight, dt_bias, decay_log, skip_gain, out_weight,
):
    tok, cot = tokens[0], cotangent[0]
    length, model = tok.shape
    taps, width = conv_weight.shape
    states = decay_log.shape[0]
    rank = dt_weight.shape[0]
    cols = xproj_weight.shape[1]
    row = lambda v: v.reshape(1, -1)
    core = bit(CORE).astype(jnp.int32)[None]
    dlog3 = decay_log.reshape(states, width // LANES, LANES)
    turned = xproj_weight.T
    sizes = [cols, rank, states, 2, taps + 1]
    used = -(-sum(sizes) // SUB) * SUB
    order = Order()
    tie, done = order.tie, order.done
    sets = [Reduced(order) for _ in range(3)]
    heights = [fits(model), fits(model), fits(model + used)]
    low = model // 2
    spans = [
        spans_of(heights[b], [(WIDE // 2, 1, b * WIDE, 0), (low, 0, 0, width + b * WIDE)]) for b in range(2)
    ] + [spans_of(heights[2], [(low, 0, 0, 0), (low, 0, 0, WIDE), (used, 2, 0, 0)])]
    state = {"targets": [blank((model, 2 * width)), blank((width, model)), blank((2 * used, WIDE))]}
    scans, backs, posts, others = {}, {}, {}, {}

    def op_front():
        state["front"] = front(
            tok, cot, jnp.concatenate([lengths, core]), row(norm_gain), in_weight, conv_weight, row(conv_bias), turned
        )
        _, send, og, _, _, mp = state["front"]
        state["og"] = swap(og, CORE)
        state["normed"] = swap(send, CORE)
        done(mp)

    def op_scan(b):
        normed, _, og, _, act, mp = state["front"]
        mp, = tie(mp)
        scans[b] = scan(
            b, core, mp, normed, og, act, in_weight, out_weight, dt_weight, row(dt_bias), dlog3, row(skip_gain)
        )
        done(scans[b][0])
        others[b] = (swap(scans[b][1], CORE), swap(scans[b][2], CORE))

    def op_out(b):
        normed, _, og, _, _, _ = state["front"]
        if b < 2:
            own = [(scans[b][0], og), (normed, scans[b][2])]
            other = [(others[b][0], state["og"]), (state["normed"], others[b][1])]
            small = ()
        else:
            own = [(normed, posts[q][0]) for q in range(2)]
            other = [(state["normed"], others[2 + q]) for q in range(2)]
            small = (posts[0][1], posts[1][1], others["small"])
        own, other, small = tie(own, other, small)
        whole = outer(core, own, other, heights[b], small)
        done(whole)
        sets[b].begin(whole)

    def op_back(b):
        _, _, _, _, act, mp = state["front"]
        mp, = tie(mp)
        backs[b] = back(b, mp, act, scans[b][4], scans[b][3], scans[b][5], dt_weight, dlog3)
        done(backs[b][0])

    def op_mix():
        v = tie(*[[backs[b][2], backs[b][4]] for b in range(2)])
        state["gmix"] = jnp.concatenate([v[0][0] + v[1][0], (v[0][1] + v[1][1])[:, rank:cols]], axis=1).astype(BF16)
        done(state["gmix"])

    def op_post(b):
        _, _, _, inner, act, _ = state["front"]
        gmix, = tie(state["gmix"])
        back_b = backs[b]
        posts[b] = post(
            b, used, gmix, scans[b][3], back_b[0], act, inner, turned, conv_weight, row(conv_bias), row(skip_gain),
            back_b[3], back_b[5].reshape(states, WIDE), back_b[6],
        )
        done(posts[b][0])
        others[2 + b] = swap(posts[b][0], CORE)
        if b == 1:
            others["small"] = swap(jnp.where(core[0] == 0, posts[1][1], posts[0][1]), CORE)

    def op_gn():
        parts = tie(posts[0][0], posts[1][0], scans[0][2], scans[1][2])
        grad_projected = jnp.concatenate([v.astype(BF16) for v in parts], axis=1)
        grad_normed = dot(grad_projected, in_weight, ((1,), (1,)))
        x = tok.astype(F32)
        inv = lax.rsqrt(jnp.mean(x * x, axis=1, keepdims=True) + EPS)
        unit = x * inv
        grad_unit = grad_normed * norm_gain
        state["grad_tokens"] = cot.astype(F32) + inv * (
            grad_unit - unit * jnp.mean(grad_unit * unit, axis=1, keepdims=True)
        )
        done(state["grad_tokens"])

    def op_mixed():
        b0, b1 = tie(scans[0][0], scans[1][0])
        live = (jnp.arange(length) < lengths[0])[:, None]
        total = dot(jnp.concatenate([b0, b1], axis=1), out_weight)
        state["mixed"] = (tok.astype(F32) + jnp.where(live, total, 0.0)).astype(BF16)
        done(state["mixed"])

    def op_put(p, pieces):
        arrays, targets = tie([v[0] for v in pieces], state["targets"])
        pieces = [(a,) + v[1:] for a, v in zip(arrays, pieces)]
        state["targets"] = put(targets, pieces, spans[p], sets[p].flags())
        done(state["targets"][0])

    for name in SEQUENCE:
        if name[0] == "p" and name[2] == ".":
            p, what = int(name[1]), name[3:]
            if what == "f":
                sets[p].fold()
            elif what == "e":
                sets[p].finish()
            elif what == "w":
                sets[p].widen()
            else:
                op_put(p, sets[p].own() if what == "own" else sets[p].arrived())
        elif name[-1] in "012":
            {"scan": op_scan, "out": op_out, "back": op_back, "post": op_post}[name[:-1]](int(name[-1]))
        else:
            {"front": op_front, "mix": op_mix, "gn": op_gn, "mixed": op_mixed}[name]()

    grad_in, grad_out, small = state["targets"]
    grad_gain = jnp.sum(grad_in * in_weight.astype(F32), axis=1) / norm_gain
    small = jnp.concatenate([small[:used], small[used:]], axis=1)
    ends = [sum(sizes[: i + 1]) for i in range(len(sizes))]
    cut = [small[e - n : e] for e, n in zip(ends, sizes)]
    return (
        state["mixed"][None], state["grad_tokens"][None],
        grad_gain, grad_in, cut[4][:taps], cut[4][taps], cut[0].T, cut[1], cut[3][0],
        cut[2], cut[3][1], grad_out,
    )


def solution(mesh):
    rows = P(("dp", "rep"), None, None)
    return jax.shard_map(
        shards,
        mesh=mesh,
        in_specs=(rows, rows, P(("dp", "rep"))) + (P(),) * 10,
        out_specs=(rows, rows) + (P(),) * 10,
        check_vma=False,
    )
```

```python
import functools
import math
import jax
import jax.numpy as jnp
from jax import lax
from jax.experimental import pallas as pl
from jax.experimental.pallas import tpu as pltpu
from jax.sharding import PartitionSpec as P

F32 = jnp.float32
BF16 = jnp.bfloat16
EPS = 1e-05
LANES = 128
SUB = 8
WIDE = 1024
SEG = 16
MIB = 1024 * 1024
LOG2E = math.log2(math.e)
CHEAP = pl.CostEstimate(flops=1, bytes_accessed=1, transcendentals=0)


def dot(a, b, dims=((1,), (0,))):
    return lax.dot_general(a, b, (dims, ((), ())), preferred_element_type=F32)


def shifted(value, rows):
    if rows == 0:
        return value
    length = value.shape[0]
    index = lax.broadcasted_iota(jnp.int32, value.shape, 0)
    moved = pltpu.roll(value, rows % length, 0)
    keep = index >= rows if rows > 0 else index < length + rows
    return jnp.where(keep, moved, 0.0)


def conv_of(inner, cw_ref, cb_ref):
    taps = cw_ref.shape[0]
    total = cb_ref[...] + cw_ref[taps - 1 : taps, :] * inner
    for k in range(taps - 1):
        total = total + cw_ref[k : k + 1, :] * shifted(inner, taps - 1 - k)
    return total


def front_kernel(
    len_ref, tok_ref, cot_ref, gain_ref, w_ref, cw_ref, cb_ref, xp_ref,
    normed_ref, send_ref, og_ref, inner_ref, act_ref, mp_ref,
):
    @pl.when(pl.program_id(0) == 0)
    def _():
        x = tok_ref[...].astype(F32)
        inv = lax.rsqrt(jnp.mean(x * x, axis=1, keepdims=True) + EPS)
        normed = (x * inv * gain_ref[...]).astype(BF16)
        normed_ref[...] = normed
        low = x.shape[1] // 2
        send_ref[...] = jnp.where(len_ref[1] == 0, normed[:, low:], normed[:, :low]).astype(F32)
        row = lax.broadcasted_iota(jnp.int32, x.shape, 0)
        og_ref[...] = jnp.where(row < len_ref[0], cot_ref[...].astype(F32), 0.0)
        mp_ref[...] = jnp.zeros_like(mp_ref)

    inner = dot(normed_ref[...], w_ref[...])
    inner_ref[...] = inner
    conv = conv_of(inner, cw_ref, cb_ref)
    act = (conv * jax.nn.sigmoid(conv)).astype(BF16)
    act_ref[...] = act
    mp_ref[...] += dot(act, xp_ref[...], ((1,), (1,)))


def front(tokens, cot, lengths, gain, in_weight, cw, cb, xproj):
    length, model = tokens.shape
    width = cw.shape[1]
    cols = xproj.shape[0]
    blk = 512
    whole = lambda shape: pl.BlockSpec(shape, lambda j: (0, 0))
    part = lambda rows: pl.BlockSpec((rows, blk), lambda j: (0, j))
    return pl.pallas_call(
        front_kernel,
        grid=(width // blk,),
        in_specs=[
            pl.BlockSpec(memory_space=pltpu.SMEM),
            whole((length, model)), whole((length, model)), whole((1, model)),
            part(model), part(cw.shape[0]), part(1),
            part(cols),
        ],
        out_specs=[
            whole((length, model)), whole((length, model // 2)), whole((length, model)),
            part(length), part(length), whole((length, cols)),
        ],
        out_shape=[
            jax.ShapeDtypeStruct((length, model), BF16),
            jax.ShapeDtypeStruct((length, model // 2), F32),
            jax.ShapeDtypeStruct((length, model), F32),
            jax.ShapeDtypeStruct((length, width), F32),
            jax.ShapeDtypeStruct((length, width), BF16),
            jax.ShapeDtypeStruct((length, cols), F32),
        ],
        compiler_params=pltpu.CompilerParams(vmem_limit_bytes=60 * MIB),
        cost_estimate=CHEAP,
        name="front",
    )(lengths, tokens, cot, gain, in_weight, cw, cb, xproj)


def splat_rows(length, count):
    return -(-length // LANES) * count * LANES


def fill_splats(mp_ref, splat_ref, first, count):
    length, cols = mp_ref.shape
    for g in range(-(-length // LANES)):
        size = min(LANES, length - g * LANES)
        rows = mp_ref[pl.ds(g * LANES, size), :]
        rows = jnp.concatenate([rows, jnp.zeros((size, LANES - cols), F32)], axis=1)
        if size < LANES:
            rows = jnp.concatenate([rows, jnp.zeros((LANES - size, LANES), F32)], axis=0)
        turned = rows.T
        for n in range(count):
            line = jnp.broadcast_to(turned[first + n : first + n + 1, :], (LANES, LANES))
            splat_ref[pl.ds((g * count + n) * LANES, size), :] = line.T[:size]


def splat(splat_ref, tb, count, n, s):
    per = LANES // SUB
    row = tb // per * (count * LANES) + tb % per * SUB + (n * LANES + s)
    return jnp.broadcast_to(splat_ref[pl.ds(row, 1), :], (SUB, LANES))


def tile_rows(tb, s):
    return pl.ds(pl.multiple_of(tb * SUB * SUB, SUB * SUB) + s, SUB, stride=SUB)


def put_tiles(ref, j, value):
    for tb in range(value.shape[0] // SUB):
        ref[pl.ds(tb * SUB * SUB + j * SUB, SUB), :] = value[tb * SUB : (tb + 1) * SUB, :]


def get_tiles(ref, j, length):
    return jnp.concatenate(
        [ref[pl.ds(tb * SUB * SUB + j * SUB, SUB), :] for tb in range(length // SUB)], axis=0
    )


def scan_kernel(
    block, core_ref, mp_ref, act_ref, dtw_ref, dtb_ref, dlog_ref, skip_ref, normed_hbm, og_hbm, win_hbm, wout_hbm,
    branch_ref, ggp_ref, send_ref, more_ref, gs_ref, step_out, mark_out,
    splat_ref, u_ref, y_ref, a_ref, gate_ref, gb_ref, normed_ref, og_ref, wg_ref, wo_ref, step_ref, mark_ref, sems,
):
    length = mp_ref.shape[0]
    rank = dtw_ref.shape[0]
    states = a_ref.shape[0]
    both = 2 * states
    width = win_hbm.shape[1] // 2
    loads = [
        pltpu.make_async_copy(src, dst, sems.at[k])
        for k, (src, dst) in enumerate((
            (normed_hbm, normed_ref), (win_hbm.at[:, pl.ds(width + block * WIDE, WIDE)], wg_ref),
            (og_hbm, og_ref), (wout_hbm.at[pl.ds(block * WIDE, WIDE), :], wo_ref),
        ))
    ]
    for load in loads:
        load.start()
    fill_splats(mp_ref, splat_ref, rank, both)
    a_ref[...] = -jnp.exp(dlog_ref[...]) * LOG2E
    delta_in = mp_ref[:, :rank].astype(BF16)
    for j in range(WIDE // LANES):
        cols = pl.ds(j * LANES, LANES)
        pre = dot(delta_in, dtw_ref[:, cols]) + dtb_ref[:, cols]
        step = jnp.maximum(pre, 0.0) + jnp.log1p(jnp.exp(-jnp.abs(pre)))
        put_tiles(step_ref, j, step)
        put_tiles(u_ref, j, step * act_ref[:, cols].astype(F32))
    stores = [
        pltpu.make_async_copy(step_ref, step_out, sems.at[4]), pltpu.make_async_copy(mark_ref, mark_out, sems.at[5])
    ]
    stores[0].start()

    def body(seg, carry):
        h = list(carry)
        base = pl.multiple_of(seg * states * SUB, states * SUB)
        for n in range(states):
            mark_ref[pl.ds(base + n * SUB, SUB), :] = h[n]

        def eight(k, h):
            h = list(h)
            tb = seg * (SEG // SUB) + k
            for s in range(SUB):
                step = step_ref[tile_rows(tb, s), :]
                u = u_ref[tile_rows(tb, s), :]
                y = None
                for n in range(states):
                    f = jnp.exp2(step * a_ref[n])
                    h[n] = f * h[n] + u * splat(splat_ref, tb, both, n, s)
                    q = h[n] * splat(splat_ref, tb, both, states + n, s)
                    y = q if y is None else y + q
                y_ref[tile_rows(tb, s), :] = y
            return tuple(h)

        return lax.fori_loop(0, SEG // SUB, eight, tuple(h))

    zero = jnp.zeros((SUB, LANES), F32)
    lax.fori_loop(0, length // SEG, body, (zero,) * states)
    stores[1].start()

    for load in loads:
        load.wait()
    og = og_ref[...].astype(BF16)
    for k in range(WIDE // 256):
        cols = pl.ds(k * 256, 256)
        gate_ref[:, cols] = dot(normed_ref[...], wg_ref[:, cols])
        gb_ref[:, cols] = dot(og, wo_ref[cols, :], ((1,), (1,)))
    for j in range(WIDE // LANES):
        cols = pl.ds(j * LANES, LANES)
        gate = gate_ref[:, cols]
        gb = gb_ref[:, cols]
        summed = get_tiles(y_ref, j, length) + skip_ref[:, cols] * act_ref[:, cols].astype(F32)
        sig = jax.nn.sigmoid(gate)
        gate_act = gate * sig
        branch = (summed * gate_act).astype(BF16)
        branch_ref[:, cols] = branch
        into = pl.ds(j * LANES % (WIDE // 2), LANES)

        @pl.when((core_ref[0] == 0) == (j * LANES >= WIDE // 2))
        def _():
            send_ref[:, into] = branch.astype(F32)
        put_tiles(gs_ref, j, gb * gate_act)
        ggp = (gb * summed * (sig * (1.0 + gate * (1.0 - sig)))).astype(BF16)
        ggp_ref[:, cols] = ggp
        to = WIDE // 2 + j * LANES
        if to < 3 * WIDE // 4:
            send_ref[:, to : to + LANES] = ggp.astype(F32)
        else:
            to = to - 3 * WIDE // 4
            more_ref[:, to : to + LANES] = ggp.astype(F32)
    for store in stores:
        store.wait()


def scan(block, core, mp, normed, og, act, in_weight, out_weight, dtw, dtb, dlog, skip):
    length, model = normed.shape
    rank = dtw.shape[0]
    states = dlog.shape[0]
    whole = lambda shape: pl.BlockSpec(shape, lambda i: (0,) * len(shape))
    col = lambda rows: pl.BlockSpec((rows, WIDE), lambda i: (0, block))
    hbm = pl.BlockSpec(memory_space=pltpu.HBM)
    tiles = (length * SUB, LANES)
    marks = (length // SEG * states * SUB, LANES)
    flat = (length, WIDE)
    send = (length, 3 * WIDE // 4)
    shape = jax.ShapeDtypeStruct
    return pl.pallas_call(
        functools.partial(scan_kernel, block),
        grid=(1,),
        in_specs=[
            pl.BlockSpec(memory_space=pltpu.SMEM), whole(mp.shape), col(length), col(rank), col(1),
            pl.BlockSpec((states, SUB, LANES), lambda i: (0, block, 0)), col(1), hbm, hbm, hbm, hbm,
        ],
        out_specs=[whole(flat)] * 2 + [whole(send)] * 2 + [whole(tiles), hbm, hbm],
        out_shape=[shape(flat, BF16)] * 2 + [shape(send, F32)] * 2 + [shape(tiles, F32)] * 2 + [shape(marks, F32)],
        scratch_shapes=[
            pltpu.VMEM((splat_rows(length, 2 * states), LANES), F32),
            pltpu.VMEM(tiles, F32),
            pltpu.VMEM(tiles, F32),
            pltpu.VMEM((states, SUB, LANES), F32),
            pltpu.VMEM(flat, F32),
            pltpu.VMEM(flat, F32),
            pltpu.VMEM(normed.shape, BF16),
            pltpu.VMEM(og.shape, F32),
            pltpu.VMEM((model, WIDE), BF16),
            pltpu.VMEM((WIDE, model), BF16),
            pltpu.VMEM(tiles, F32),
            pltpu.VMEM(marks, F32),
            pltpu.SemaphoreType.DMA((6,)),
        ],
        compiler_params=pltpu.CompilerParams(vmem_limit_bytes=60 * MIB),
        cost_estimate=CHEAP,
        name=f"scan{block}",
    )(core, mp, act, dtw, dtb, dlog, skip, normed, og, in_weight, out_weight)


def back_kernel(
    first, mp_ref, act_ref, step_ref, gs_ref, mark_ref, dtw_ref, dlog_ref, *rest,
):
    if not first:
        carry_in, rest = rest[0], rest[1:]
    (
        gact_ref, gdelta_ref, gdtw_ref, gwr_ref, carry_ref, rows_ref, glin_ref,
        splat_ref, act_t_ref, gd_ref, gu_ref, a_ref, f_ref, h_ref, turn_ref, part_ref,
    ) = rest
    length = mp_ref.shape[0]
    rank = dtw_ref.shape[0]
    states = a_ref.shape[0]
    both = 2 * states
    fill_splats(mp_ref, splat_ref, rank, both)
    a_ref[...] = -jnp.exp(dlog_ref[...])
    for j in range(WIDE // LANES):
        put_tiles(act_t_ref, j, act_ref[:, pl.ds(j * LANES, LANES)].astype(F32))
    per = SEG // SUB

    groups = states // SUB
    if first:
        carry_ref[...] = jnp.zeros_like(carry_ref)
    else:
        carry_ref[...] = carry_in[...]

    def segment(i, _):
        seg = length // SEG - 1 - i
        for q in range(groups):
            mine = range(q * SUB, (q + 1) * SUB)
            rates = [a_ref[n] for n in mine]
            base = pl.multiple_of(seg * states * SUB, states * SUB)
            start = [mark_ref[pl.ds(base + n * SUB, SUB), :] for n in mine]
            for j in range(SUB):
                h_ref[0, j] = start[j]

            def again(k, hs):
                hs = list(hs)
                tb = seg * per + k
                for s in range(SUB):
                    step = step_ref[tile_rows(tb, s), :]
                    u = step * act_t_ref[tile_rows(tb, s), :]
                    step2 = step * LOG2E
                    for j, n in enumerate(mine):
                        f = jnp.exp2(step2 * rates[j])
                        f_ref[k * SUB + s, j] = f
                        hs[j] = f * hs[j] + u * splat(splat_ref, tb, both, n, s)
                        h_ref[k * SUB + s + 1, j] = hs[j]
                return tuple(hs)

            last = lax.fori_loop(0, per, again, tuple(start))

            def reverse(k2, carry):
                dhs, gas, now = (list(c) for c in carry)
                k = per - 1 - k2
                tb = seg * per + k
                for s in reversed(range(SUB)):
                    g = gs_ref[tile_rows(tb, s), :]
                    step = step_ref[tile_rows(tb, s), :]
                    u = step * act_t_ref[tile_rows(tb, s), :]
                    gd = gu = None
                    ws, rs = [], []
                    for j, n in enumerate(mine):
                        dh = dhs[j] + g * splat(splat_ref, tb, both, states + n, s)
                        before = h_ref[k * SUB + s, j]
                        rs.append(now[j] * g)
                        ws.append(dh * u)
                        t = dh * splat(splat_ref, tb, both, n, s)
                        gu = t if gu is None else gu + t
                        dhs[j] = dh * f_ref[k * SUB + s, j]
                        ga = dhs[j] * before
                        t = ga * rates[j]
                        gd = t if gd is None else gd + t
                        gas[j] = gas[j] + ga * step
                        now[j] = before
                    if q == 0:
                        gd_ref[tile_rows(tb, s), :] = gd
                        gu_ref[tile_rows(tb, s), :] = gu
                    else:
                        gd_ref[tile_rows(tb, s), :] = gd_ref[tile_rows(tb, s), :] + gd
                        gu_ref[tile_rows(tb, s), :] = gu_ref[tile_rows(tb, s), :] + gu
                    for slot, values in ((0, ws), (1, rs)):
                        at = (s * 2 + slot) * SUB * SUB
                        for j in range(SUB):
                            turn_ref[pl.ds(at + j * SUB, SUB), :] = values[j]
                        total = turn_ref[pl.ds(at, SUB, stride=SUB), :]
                        for j in range(1, SUB):
                            total = total + turn_ref[pl.ds(at + j, SUB, stride=SUB), :]
                        row = tb * (both * SUB) + (slot * states + q * SUB) * SUB + s
                        part_ref[pl.ds(row, SUB, stride=SUB), :] = total
                return (tuple(dhs), tuple(gas), tuple(now))

            begin = (
                tuple(carry_ref[0, n] for n in mine), tuple(carry_ref[1, n] for n in mine), last
            )
            dhs, gas, _ = lax.fori_loop(0, per, reverse, begin)
            for j, n in enumerate(mine):
                carry_ref[0, n] = dhs[j]
                carry_ref[1, n] = gas[j]
        return 0

    lax.fori_loop(0, length // SEG, segment, 0)
    row = lax.broadcasted_iota(jnp.int32, (2 * LANES, LANES), 0)
    lane = lax.broadcasted_iota(jnp.int32, (2 * LANES, LANES), 1)
    gwr = None
    for n in range(0, both, 2):
        pieces = []
        for k in range(2):
            pieces.append(jnp.concatenate(
                [part_ref[pl.ds((tb * both + n + k) * SUB, SUB), :] for tb in range(length // SUB)], axis=0
            ).astype(BF16))
        into = jnp.where(lane == rank + n + row // LANES, 1.0, 0.0).astype(BF16)
        term = dot(jnp.concatenate(pieces, axis=1), into)
        gwr = term if gwr is None else gwr + term
    gwr_ref[...] = gwr

    for j in range(WIDE // LANES):
        cols = pl.ds(j * LANES, LANES)
        act = act_ref[:, cols].astype(F32)
        step = get_tiles(step_ref, j, length)
        gs = get_tiles(gs_ref, j, length)
        gu = get_tiles(gu_ref, j, length)
        gstep = get_tiles(gd_ref, j, length) + gu * act
        gpre = gstep * (1.0 - jnp.exp(-step))
        glin_ref[:, cols] = gpre.astype(BF16)
        rows_ref[0:1, cols] = jnp.sum(gpre, axis=0, keepdims=True)
        rows_ref[1:2, cols] = jnp.sum(gs * act, axis=0, keepdims=True)
        gact_ref[:, cols] = gu * step
    delta_in = mp_ref[:, :rank].astype(BF16)
    gdtw_ref[...] = dot(delta_in, glin_ref[...], ((0,), (0,)))
    gdelta_ref[...] = dot(glin_ref[...], dtw_ref[...], ((1,), (1,)))


def back(block, part, parts, mp, act, step, gs, marks, dtw, dlog, carry=None):
    length = act.shape[0] // parts
    rank = dtw.shape[0]
    states = dlog.shape[0]
    first = carry is None
    whole = lambda shape: pl.BlockSpec(shape, lambda i: (0,) * len(shape))
    mine = lambda v: pl.BlockSpec((v.shape[0] // parts, v.shape[1]), lambda i: (part, 0))
    flat = jax.ShapeDtypeStruct((length, WIDE), F32)
    outs = [
        flat,
        jax.ShapeDtypeStruct((length, rank), F32),
        jax.ShapeDtypeStruct((rank, WIDE), F32),
        jax.ShapeDtypeStruct((length, LANES), F32),
        jax.ShapeDtypeStruct((2, states, SUB, LANES), F32),
        jax.ShapeDtypeStruct((2, WIDE), F32),
    ]
    tiles = pltpu.VMEM((length * SUB, LANES), F32)
    return pl.pallas_call(
        functools.partial(back_kernel, first),
        grid=(1,),
        in_specs=[
            mine(mp), pl.BlockSpec((length, WIDE), lambda i: (part, block)), mine(step), mine(gs), mine(marks),
            pl.BlockSpec((rank, WIDE), lambda i: (0, block)),
            pl.BlockSpec((states, SUB, LANES), lambda i: (0, block, 0)),
        ] + ([] if first else [whole(carry.shape)]),
        out_specs=[whole(o.shape) for o in outs],
        out_shape=outs,
        scratch_shapes=[
            pltpu.VMEM((length, WIDE), BF16),
            pltpu.VMEM((splat_rows(length, 2 * states), LANES), F32),
            tiles, tiles, tiles,
            pltpu.VMEM((states, SUB, LANES), F32),
            pltpu.VMEM((SEG, SUB, SUB, LANES), F32),
            pltpu.VMEM((SEG + 1, SUB, SUB, LANES), F32),
            pltpu.VMEM((2 * SUB * SUB * SUB, LANES), F32),
            pltpu.VMEM((length * 2 * states, LANES), F32),
        ],
        compiler_params=pltpu.CompilerParams(vmem_limit_bytes=36 * MIB),
        cost_estimate=CHEAP,
        name=f"back{block}{part}",
    )(mp, act, step, gs, marks, dtw, dlog, *([] if first else [carry]))


def post_kernel(
    parts, gs_ref, act_ref, inner_ref, xp_ref, cw_ref, cb_ref, skip_ref, carry_ref, dlog_ref, *rest,
):
    gact_refs, gdtw_refs, two_refs = rest[:parts], rest[parts : 2 * parts], rest[2 * parts : 3 * parts]
    gdelta_refs, gwr_refs = rest[3 * parts : 5 * parts], rest[5 * parts : 7 * parts]
    gi_ref, small_ref = rest[7 * parts :]
    total_of = lambda refs: sum([ref[...] for ref in refs[1:]], refs[0][...])
    length = act_ref.shape[0]
    taps = cw_ref.shape[0]
    states = dlog_ref.shape[0]
    lines = []
    for k in range(parts):
        delta = gdelta_refs[k][...] + gdelta_refs[parts + k][...]
        rest_of = (gwr_refs[k][...] + gwr_refs[parts + k][...])[:, : xp_ref.shape[0]]
        room = jnp.zeros((delta.shape[0], xp_ref.shape[0] - delta.shape[1]), F32)
        lines.append(jnp.concatenate([delta, room], axis=1) + rest_of)
    gmix = jnp.concatenate(lines, axis=0).astype(BF16)
    share = dot(gmix, xp_ref[...])
    sizes = [xp_ref.shape[0], gdtw_refs[0].shape[0], states, two_refs[0].shape[0]]
    ends = [sum(sizes[: i + 1]) for i in range(4)]
    small_ref[: ends[0], :] = dot(gmix, act_ref[...], ((0,), (0,)))
    small_ref[ends[0] : ends[1], :] = total_of(gdtw_refs)
    for n in range(states):
        for j in range(SUB):
            small_ref[ends[1] + n : ends[1] + n + 1, j * LANES : (j + 1) * LANES] = carry_ref[1, n, j : j + 1, :]
    small_ref[ends[1] : ends[2], :] = small_ref[ends[1] : ends[2], :] * -jnp.exp(dlog_ref[...])
    small_ref[ends[2] : ends[3], :] = total_of(two_refs)
    small_ref[ends[3] + taps + 1 :, :] = jnp.zeros((small_ref.shape[0] - ends[3] - taps - 1, WIDE), F32)
    for j in range(WIDE // LANES):
        cols = pl.ds(j * LANES, LANES)
        inner = inner_ref[:, cols]
        cw = cw_ref[:, cols]
        conv = conv_of(inner, cw, cb_ref[:, cols])
        sig = jax.nn.sigmoid(conv)
        gact = (
            get_tiles(gs_ref, j, length) * skip_ref[:, cols]
            + jnp.concatenate([ref[:, cols] for ref in gact_refs], axis=0)
            + share[:, j * LANES : (j + 1) * LANES]
        )
        gconv = gact * (sig * (1.0 + conv * (1.0 - sig)))
        at = ends[3]
        small_ref[at + taps : at + taps + 1, cols] = jnp.sum(gconv, axis=0, keepdims=True)
        total = None
        for k in range(taps):
            small_ref[at + k : at + k + 1, cols] = jnp.sum(
                gconv * shifted(inner, taps - 1 - k), axis=0, keepdims=True
            )
            term = cw[k : k + 1, :] * shifted(gconv, k + 1 - taps)
            total = term if total is None else total + term
        gi_ref[:, cols] = total


def post(block, lines, gs, act, inner, xproj, cw, cb, skip, carry, dlog, gact, gdtw, two, gdelta, gwr):
    length = act.shape[0]
    cols = xproj.shape[0]
    taps = cw.shape[0]
    whole = lambda shape: pl.BlockSpec(shape, lambda i: (0,) * len(shape))
    col = lambda rows, at: pl.BlockSpec((rows, WIDE), lambda i: (0, at))
    outs = [jax.ShapeDtypeStruct((length, WIDE), F32), jax.ShapeDtypeStruct((lines, WIDE), F32)]
    return pl.pallas_call(
        functools.partial(post_kernel, len(gact)),
        grid=(1,),
        in_specs=[
            whole(gs.shape), col(length, block), col(length, block),
            col(cols, block), col(taps, block), col(1, block), col(1, block),
            whole(carry.shape), col(dlog.shape[0], block),
        ] + [whole(v.shape) for v in [*gact, *gdtw, *two, *gdelta, *gwr]],
        out_specs=[whole(o.shape) for o in outs],
        out_shape=outs,
        compiler_params=pltpu.CompilerParams(vmem_limit_bytes=60 * MIB),
        cost_estimate=CHEAP,
        name=f"post{block}",
    )(gs, act, inner, xproj, cw, cb, skip, carry, dlog, *gact, *gdtw, *two, *gdelta, *gwr)


def outer(core, own, other, sizes, flags, weight=None, cols=(), gains=(), small=()):
    length = own[0][0].shape[0]
    low, wide = own[0][0].shape[1] // 2, own[0][1].shape[1]
    halves = [v // 2 for v in sizes for _ in range(2)]
    starts = [sum(halves[:k]) for k in range(len(halves))]
    blk = 256
    total = sum(sizes)
    at_core = len(sizes)
    big, moves = [], []
    for c in range(2):
        for k, pieces in enumerate(([(own[c][0], None, low)], other[c][0], [(own[c][1], 0, wide)], other[c][1])):
            to = 0
            for array, col, count in pieces:
                moves.append((len(big), 4 * c + k, col, to, count))
                big.append(array)
                to += count
    n_big = len(big)
    n_buf = 8
    with_gain = weight is not None
    extra = ([weight] if with_gain else []) + list(gains) + list(small)

    def body(flag_ref, *refs):
        ins, refs = refs[: n_big + len(extra)], refs[n_big + len(extra) :]
        outs, refs = refs[: len(halves) + with_gain], refs[len(halves) + with_gain :]
        bufs, refs = refs[:n_buf], refs[n_buf:]
        w_bufs, refs = (refs[: len(cols)], refs[len(cols) :])
        lefts, rights, result, sem_in, sem_w, sem_out = refs
        loads = []
        for k, buf, col, to, count in moves:
            col = pl.multiple_of(flag_ref[at_core] * low, LANES) if col is None else col
            loads.append(pltpu.make_async_copy(
                ins[k].at[:, pl.ds(col, count)], bufs[buf].at[:, pl.ds(to, count)], sem_in.at[k]
            ))
            loads[-1].start()
        w_loads = []
        for q, (c, col) in enumerate(cols):
            src = ins[n_big].at[pl.ds(pl.multiple_of(flag_ref[at_core] * low, SUB), low), pl.ds(col, wide)]
            w_loads.append(pltpu.make_async_copy(src, w_bufs[q], sem_w.at[q]))
            w_loads[-1].start()

        def copy(k, flip):
            c, h = k // 2, k % 2
            return pltpu.make_async_copy(
                result.at[pl.ds(starts[k], halves[k]), :], outs[2 * c + flip], sem_out.at[k]
            )

        def each(k, act):
            c, h = k // 2, k % 2
            for flip in range(2):
                @pl.when((flag_ref[c] == h) == bool(flip))
                def _():
                    getattr(copy(k, flip), act)()

        ready, sent = 0, 0
        gain = None
        for c in range(2):
            for k, buf, _, _, _ in moves:
                if buf // 4 == c:
                    loads[k].wait()
            lefts[:length] = bufs[4 * c][...].astype(BF16)
            lefts[length:] = bufs[4 * c + 1][...].astype(BF16)
            rights[:length] = bufs[4 * c + 2][...].astype(BF16)
            rights[length:] = bufs[4 * c + 3][...].astype(BF16)
            for m in range(0, low, blk):
                result[c * low + m : c * low + m + blk, :] = dot(lefts[:, m : m + blk], rights[...], ((0,), (0,)))
                ready = c * low + m + blk
                while sent < len(halves) and starts[sent] + halves[sent] <= ready:
                    each(sent, "start")
                    sent += 1
            for q, (pair, _) in enumerate(cols):
                if pair == c:
                    w_loads[q].wait()
                    for j in range(0, wide, LANES):
                        term = result[c * low : (c + 1) * low, j : j + LANES] * w_bufs[q][:, j : j + LANES].astype(F32)
                        gain = term if gain is None else gain + term
        if small:
            a, b, got = ins[-3:]
            lines = got.shape[0]
            result[2 * low : 2 * low + lines, :] = jnp.where(flag_ref[at_core] == 0, a[...], b[...]) + got[...]
            for ref in ins[n_big + 1 : n_big + 1 + len(gains)]:
                gain = gain + ref[...]
            rows = low // (wide // LANES)
            for j in range(wide // LANES):
                result[2 * low + lines : 2 * low + lines + rows, j * LANES : (j + 1) * LANES] = gain[j * rows : (j + 1) * rows]
            if 2 * low + lines + rows < total:
                result[2 * low + lines + rows :, :] = jnp.zeros((total - 2 * low - lines - rows, wide), F32)
        elif 2 * low < total:
            result[2 * low :, :] = jnp.zeros((total - 2 * low, wide), F32)
        if with_gain:
            outs[-1][...] = gain
        while sent < len(halves):
            each(sent, "start")
            sent += 1
        for k in range(len(halves)):
            each(k, "wait")

    hbm = pl.BlockSpec(memory_space=pltpu.HBM)
    vmem = lambda v: pl.BlockSpec(v.shape, lambda i, ix: (0, 0))
    out_shape = [jax.ShapeDtypeStruct((v // 2, wide), F32) for v in sizes for _ in range(2)]
    out_specs = [hbm] * len(out_shape)
    if with_gain:
        out_shape.append(jax.ShapeDtypeStruct((low, LANES), F32))
        out_specs.append(pl.BlockSpec((low, LANES), lambda i, ix: (0, 0)))
    buffers = [
        pltpu.VMEM((length, low if k % 4 < 2 else wide), own[k // 4][k % 4 // 2].dtype if k % 2 == 0 else F32) for k in range(n_buf)
    ] + [pltpu.VMEM((low, wide), BF16) for _ in cols]
    return pl.pallas_call(
        body,
        out_shape=out_shape,
        grid_spec=pltpu.PrefetchScalarGridSpec(
            num_scalar_prefetch=1, grid=(1,),
            in_specs=[hbm] * n_big + ([hbm] if with_gain else []) + [vmem(v) for v in [*gains, *small]],
            out_specs=out_specs,
            scratch_shapes=buffers + [
                pltpu.VMEM((2 * length, low), BF16), pltpu.VMEM((2 * length, wide), BF16), pltpu.VMEM((total, wide), F32),
                pltpu.SemaphoreType.DMA((n_big,)), pltpu.SemaphoreType.DMA((max(len(cols), 1),)),
                pltpu.SemaphoreType.DMA((len(halves),)),
            ],
        ),
        compiler_params=pltpu.CompilerParams(vmem_limit_bytes=60 * MIB),
        cost_estimate=CHEAP,
        name="outer",
    )(flags, *big, *extra)


def step_call(body, name, index, ins, in_specs, outs):
    return pl.pallas_call(
        body,
        out_shape=outs,
        grid_spec=pltpu.PrefetchScalarGridSpec(
            num_scalar_prefetch=1, grid=(1,), in_specs=in_specs,
            out_specs=[pl.BlockSpec(o.shape, lambda i, ix: (0, 0)) for o in outs],
        ),
        compiler_params=pltpu.CompilerParams(vmem_limit_bytes=20 * MIB),
        cost_estimate=CHEAP,
        name=name,
    )(index, *ins)


def rows_of(rows, cols):
    return jax.ShapeDtypeStruct((rows, cols), F32)


def fold_call(index, kept, got, merged):
    n = len(kept)
    ins, specs, sends, keeps = [], [], [], []
    for c in range(n):
        size, cols = kept[c].shape[0] // 2, kept[c].shape[1]
        base = 2 * c if len(got) < n else 0
        for flip in (0, 1):
            at = lambda i, ix, c=c, flip=flip, base=0: (base + (ix[c] if flip else 1 - ix[c]), 0)
            ins += [kept[c], got[c % len(got)]]
            specs += [pl.BlockSpec((size, cols), at), pl.BlockSpec((size, cols), functools.partial(at, base=base))]
        sends.append(rows_of(size, cols))
        keeps.append(rows_of(size, cols))
    sizes = [v.shape[0] for v in sends]
    if merged:
        sends = [rows_of(sum(sizes), cols)]

    def body(ix, *refs):
        outs = refs[4 * n :]
        for c in range(n):
            for flip in (0, 1):
                a, b = refs[4 * c + 2 * flip : 4 * c + 2 * flip + 2]
                if flip:
                    outs[len(sends) + c][...] = a[...] + b[...]
                elif merged:
                    outs[0][sum(sizes[:c]) : sum(sizes[: c + 1]), :] = a[...] + b[...]
                else:
                    outs[c][...] = a[...] + b[...]

    out = step_call(body, "fold", index, ins, specs, sends + keeps)
    return list(out[: len(sends)]), list(out[len(sends) :])


def last_call(index, kept, got):
    n = len(kept)
    sizes = [v.shape[0] for v in kept]
    cols = kept[0].shape[1]
    specs = [pl.BlockSpec(v.shape, lambda i, ix: (0, 0)) for v in [*kept, *got]]

    def body(ix, *refs):
        for c in range(n):
            at = slice(sum(sizes[:c]), sum(sizes[: c + 1]))
            refs[-1][at, :] = refs[c][...] + (refs[n + c][...] if len(got) == n else refs[n][at, :])

    return step_call(body, "last", index, [*kept, *got], specs, [rows_of(sum(sizes), cols)])[0]


def widen_call(index, sizes, share, got, merged):
    cols = share[0].shape[1]
    ins = [*share, *got]
    specs = [pl.BlockSpec(v.shape, lambda i, ix: (0, 0)) for v in ins]
    n = len(share)

    def body(ix, *refs):
        outs = refs[n + len(got) :]
        for c, size in enumerate(sizes):
            low = sum(sizes[:c])
            for side, at in ((refs[:n], ix[c]), (refs[n : n + len(got)], 1 - ix[c])):
                value = side[c][...] if len(side) == len(sizes) else side[0][low : low + size, :]
                if merged:
                    outs[0][pl.ds(pl.multiple_of(2 * low + at * size, SUB), size), :] = value
                else:
                    outs[c][pl.ds(pl.multiple_of(at * size, SUB), size), :] = value

    outs = [rows_of(2 * sum(sizes), cols)] if merged else [rows_of(2 * s, cols) for s in sizes]
    return list(step_call(body, "widen", index, ins, specs, outs))


def blank(shape):
    return pl.pallas_call(
        lambda ref: None, out_shape=jax.ShapeDtypeStruct(shape, F32),
        out_specs=pl.BlockSpec(memory_space=pltpu.HBM), name="blank",
        compiler_params=pltpu.CompilerParams(vmem_limit_bytes=16 * MIB), cost_estimate=CHEAP,
    )()


def put(targets, pieces, parts, sizes, flags):
    def spans(chunk, h):
        low = sum(sizes[:chunk]) + h * (sizes[chunk] // 2)
        return spans_of(parts, low, low + sizes[chunk] // 2)

    arrays = [p[0] for p in pieces]
    n = len(targets)
    sems = max(len(spans(p[1], h)) for p in pieces for h in range(2))

    def body(flag_ref, *refs):
        values = refs[n : n + len(arrays)]
        outs, sem = refs[n + len(arrays) : -1], refs[-1]

        def copies(k, h):
            _, chunk, _, at = pieces[k]
            made = []
            for q, (first, rows, target, row, per, col) in enumerate(spans(chunk, h)):
                to = outs[target].at[
                    pl.ds(pl.multiple_of(flag_ref[at] * per + row, SUB), rows), pl.ds(col, arrays[k].shape[1])
                ]
                made.append(pltpu.make_async_copy(values[k].at[pl.ds(first, rows), :], to, sem.at[k * sems + q]))
            return made

        for act in ("start", "wait"):
            for k in range(len(arrays)):
                for h in range(2):
                    @pl.when(flag_ref[pieces[k][2]] == h)
                    def _():
                        for copy in copies(k, h):
                            getattr(copy, act)()

    return pl.pallas_call(
        body,
        out_shape=[jax.ShapeDtypeStruct(t.shape, F32) for t in targets],
        grid_spec=pltpu.PrefetchScalarGridSpec(
            num_scalar_prefetch=1, grid=(1,),
            in_specs=[pl.BlockSpec(memory_space=pltpu.HBM)] * n
            + [pl.BlockSpec(a.shape, lambda i, ix: (0, 0)) for a in arrays],
            out_specs=[pl.BlockSpec(memory_space=pltpu.HBM)] * n,
            scratch_shapes=[pltpu.SemaphoreType.DMA((len(arrays) * sems,))],
        ),
        input_output_aliases={1 + k: k for k in range(n)},
        compiler_params=pltpu.CompilerParams(vmem_limit_bytes=20 * MIB),
        cost_estimate=CHEAP,
        name="put",
    )(flags, *targets, *arrays)


def bits_of(axis):
    return lax.axis_size(axis).bit_length() - 1


def bit(step):
    return (lax.axis_index(step[0]) >> step[1]) & 1


def swap(value, step):
    axis, place = step
    size = lax.axis_size(axis)
    return lax.ppermute(value, axis, [(i, i ^ (1 << place)) for i in range(size)])


CORE = ("rep", 0)


def orders(*heads):
    axes = {"x": ("dp", 0), "y": ("rep", 1), "z": ("dp", 1)}
    rest = [("dp", b) for b in range(2, bits_of("dp"))] + [("rep", b) for b in range(2, bits_of("rep"))]
    return [[axes[a] for a in head] + rest for head in heads]


class Order:
    def __init__(self):
        self.last = None

    def tie(self, *values):
        if self.last is None:
            return values
        return lax.optimization_barrier((values, self.last))[0]

    def done(self, value):
        self.last = value


class Reduced:
    def __init__(self, order, steps):
        self.order = order
        self.steps = steps
        self.count = len(steps[0])
        self.share = None

    def index(self, k):
        return jnp.stack([bit(s[k]) for s in self.steps]).astype(jnp.int32)

    def same(self, k):
        return all(s[k] == self.steps[0][k] for s in self.steps)

    def send(self, k, values):
        if len(values) == 1:
            return [swap(values[0], self.steps[0][k])]
        return [swap(v, s[k]) for v, s in zip(values, self.steps)]

    def begin(self, sends, keeps):
        self.k = 0
        self.kept = keeps
        self.got = self.send(0, sends)

    def fold(self):
        k = self.k + 1
        kept, got = self.order.tie(self.kept, self.got)
        if k == self.count:
            self.share = [last_call(self.index(0), kept, got)]
            self.sizes = [v.shape[0] for v in kept]
            if any(v % SUB for v in self.sizes):
                cut = [sum(self.sizes[:c]) for c in range(len(kept))]
                self.share = [lax.slice_in_dim(self.share[0], a, a + n) for a, n in zip(cut, self.sizes)]
            self.order.done(self.share[0])
            self.k = k - 1
            return
        equal = len({v.shape[0] for v in kept}) == 1
        merged = self.same(k) and (equal or k == self.count - 1)
        if any(v.shape[0] % (2 * SUB) for v in kept):
            if len(got) < len(kept):
                size = kept[0].shape[0]
                got = [lax.slice_in_dim(got[0], c * size, (c + 1) * size) for c in range(len(kept))]
            total = [a + b for a, b in zip(kept, got)]
            index = [bit(s[k]) for s in self.steps]
            half = lambda v, i: lax.dynamic_slice_in_dim(v, i * (v.shape[0] // 2), v.shape[0] // 2, 0)
            sends = [half(v, 1 - i) for v, i in zip(total, index)]
            self.kept = [half(v, i) for v, i in zip(total, index)]
        else:
            sends, self.kept = fold_call(self.index(k), kept, got, merged)
        self.order.done(self.kept[0])
        self.k = k
        self.got = self.send(k, sends)

    def finish(self):
        while self.share is None:
            self.fold()

    def back(self):
        self.got = self.send(self.k, self.share)
        while self.k > 3:
            self.widen()

    def origin(self, device, chunk):
        ranks = {"rep": device % lax.axis_size("rep"), "dp": device // lax.axis_size("rep")}
        block = 0
        for axis, place in self.steps[chunk]:
            block = 2 * block + (ranks[axis] >> place & 1)
        sizes = [v << self.count for v in self.sizes]
        return sum(sizes[:chunk]) + block * self.sizes[chunk]

    def widen(self):
        k = self.k
        share, got = self.order.tie(self.share, self.got)
        if any(v % SUB for v in self.sizes):
            pick = [bit(s[k]) == 0 for s in self.steps]
            self.share = [
                jnp.where(p, jnp.concatenate([v, g]), jnp.concatenate([g, v])) for p, v, g in zip(pick, share, got)
            ]
        else:
            self.share = widen_call(self.index(k), self.sizes, share, got, self.same(k - 1))
        self.sizes = [2 * v for v in self.sizes]
        self.order.done(self.share[0])
        self.k = k - 1
        self.got = self.send(k - 1, self.share)
        if k == 1:
            self.across = [swap(v, CORE) for v in self.share]

    def own(self):
        n = len(self.steps)
        return [(v, c, c, 2 * n) for c, v in enumerate(self.share)] + [(v, c, c, 2 * n + 1) for c, v in enumerate(self.across)]

    def arrived(self):
        n = len(self.steps)
        got = self.order.tie(*self.got)
        return [(v, c, n + c, 2 * n) for c, v in enumerate(got)] + [
            (swap(v, CORE), c, n + c, 2 * n + 1) for c, v in enumerate(got)
        ]

    def flags(self):
        mine = [bit(s[0]) for s in self.steps]
        core = bit(CORE)
        return jnp.stack(mine + [1 - i for i in mine] + [core, 1 - core]).astype(jnp.int32)


def spans_of(parts, low, high):
    found, start = [], 0
    for rows, target, row, col in parts:
        a, b = max(low, start), min(high, start + rows)
        if a < b:
            found.append((a - low, b - a, target, row + a - start, rows, col))
        start += rows
    return found


def deal(targets, gathered, sets, parts):
    n = len(targets)
    cols = gathered.shape[1]
    devices = lax.axis_size("dp") * lax.axis_size("rep")
    per = 4
    rows = gathered.shape[0] // devices
    moves = []
    for device in range(devices):
        mine, start = [], 0
        for p, layout in zip(sets, parts):
            for c, size in enumerate(p.sizes):
                low = p.origin(device, c)
                for first, count, target, row, whole, col in spans_of(layout, low, low + size):
                    mine.append((start + first, count, target, row + device % 2 * whole, col))
                start += size
        moves.append(mine)
    most = max(sum(len(m) for m in moves[g : g + per]) for g in range(0, devices, per))

    def body(*refs):
        value, outs, sem = refs[n], refs[n + 1 : -1], refs[-1]
        for g in range(0, devices, per):
            @pl.when(pl.program_id(0) == g // per)
            def _():
                copies = []
                for d in range(per):
                    for first, count, target, row, col in moves[g + d]:
                        copies.append(pltpu.make_async_copy(
                            value.at[pl.ds(d * rows + first, count), :],
                            outs[target].at[pl.ds(row, count), pl.ds(col, cols)],
                            sem.at[len(copies)],
                        ))
                        copies[-1].start()
                for copy in copies:
                    copy.wait()

    return pl.pallas_call(
        body,
        out_shape=[jax.ShapeDtypeStruct(t.shape, F32) for t in targets],
        grid=(devices // per,),
        in_specs=[pl.BlockSpec(memory_space=pltpu.HBM)] * n + [pl.BlockSpec((per * rows, cols), lambda i: (i, 0))],
        out_specs=[pl.BlockSpec(memory_space=pltpu.HBM)] * n,
        scratch_shapes=[pltpu.SemaphoreType.DMA((most,))],
        input_output_aliases={k: k for k in range(n)},
        compiler_params=pltpu.CompilerParams(vmem_limit_bytes=60 * MIB),
        cost_estimate=CHEAP,
        name="deal",
    )(*targets, gathered)


SEQUENCE = (
    "front", "scan0", "out0", "scan1", "mixed", "p0.f", "out1", "back01", "p0.f", "p1.f", "back00", "p0.f", "p1.f", "back11",
    "p0.e", "p1.f", "back10", "p1.e", "ag", "post0", "post1", "out2", "gn",
    "p2.f", "p2.f", "p2.f", "p2.e", "p2.b", "p2.w", "p2.w", "p2.w", "deal", "p2.own", "p2.got",
)
PARTS = 2


def shards(
    tokens, cotangent, lengths, norm_gain, in_weight, conv_weight, conv_bias, xproj_weight,
    dt_weight, dt_bias, decay_log, skip_gain, out_weight,
):
    tok, cot = tokens[0], cotangent[0]
    length, model = tok.shape
    taps, width = conv_weight.shape
    states = decay_log.shape[0]
    rank = dt_weight.shape[0]
    cols = xproj_weight.shape[1]
    row = lambda v: v.reshape(1, -1)
    core = bit(CORE).astype(jnp.int32)[None]
    dlog3 = decay_log.reshape(states, width // LANES, LANES)
    turned = xproj_weight.T
    sizes = [cols, rank, states, 2, taps + 1]
    used = -(-sum(sizes) // SUB) * SUB
    gain_rows = model // 2 // (WIDE // LANES)
    order = Order()
    tie, done = order.tie, order.done
    sets = [Reduced(order, orders(*heads)) for heads in (("xyz", "yxz"), ("xyz", "yzx", "zxy"), ("xyz", "zxy", "yzx"))]
    low = model // 2
    third = 3 * model // 8
    heights = [[low, low], [third, third, model - 2 * third], [third, third, low]]
    parts = [[(WIDE // 2, 1, b * WIDE, 0), (low, 0, 0, width + b * WIDE)] for b in range(2)]
    parts.append([(low, 0, 0, 0), (low, 0, 0, WIDE), (used + gain_rows, 2, 0, 0)])
    state = {"targets": [blank((model, 2 * width)), blank((width, model)), blank((2 * (used + gain_rows), WIDE))]}
    scans, backs, posts, others, gains = {}, {}, {}, {}, {}

    def op_front():
        state["front"] = front(
            tok, cot, jnp.concatenate([lengths, core]), row(norm_gain), in_weight, conv_weight, row(conv_bias), turned
        )
        _, send, og, _, _, mp = state["front"]
        state["og"] = swap(og, CORE)
        state["normed"] = swap(send, CORE)
        done(mp)

    def op_scan(b):
        normed, _, og, _, act, mp = state["front"]
        mp, = tie(mp)
        scans[b] = scan(
            b, core, mp, normed, og, act, in_weight, out_weight, dt_weight, row(dt_bias), dlog3, row(skip_gain)
        )
        done(scans[b][0])
        others[b] = (swap(scans[b][2], CORE), swap(scans[b][3], CORE))

    def op_out(b):
        normed, _, og, _, _, _ = state["front"]
        if b < 2:
            own = [(scans[b][0], og), (normed, scans[b][1])]
            one, two = others[b]
            low = model // 2
            other = [
                ([(one, 0, low)], [(state["og"], 0, model)]),
                ([(state["normed"], 0, low)], [(one, low, one.shape[1] - low), (two, 0, two.shape[1])]),
            ]
            small = ()
        else:
            own = [(normed, posts[q][0]) for q in range(2)]
            other = [([(state["normed"], 0, model // 2)], [(others[2 + q], 0, WIDE)]) for q in range(2)]
            small = (posts[0][1], posts[1][1], others["small"])
        own, arrays, small = tie(own, [[[p[0] for p in pieces] for pieces in pair] for pair in other], small)
        other = [
            [[(a, *p[1:]) for a, p in zip(array, pieces)] for array, pieces in zip(pair, cut)]
            for pair, cut in zip(arrays, other)
        ]
        flags = jnp.concatenate([sets[b].index(0), core])
        if b < 2:
            got = outer(core, own, other, heights[b], flags, in_weight, ((1, width + b * WIDE),))
            gains[b] = got[-1]
        else:
            got = outer(
                core, own, other, heights[b], flags, in_weight, ((0, 0), (1, WIDE)), (gains[0], gains[1]), small
            )
        done(got[1])
        chunks = len(heights[b])
        sets[b].begin(got[0 : 2 * chunks : 2], got[1 : 2 * chunks : 2])

    def op_back(b, part):
        _, _, _, _, act, mp = state["front"]
        mp, = tie(mp)
        carry = backs[b, part + 1][4] if part < PARTS - 1 else None
        backs[b, part] = back(
            b, part, PARTS, mp, act, scans[b][5], scans[b][4], scans[b][6], dt_weight, dlog3, carry
        )
        done(backs[b, part][0])

    def op_post(b):
        _, _, _, inner, act, _ = state["front"]
        parts, every = tie([backs[b, k] for k in range(PARTS)], [backs[q, k][1:4:2] for q in range(2) for k in range(PARTS)])
        posts[b] = post(
            b, used, scans[b][4], act, inner, turned, conv_weight, row(conv_bias), row(skip_gain), parts[0][4], decay_log,
            [p[0] for p in parts], [p[2] for p in parts], [p[5] for p in parts], [v[0] for v in every], [v[1] for v in every],
        )
        done(posts[b][0])
        others[2 + b] = swap(posts[b][0], CORE)
        if b == 1:
            others["small"] = swap(jnp.where(core[0] == 0, posts[1][1], posts[0][1]), CORE)

    def op_gn():
        parts = tie(posts[0][0], posts[1][0], scans[0][1], scans[1][1])
        grad_projected = jnp.concatenate([v.astype(BF16) for v in parts], axis=1)
        grad_normed = dot(grad_projected, in_weight, ((1,), (1,)))
        x = tok.astype(F32)
        inv = lax.rsqrt(jnp.mean(x * x, axis=1, keepdims=True) + EPS)
        unit = x * inv
        grad_unit = grad_normed * norm_gain
        state["grad_tokens"] = cot.astype(F32) + inv * (
            grad_unit - unit * jnp.mean(grad_unit * unit, axis=1, keepdims=True)
        )
        done(state["grad_tokens"])

    def op_mixed():
        b0, b1 = tie(scans[0][0], scans[1][0])
        live = (jnp.arange(length) < lengths[0])[:, None]
        total = dot(jnp.concatenate([b0, b1], axis=1), out_weight)
        state["mixed"] = (tok.astype(F32) + jnp.where(live, total, 0.0)).astype(BF16)
        done(state["mixed"])

    def op_put(p, pieces):
        arrays, targets = tie([v[0] for v in pieces], state["targets"])
        pieces = [(a,) + v[1:] for a, v in zip(arrays, pieces)]
        state["targets"] = put(targets, pieces, parts[p], heights[p], sets[p].flags())
        done(state["targets"][0])

    def op_ag():
        state["split"] = all(v % SUB == 0 for p in sets[:2] for v in p.sizes)
        if state["split"]:
            mine = jnp.concatenate([p.share[0] for p in sets[:2]])
            state["gathered"] = lax.all_gather(mine, ("dp", "rep"), axis=0, tiled=True)
        else:
            for p in sets[:2]:
                p.back()

    def op_deal():
        if state["split"]:
            gathered, targets = tie(state["gathered"], state["targets"])
            state["targets"] = deal(targets, gathered, sets[:2], parts[:2])
            done(state["targets"][0])
            return
        for p in range(2):
            while sets[p].k > 0:
                sets[p].widen()
            op_put(p, sets[p].own())
            op_put(p, sets[p].arrived())

    for name in SEQUENCE:
        if name[0] == "p" and name[2] == ".":
            p, what = int(name[1]), name[3:]
            if what == "f":
                sets[p].fold()
            elif what == "e":
                sets[p].finish()
            elif what == "b":
                sets[p].back()
            elif what == "w":
                sets[p].widen()
            else:
                op_put(p, sets[p].own() if what == "own" else sets[p].arrived())
        elif name[:4] == "back":
            op_back(int(name[4]), int(name[5]))
        elif name[-1] in "012":
            {"scan": op_scan, "out": op_out, "post": op_post}[name[:-1]](int(name[-1]))
        else:
            {"front": op_front, "gn": op_gn, "mixed": op_mixed, "ag": op_ag, "deal": op_deal}[name]()

    grad_in, grad_out, small = state["targets"]
    lines = small.reshape(2, used + gain_rows, WIDE)
    grad_gain = jnp.sum(lines[:, used:].reshape(2, gain_rows, WIDE // LANES, LANES), axis=3)
    grad_gain = jnp.swapaxes(grad_gain, 1, 2).reshape(-1) / norm_gain
    small = jnp.concatenate([lines[0, :used], lines[1, :used]], axis=1)
    ends = [sum(sizes[: i + 1]) for i in range(len(sizes))]
    cut = [small[e - n : e] for e, n in zip(ends, sizes)]
    return (
        state["mixed"][None], state["grad_tokens"][None],
        grad_gain, grad_in, cut[4][:taps], cut[4][taps], cut[0].T, cut[1], cut[3][0],
        cut[2], cut[3][1], grad_out,
    )


def solution(mesh):
    rows = P(("dp", "rep"), None, None)
    return jax.shard_map(
        shards,
        mesh=mesh,
        in_specs=(rows, rows, P(("dp", "rep"))) + (P(),) * 10,
        out_specs=(rows, rows) + (P(),) * 10,
        check_vma=False,
    )
```

```python
import functools
import math
import jax
import jax.numpy as jnp
from jax import lax
from jax.experimental import pallas as pl
from jax.experimental.pallas import tpu as pltpu
from jax.sharding import PartitionSpec as P

F32 = jnp.float32
BF16 = jnp.bfloat16
EPS = 1e-05
LANES = 128
SUB = 8
WIDE = 1024
SEG = 16
MIB = 1024 * 1024
LOG2E = math.log2(math.e)
CHEAP = pl.CostEstimate(flops=1, bytes_accessed=1, transcendentals=0)


def dot(a, b, dims=((1,), (0,))):
    return lax.dot_general(a, b, (dims, ((), ())), preferred_element_type=F32)


def shifted(value, rows):
    if rows == 0:
        return value
    length = value.shape[0]
    index = lax.broadcasted_iota(jnp.int32, value.shape, 0)
    moved = pltpu.roll(value, rows % length, 0)
    keep = index >= rows if rows > 0 else index < length + rows
    return jnp.where(keep, moved, 0.0)


def conv_of(inner, cw_ref, cb_ref):
    taps = cw_ref.shape[0]
    total = cb_ref[...] + cw_ref[taps - 1 : taps, :] * inner
    for k in range(taps - 1):
        total = total + cw_ref[k : k + 1, :] * shifted(inner, taps - 1 - k)
    return total


def front_kernel(
    len_ref, tok_ref, cot_ref, gain_ref, w_ref, cw_ref, cb_ref, xp_ref,
    normed_ref, send_ref, og_ref, inner_ref, act_ref, mp_ref,
):
    @pl.when(pl.program_id(0) == 0)
    def _():
        x = tok_ref[...].astype(F32)
        inv = lax.rsqrt(jnp.mean(x * x, axis=1, keepdims=True) + EPS)
        normed = (x * inv * gain_ref[...]).astype(BF16)
        normed_ref[...] = normed
        low = x.shape[1] // 2
        send_ref[...] = jnp.where(len_ref[1] == 0, normed[:, low:], normed[:, :low]).astype(F32)
        row = lax.broadcasted_iota(jnp.int32, x.shape, 0)
        og_ref[...] = jnp.where(row < len_ref[0], cot_ref[...].astype(F32), 0.0)
        mp_ref[...] = jnp.zeros_like(mp_ref)

    inner = dot(normed_ref[...], w_ref[...])
    inner_ref[...] = inner
    conv = conv_of(inner, cw_ref, cb_ref)
    act = (conv * jax.nn.sigmoid(conv)).astype(BF16)
    act_ref[...] = act
    mp_ref[...] += dot(act, xp_ref[...], ((1,), (1,)))


def front(tokens, cot, lengths, gain, in_weight, cw, cb, xproj):
    length, model = tokens.shape
    width = cw.shape[1]
    cols = xproj.shape[0]
    blk = 512
    whole = lambda shape: pl.BlockSpec(shape, lambda j: (0, 0))
    part = lambda rows: pl.BlockSpec((rows, blk), lambda j: (0, j))
    return pl.pallas_call(
        front_kernel,
        grid=(width // blk,),
        in_specs=[
            pl.BlockSpec(memory_space=pltpu.SMEM),
            whole((length, model)), whole((length, model)), whole((1, model)),
            part(model), part(cw.shape[0]), part(1),
            part(cols),
        ],
        out_specs=[
            whole((length, model)), whole((length, model // 2)), whole((length, model)),
            part(length), part(length), whole((length, cols)),
        ],
        out_shape=[
            jax.ShapeDtypeStruct((length, model), BF16),
            jax.ShapeDtypeStruct((length, model // 2), F32),
            jax.ShapeDtypeStruct((length, model), F32),
            jax.ShapeDtypeStruct((length, width), F32),
            jax.ShapeDtypeStruct((length, width), BF16),
            jax.ShapeDtypeStruct((length, cols), F32),
        ],
        compiler_params=pltpu.CompilerParams(vmem_limit_bytes=60 * MIB),
        cost_estimate=CHEAP,
        name="front",
    )(lengths, tokens, cot, gain, in_weight, cw, cb, xproj)


def splat_rows(length, count):
    return -(-length // LANES) * count * LANES


def fill_splats(mp_ref, splat_ref, first, count):
    length, cols = mp_ref.shape
    for g in range(-(-length // LANES)):
        size = min(LANES, length - g * LANES)
        rows = mp_ref[pl.ds(g * LANES, size), :]
        rows = jnp.concatenate([rows, jnp.zeros((size, LANES - cols), F32)], axis=1)
        if size < LANES:
            rows = jnp.concatenate([rows, jnp.zeros((LANES - size, LANES), F32)], axis=0)
        turned = rows.T
        for n in range(count):
            line = jnp.broadcast_to(turned[first + n : first + n + 1, :], (LANES, LANES))
            splat_ref[pl.ds((g * count + n) * LANES, size), :] = line.T[:size]


def splat(splat_ref, tb, count, n, s):
    per = LANES // SUB
    row = tb // per * (count * LANES) + tb % per * SUB + (n * LANES + s)
    return jnp.broadcast_to(splat_ref[pl.ds(row, 1), :], (SUB, LANES))


def tile_rows(tb, s):
    return pl.ds(pl.multiple_of(tb * SUB * SUB, SUB * SUB) + s, SUB, stride=SUB)


def put_tiles(ref, j, value):
    for tb in range(value.shape[0] // SUB):
        ref[pl.ds(tb * SUB * SUB + j * SUB, SUB), :] = value[tb * SUB : (tb + 1) * SUB, :]


def get_tiles(ref, j, length):
    return jnp.concatenate(
        [ref[pl.ds(tb * SUB * SUB + j * SUB, SUB), :] for tb in range(length // SUB)], axis=0
    )


def scan_kernel(
    block, core_ref, mp_ref, act_ref, dtw_ref, dtb_ref, dlog_ref, skip_ref, normed_hbm, og_hbm, win_hbm, wout_hbm,
    branch_ref, ggp_ref, send_ref, more_ref, gs_ref, step_out, mark_out,
    splat_ref, u_ref, y_ref, a_ref, gate_ref, gb_ref, normed_ref, og_ref, wg_ref, wo_ref, step_ref, mark_ref, sems,
):
    length = mp_ref.shape[0]
    rank = dtw_ref.shape[0]
    states = a_ref.shape[0]
    both = 2 * states
    width = win_hbm.shape[1] // 2
    loads = [
        pltpu.make_async_copy(src, dst, sems.at[k])
        for k, (src, dst) in enumerate((
            (normed_hbm, normed_ref), (win_hbm.at[:, pl.ds(width + block * WIDE, WIDE)], wg_ref),
            (og_hbm, og_ref), (wout_hbm.at[pl.ds(block * WIDE, WIDE), :], wo_ref),
        ))
    ]
    for load in loads:
        load.start()
    fill_splats(mp_ref, splat_ref, rank, both)
    a_ref[...] = -jnp.exp(dlog_ref[...]) * LOG2E
    delta_in = mp_ref[:, :rank].astype(BF16)
    for j in range(WIDE // LANES):
        cols = pl.ds(j * LANES, LANES)
        pre = dot(delta_in, dtw_ref[:, cols]) + dtb_ref[:, cols]
        step = jnp.maximum(pre, 0.0) + jnp.log1p(jnp.exp(-jnp.abs(pre)))
        put_tiles(step_ref, j, step)
        put_tiles(u_ref, j, step * act_ref[:, cols].astype(F32))
    stores = [
        pltpu.make_async_copy(step_ref, step_out, sems.at[4]), pltpu.make_async_copy(mark_ref, mark_out, sems.at[5])
    ]
    stores[0].start()

    def body(seg, carry):
        h = list(carry)
        base = pl.multiple_of(seg * states * SUB, states * SUB)
        for n in range(states):
            mark_ref[pl.ds(base + n * SUB, SUB), :] = h[n]

        def eight(k, h):
            h = list(h)
            tb = seg * (SEG // SUB) + k
            for s in range(SUB):
                step = step_ref[tile_rows(tb, s), :]
                u = u_ref[tile_rows(tb, s), :]
                y = None
                for n in range(states):
                    f = jnp.exp2(step * a_ref[n])
                    h[n] = f * h[n] + u * splat(splat_ref, tb, both, n, s)
                    q = h[n] * splat(splat_ref, tb, both, states + n, s)
                    y = q if y is None else y + q
                y_ref[tile_rows(tb, s), :] = y
            return tuple(h)

        return lax.fori_loop(0, SEG // SUB, eight, tuple(h))

    zero = jnp.zeros((SUB, LANES), F32)
    lax.fori_loop(0, length // SEG, body, (zero,) * states)
    stores[1].start()

    for load in loads:
        load.wait()
    og = og_ref[...].astype(BF16)
    for k in range(WIDE // 256):
        cols = pl.ds(k * 256, 256)
        gate_ref[:, cols] = dot(normed_ref[...], wg_ref[:, cols])
        gb_ref[:, cols] = dot(og, wo_ref[cols, :], ((1,), (1,)))
    for j in range(WIDE // LANES):
        cols = pl.ds(j * LANES, LANES)
        gate = gate_ref[:, cols]
        gb = gb_ref[:, cols]
        summed = get_tiles(y_ref, j, length) + skip_ref[:, cols] * act_ref[:, cols].astype(F32)
        sig = jax.nn.sigmoid(gate)
        gate_act = gate * sig
        branch = (summed * gate_act).astype(BF16)
        branch_ref[:, cols] = branch
        into = pl.ds(j * LANES % (WIDE // 2), LANES)

        @pl.when((core_ref[0] == 0) == (j * LANES >= WIDE // 2))
        def _():
            send_ref[:, into] = branch.astype(F32)
        put_tiles(gs_ref, j, gb * gate_act)
        ggp = (gb * summed * (sig * (1.0 + gate * (1.0 - sig)))).astype(BF16)
        ggp_ref[:, cols] = ggp
        to = WIDE // 2 + j * LANES
        if to < 3 * WIDE // 4:
            send_ref[:, to : to + LANES] = ggp.astype(F32)
        else:
            to = to - 3 * WIDE // 4
            more_ref[:, to : to + LANES] = ggp.astype(F32)
    for store in stores:
        store.wait()


def scan(block, core, mp, normed, og, act, in_weight, out_weight, dtw, dtb, dlog, skip):
    length, model = normed.shape
    rank = dtw.shape[0]
    states = dlog.shape[0]
    whole = lambda shape: pl.BlockSpec(shape, lambda i: (0,) * len(shape))
    col = lambda rows: pl.BlockSpec((rows, WIDE), lambda i: (0, block))
    hbm = pl.BlockSpec(memory_space=pltpu.HBM)
    tiles = (length * SUB, LANES)
    marks = (length // SEG * states * SUB, LANES)
    flat = (length, WIDE)
    send = (length, 3 * WIDE // 4)
    shape = jax.ShapeDtypeStruct
    return pl.pallas_call(
        functools.partial(scan_kernel, block),
        grid=(1,),
        in_specs=[
            pl.BlockSpec(memory_space=pltpu.SMEM), whole(mp.shape), col(length), col(rank), col(1),
            pl.BlockSpec((states, SUB, LANES), lambda i: (0, block, 0)), col(1), hbm, hbm, hbm, hbm,
        ],
        out_specs=[whole(flat)] * 2 + [whole(send)] * 2 + [whole(tiles), hbm, hbm],
        out_shape=[shape(flat, BF16)] * 2 + [shape(send, F32)] * 2 + [shape(tiles, F32)] * 2 + [shape(marks, F32)],
        scratch_shapes=[
            pltpu.VMEM((splat_rows(length, 2 * states), LANES), F32),
            pltpu.VMEM(tiles, F32),
            pltpu.VMEM(tiles, F32),
            pltpu.VMEM((states, SUB, LANES), F32),
            pltpu.VMEM(flat, F32),
            pltpu.VMEM(flat, F32),
            pltpu.VMEM(normed.shape, BF16),
            pltpu.VMEM(og.shape, F32),
            pltpu.VMEM((model, WIDE), BF16),
            pltpu.VMEM((WIDE, model), BF16),
            pltpu.VMEM(tiles, F32),
            pltpu.VMEM(marks, F32),
            pltpu.SemaphoreType.DMA((6,)),
        ],
        compiler_params=pltpu.CompilerParams(vmem_limit_bytes=60 * MIB),
        cost_estimate=CHEAP,
        name=f"scan{block}",
    )(core, mp, act, dtw, dtb, dlog, skip, normed, og, in_weight, out_weight)


def back_kernel(
    first, mp_ref, act_ref, step_ref, gs_ref, mark_ref, dtw_ref, dlog_ref, *rest,
):
    if not first:
        carry_in, rest = rest[0], rest[1:]
    (
        gact_ref, gdelta_ref, gdtw_ref, gwr_ref, carry_ref, rows_ref, glin_ref,
        splat_ref, act_t_ref, gd_ref, gu_ref, a_ref, f_ref, h_ref, turn_ref, part_ref,
    ) = rest
    length = mp_ref.shape[0]
    rank = dtw_ref.shape[0]
    states = a_ref.shape[0]
    both = 2 * states
    fill_splats(mp_ref, splat_ref, rank, both)
    a_ref[...] = -jnp.exp(dlog_ref[...])
    for j in range(WIDE // LANES):
        put_tiles(act_t_ref, j, act_ref[:, pl.ds(j * LANES, LANES)].astype(F32))
    per = SEG // SUB

    groups = states // SUB
    if first:
        carry_ref[...] = jnp.zeros_like(carry_ref)
    else:
        carry_ref[...] = carry_in[...]

    def segment(i, _):
        seg = length // SEG - 1 - i
        for q in range(groups):
            mine = range(q * SUB, (q + 1) * SUB)
            rates = [a_ref[n] for n in mine]
            base = pl.multiple_of(seg * states * SUB, states * SUB)
            start = [mark_ref[pl.ds(base + n * SUB, SUB), :] for n in mine]
            for j in range(SUB):
                h_ref[0, j] = start[j]

            def again(k, hs):
                hs = list(hs)
                tb = seg * per + k
                for s in range(SUB):
                    step = step_ref[tile_rows(tb, s), :]
                    u = step * act_t_ref[tile_rows(tb, s), :]
                    step2 = step * LOG2E
                    for j, n in enumerate(mine):
                        f = jnp.exp2(step2 * rates[j])
                        f_ref[k * SUB + s, j] = f
                        hs[j] = f * hs[j] + u * splat(splat_ref, tb, both, n, s)
                        h_ref[k * SUB + s + 1, j] = hs[j]
                return tuple(hs)

            last = lax.fori_loop(0, per, again, tuple(start))

            def reverse(k2, carry):
                dhs, gas, now = (list(c) for c in carry)
                k = per - 1 - k2
                tb = seg * per + k
                for s in reversed(range(SUB)):
                    g = gs_ref[tile_rows(tb, s), :]
                    step = step_ref[tile_rows(tb, s), :]
                    u = step * act_t_ref[tile_rows(tb, s), :]
                    gd = gu = None
                    ws, rs = [], []
                    for j, n in enumerate(mine):
                        dh = dhs[j] + g * splat(splat_ref, tb, both, states + n, s)
                        before = h_ref[k * SUB + s, j]
                        rs.append(now[j] * g)
                        ws.append(dh * u)
                        t = dh * splat(splat_ref, tb, both, n, s)
                        gu = t if gu is None else gu + t
                        dhs[j] = dh * f_ref[k * SUB + s, j]
                        ga = dhs[j] * before
                        t = ga * rates[j]
                        gd = t if gd is None else gd + t
                        gas[j] = gas[j] + ga * step
                        now[j] = before
                    if q == 0:
                        gd_ref[tile_rows(tb, s), :] = gd
                        gu_ref[tile_rows(tb, s), :] = gu
                    else:
                        gd_ref[tile_rows(tb, s), :] = gd_ref[tile_rows(tb, s), :] + gd
                        gu_ref[tile_rows(tb, s), :] = gu_ref[tile_rows(tb, s), :] + gu
                    for slot, values in ((0, ws), (1, rs)):
                        at = (s * 2 + slot) * SUB * SUB
                        for j in range(SUB):
                            turn_ref[pl.ds(at + j * SUB, SUB), :] = values[j]
                        total = turn_ref[pl.ds(at, SUB, stride=SUB), :]
                        for j in range(1, SUB):
                            total = total + turn_ref[pl.ds(at + j, SUB, stride=SUB), :]
                        row = tb * (both * SUB) + (slot * states + q * SUB) * SUB + s
                        part_ref[pl.ds(row, SUB, stride=SUB), :] = total
                return (tuple(dhs), tuple(gas), tuple(now))

            begin = (
                tuple(carry_ref[0, n] for n in mine), tuple(carry_ref[1, n] for n in mine), last
            )
            dhs, gas, _ = lax.fori_loop(0, per, reverse, begin)
            for j, n in enumerate(mine):
                carry_ref[0, n] = dhs[j]
                carry_ref[1, n] = gas[j]
        return 0

    lax.fori_loop(0, length // SEG, segment, 0)
    row = lax.broadcasted_iota(jnp.int32, (2 * LANES, LANES), 0)
    lane = lax.broadcasted_iota(jnp.int32, (2 * LANES, LANES), 1)
    gwr = None
    for n in range(0, both, 2):
        pieces = []
        for k in range(2):
            pieces.append(jnp.concatenate(
                [part_ref[pl.ds((tb * both + n + k) * SUB, SUB), :] for tb in range(length // SUB)], axis=0
            ).astype(BF16))
        into = jnp.where(lane == rank + n + row // LANES, 1.0, 0.0).astype(BF16)
        term = dot(jnp.concatenate(pieces, axis=1), into)
        gwr = term if gwr is None else gwr + term
    gwr_ref[...] = gwr

    for j in range(WIDE // LANES):
        cols = pl.ds(j * LANES, LANES)
        act = act_ref[:, cols].astype(F32)
        step = get_tiles(step_ref, j, length)
        gs = get_tiles(gs_ref, j, length)
        gu = get_tiles(gu_ref, j, length)
        gstep = get_tiles(gd_ref, j, length) + gu * act
        gpre = gstep * (1.0 - jnp.exp(-step))
        glin_ref[:, cols] = gpre.astype(BF16)
        rows_ref[0:1, cols] = jnp.sum(gpre, axis=0, keepdims=True)
        rows_ref[1:2, cols] = jnp.sum(gs * act, axis=0, keepdims=True)
        gact_ref[:, cols] = gu * step
    delta_in = mp_ref[:, :rank].astype(BF16)
    gdtw_ref[...] = dot(delta_in, glin_ref[...], ((0,), (0,)))
    gdelta_ref[...] = dot(glin_ref[...], dtw_ref[...], ((1,), (1,)))


def back(block, part, parts, mp, act, step, gs, marks, dtw, dlog, carry=None):
    length = act.shape[0] // parts
    rank = dtw.shape[0]
    states = dlog.shape[0]
    first = carry is None
    whole = lambda shape: pl.BlockSpec(shape, lambda i: (0,) * len(shape))
    mine = lambda v: pl.BlockSpec((v.shape[0] // parts, v.shape[1]), lambda i: (part, 0))
    flat = jax.ShapeDtypeStruct((length, WIDE), F32)
    outs = [
        flat,
        jax.ShapeDtypeStruct((length, rank), F32),
        jax.ShapeDtypeStruct((rank, WIDE), F32),
        jax.ShapeDtypeStruct((length, LANES), F32),
        jax.ShapeDtypeStruct((2, states, SUB, LANES), F32),
        jax.ShapeDtypeStruct((2, WIDE), F32),
    ]
    tiles = pltpu.VMEM((length * SUB, LANES), F32)
    return pl.pallas_call(
        functools.partial(back_kernel, first),
        grid=(1,),
        in_specs=[
            mine(mp), pl.BlockSpec((length, WIDE), lambda i: (part, block)), mine(step), mine(gs), mine(marks),
            pl.BlockSpec((rank, WIDE), lambda i: (0, block)),
            pl.BlockSpec((states, SUB, LANES), lambda i: (0, block, 0)),
        ] + ([] if first else [whole(carry.shape)]),
        out_specs=[whole(o.shape) for o in outs],
        out_shape=outs,
        scratch_shapes=[
            pltpu.VMEM((length, WIDE), BF16),
            pltpu.VMEM((splat_rows(length, 2 * states), LANES), F32),
            tiles, tiles, tiles,
            pltpu.VMEM((states, SUB, LANES), F32),
            pltpu.VMEM((SEG, SUB, SUB, LANES), F32),
            pltpu.VMEM((SEG + 1, SUB, SUB, LANES), F32),
            pltpu.VMEM((2 * SUB * SUB * SUB, LANES), F32),
            pltpu.VMEM((length * 2 * states, LANES), F32),
        ],
        compiler_params=pltpu.CompilerParams(vmem_limit_bytes=36 * MIB),
        cost_estimate=CHEAP,
        name=f"back{block}{part}",
    )(mp, act, step, gs, marks, dtw, dlog, *([] if first else [carry]))


def post_kernel(
    parts, gs_ref, act_ref, inner_ref, xp_ref, cw_ref, cb_ref, skip_ref, carry_ref, dlog_ref, *rest,
):
    gact_refs, gdtw_refs, two_refs = rest[:parts], rest[parts : 2 * parts], rest[2 * parts : 3 * parts]
    gdelta_refs, gwr_refs = rest[3 * parts : 5 * parts], rest[5 * parts : 7 * parts]
    gi_ref, small_ref = rest[7 * parts :]
    total_of = lambda refs: sum([ref[...] for ref in refs[1:]], refs[0][...])
    length = act_ref.shape[0]
    taps = cw_ref.shape[0]
    states = dlog_ref.shape[0]
    lines = []
    for k in range(parts):
        delta = gdelta_refs[k][...] + gdelta_refs[parts + k][...]
        rest_of = (gwr_refs[k][...] + gwr_refs[parts + k][...])[:, : xp_ref.shape[0]]
        room = jnp.zeros((delta.shape[0], xp_ref.shape[0] - delta.shape[1]), F32)
        lines.append(jnp.concatenate([delta, room], axis=1) + rest_of)
    gmix = jnp.concatenate(lines, axis=0).astype(BF16)
    share = dot(gmix, xp_ref[...])
    sizes = [xp_ref.shape[0], gdtw_refs[0].shape[0], states, two_refs[0].shape[0]]
    ends = [sum(sizes[: i + 1]) for i in range(4)]
    small_ref[: ends[0], :] = dot(gmix, act_ref[...], ((0,), (0,)))
    small_ref[ends[0] : ends[1], :] = total_of(gdtw_refs)
    for n in range(states):
        for j in range(SUB):
            small_ref[ends[1] + n : ends[1] + n + 1, j * LANES : (j + 1) * LANES] = carry_ref[1, n, j : j + 1, :]
    small_ref[ends[1] : ends[2], :] = small_ref[ends[1] : ends[2], :] * -jnp.exp(dlog_ref[...])
    small_ref[ends[2] : ends[3], :] = total_of(two_refs)
    small_ref[ends[3] + taps + 1 :, :] = jnp.zeros((small_ref.shape[0] - ends[3] - taps - 1, WIDE), F32)
    for j in range(WIDE // LANES):
        cols = pl.ds(j * LANES, LANES)
        inner = inner_ref[:, cols]
        cw = cw_ref[:, cols]
        conv = conv_of(inner, cw, cb_ref[:, cols])
        sig = jax.nn.sigmoid(conv)
        gact = (
            get_tiles(gs_ref, j, length) * skip_ref[:, cols]
            + jnp.concatenate([ref[:, cols] for ref in gact_refs], axis=0)
            + share[:, j * LANES : (j + 1) * LANES]
        )
        gconv = gact * (sig * (1.0 + conv * (1.0 - sig)))
        at = ends[3]
        small_ref[at + taps : at + taps + 1, cols] = jnp.sum(gconv, axis=0, keepdims=True)
        total = None
        for k in range(taps):
            small_ref[at + k : at + k + 1, cols] = jnp.sum(
                gconv * shifted(inner, taps - 1 - k), axis=0, keepdims=True
            )
            term = cw[k : k + 1, :] * shifted(gconv, k + 1 - taps)
            total = term if total is None else total + term
        gi_ref[:, cols] = total


def post(block, lines, gs, act, inner, xproj, cw, cb, skip, carry, dlog, gact, gdtw, two, gdelta, gwr):
    length = act.shape[0]
    cols = xproj.shape[0]
    taps = cw.shape[0]
    whole = lambda shape: pl.BlockSpec(shape, lambda i: (0,) * len(shape))
    col = lambda rows, at: pl.BlockSpec((rows, WIDE), lambda i: (0, at))
    outs = [jax.ShapeDtypeStruct((length, WIDE), F32), jax.ShapeDtypeStruct((lines, WIDE), F32)]
    return pl.pallas_call(
        functools.partial(post_kernel, len(gact)),
        grid=(1,),
        in_specs=[
            whole(gs.shape), col(length, block), col(length, block),
            col(cols, block), col(taps, block), col(1, block), col(1, block),
            whole(carry.shape), col(dlog.shape[0], block),
        ] + [whole(v.shape) for v in [*gact, *gdtw, *two, *gdelta, *gwr]],
        out_specs=[whole(o.shape) for o in outs],
        out_shape=outs,
        compiler_params=pltpu.CompilerParams(vmem_limit_bytes=60 * MIB),
        cost_estimate=CHEAP,
        name=f"post{block}",
    )(gs, act, inner, xproj, cw, cb, skip, carry, dlog, *gact, *gdtw, *two, *gdelta, *gwr)


def outer(core, own, other, sizes, flags, weight=None, cols=(), gains=(), small=()):
    length = own[0][0].shape[0]
    low, wide = own[0][0].shape[1] // 2, own[0][1].shape[1]
    halves = [v // 2 for v in sizes for _ in range(2)]
    starts = [sum(halves[:k]) for k in range(len(halves))]
    blk = 256
    total = sum(sizes)
    at_core = len(sizes)
    big, moves = [], []
    for c in range(2):
        for k, pieces in enumerate(([(own[c][0], None, low)], other[c][0], [(own[c][1], 0, wide)], other[c][1])):
            to = 0
            for array, col, count in pieces:
                moves.append((len(big), 4 * c + k, col, to, count))
                big.append(array)
                to += count
    n_big = len(big)
    n_buf = 8
    with_gain = weight is not None
    extra = ([weight] if with_gain else []) + list(gains) + list(small)

    def body(flag_ref, *refs):
        ins, refs = refs[: n_big + len(extra)], refs[n_big + len(extra) :]
        outs, refs = refs[: len(halves) + with_gain], refs[len(halves) + with_gain :]
        bufs, refs = refs[:n_buf], refs[n_buf:]
        w_bufs, refs = (refs[: len(cols)], refs[len(cols) :])
        lefts, rights, result, sem_in, sem_w, sem_out = refs
        loads = []
        for k, buf, col, to, count in moves:
            col = pl.multiple_of(flag_ref[at_core] * low, LANES) if col is None else col
            loads.append(pltpu.make_async_copy(
                ins[k].at[:, pl.ds(col, count)], bufs[buf].at[:, pl.ds(to, count)], sem_in.at[k]
            ))
            loads[-1].start()
        w_loads = []
        for q, (c, col) in enumerate(cols):
            src = ins[n_big].at[pl.ds(pl.multiple_of(flag_ref[at_core] * low, SUB), low), pl.ds(col, wide)]
            w_loads.append(pltpu.make_async_copy(src, w_bufs[q], sem_w.at[q]))
            w_loads[-1].start()

        def copy(k, flip):
            c, h = k // 2, k % 2
            return pltpu.make_async_copy(
                result.at[pl.ds(starts[k], halves[k]), :], outs[2 * c + flip], sem_out.at[k]
            )

        def each(k, act):
            c, h = k // 2, k % 2
            for flip in range(2):
                @pl.when((flag_ref[c] == h) == bool(flip))
                def _():
                    getattr(copy(k, flip), act)()

        ready, sent = 0, 0
        gain = None
        for c in range(2):
            for k, buf, _, _, _ in moves:
                if buf // 4 == c:
                    loads[k].wait()
            lefts[:length] = bufs[4 * c][...].astype(BF16)
            lefts[length:] = bufs[4 * c + 1][...].astype(BF16)
            rights[:length] = bufs[4 * c + 2][...].astype(BF16)
            rights[length:] = bufs[4 * c + 3][...].astype(BF16)
            for m in range(0, low, blk):
                result[c * low + m : c * low + m + blk, :] = dot(lefts[:, m : m + blk], rights[...], ((0,), (0,)))
                ready = c * low + m + blk
                while sent < len(halves) and starts[sent] + halves[sent] <= ready:
                    each(sent, "start")
                    sent += 1
            for q, (pair, _) in enumerate(cols):
                if pair == c:
                    w_loads[q].wait()
                    for j in range(0, wide, LANES):
                        term = result[c * low : (c + 1) * low, j : j + LANES] * w_bufs[q][:, j : j + LANES].astype(F32)
                        gain = term if gain is None else gain + term
        if small:
            a, b, got = ins[-3:]
            lines = got.shape[0]
            result[2 * low : 2 * low + lines, :] = jnp.where(flag_ref[at_core] == 0, a[...], b[...]) + got[...]
            for ref in ins[n_big + 1 : n_big + 1 + len(gains)]:
                gain = gain + ref[...]
            rows = low // (wide // LANES)
            for j in range(wide // LANES):
                result[2 * low + lines : 2 * low + lines + rows, j * LANES : (j + 1) * LANES] = gain[j * rows : (j + 1) * rows]
            if 2 * low + lines + rows < total:
                result[2 * low + lines + rows :, :] = jnp.zeros((total - 2 * low - lines - rows, wide), F32)
        elif 2 * low < total:
            result[2 * low :, :] = jnp.zeros((total - 2 * low, wide), F32)
        if with_gain:
            outs[-1][...] = gain
        while sent < len(halves):
            each(sent, "start")
            sent += 1
        for k in range(len(halves)):
            each(k, "wait")

    hbm = pl.BlockSpec(memory_space=pltpu.HBM)
    vmem = lambda v: pl.BlockSpec(v.shape, lambda i, ix: (0, 0))
    out_shape = [jax.ShapeDtypeStruct((v // 2, wide), F32) for v in sizes for _ in range(2)]
    out_specs = [hbm] * len(out_shape)
    if with_gain:
        out_shape.append(jax.ShapeDtypeStruct((low, LANES), F32))
        out_specs.append(pl.BlockSpec((low, LANES), lambda i, ix: (0, 0)))
    buffers = [
        pltpu.VMEM((length, low if k % 4 < 2 else wide), own[k // 4][k % 4 // 2].dtype if k % 2 == 0 else F32) for k in range(n_buf)
    ] + [pltpu.VMEM((low, wide), BF16) for _ in cols]
    return pl.pallas_call(
        body,
        out_shape=out_shape,
        grid_spec=pltpu.PrefetchScalarGridSpec(
            num_scalar_prefetch=1, grid=(1,),
            in_specs=[hbm] * n_big + ([hbm] if with_gain else []) + [vmem(v) for v in [*gains, *small]],
            out_specs=out_specs,
            scratch_shapes=buffers + [
                pltpu.VMEM((2 * length, low), BF16), pltpu.VMEM((2 * length, wide), BF16), pltpu.VMEM((total, wide), F32),
                pltpu.SemaphoreType.DMA((n_big,)), pltpu.SemaphoreType.DMA((max(len(cols), 1),)),
                pltpu.SemaphoreType.DMA((len(halves),)),
            ],
        ),
        compiler_params=pltpu.CompilerParams(vmem_limit_bytes=60 * MIB),
        cost_estimate=CHEAP,
        name="outer",
    )(flags, *big, *extra)


def step_call(body, name, index, ins, in_specs, outs):
    return pl.pallas_call(
        body,
        out_shape=outs,
        grid_spec=pltpu.PrefetchScalarGridSpec(
            num_scalar_prefetch=1, grid=(1,), in_specs=in_specs,
            out_specs=[pl.BlockSpec(o.shape, lambda i, ix: (0, 0)) for o in outs],
        ),
        compiler_params=pltpu.CompilerParams(vmem_limit_bytes=20 * MIB),
        cost_estimate=CHEAP,
        name=name,
    )(index, *ins)


def rows_of(rows, cols):
    return jax.ShapeDtypeStruct((rows, cols), F32)


def fold_call(index, kept, got, merged):
    n = len(kept)
    ins, specs, sends, keeps = [], [], [], []
    for c in range(n):
        size, cols = kept[c].shape[0] // 2, kept[c].shape[1]
        base = 2 * c if len(got) < n else 0
        for flip in (0, 1):
            at = lambda i, ix, c=c, flip=flip, base=0: (base + (ix[c] if flip else 1 - ix[c]), 0)
            ins += [kept[c], got[c % len(got)]]
            specs += [pl.BlockSpec((size, cols), at), pl.BlockSpec((size, cols), functools.partial(at, base=base))]
        sends.append(rows_of(size, cols))
        keeps.append(rows_of(size, cols))
    sizes = [v.shape[0] for v in sends]
    if merged:
        sends = [rows_of(sum(sizes), cols)]

    def body(ix, *refs):
        outs = refs[4 * n :]
        for c in range(n):
            for flip in (0, 1):
                a, b = refs[4 * c + 2 * flip : 4 * c + 2 * flip + 2]
                if flip:
                    outs[len(sends) + c][...] = a[...] + b[...]
                elif merged:
                    outs[0][sum(sizes[:c]) : sum(sizes[: c + 1]), :] = a[...] + b[...]
                else:
                    outs[c][...] = a[...] + b[...]

    out = step_call(body, "fold", index, ins, specs, sends + keeps)
    return list(out[: len(sends)]), list(out[len(sends) :])


def last_call(index, kept, got):
    n = len(kept)
    sizes = [v.shape[0] for v in kept]
    cols = kept[0].shape[1]
    specs = [pl.BlockSpec(v.shape, lambda i, ix: (0, 0)) for v in [*kept, *got]]

    def body(ix, *refs):
        for c in range(n):
            at = slice(sum(sizes[:c]), sum(sizes[: c + 1]))
            refs[-1][at, :] = refs[c][...] + (refs[n + c][...] if len(got) == n else refs[n][at, :])

    return step_call(body, "last", index, [*kept, *got], specs, [rows_of(sum(sizes), cols)])[0]


def widen_call(index, sizes, share, got, merged):
    cols = share[0].shape[1]
    ins = [*share, *got]
    specs = [pl.BlockSpec(v.shape, lambda i, ix: (0, 0)) for v in ins]
    n = len(share)

    def body(ix, *refs):
        outs = refs[n + len(got) :]
        for c, size in enumerate(sizes):
            low = sum(sizes[:c])
            for side, at in ((refs[:n], ix[c]), (refs[n : n + len(got)], 1 - ix[c])):
                value = side[c][...] if len(side) == len(sizes) else side[0][low : low + size, :]
                if merged:
                    outs[0][pl.ds(pl.multiple_of(2 * low + at * size, SUB), size), :] = value
                else:
                    outs[c][pl.ds(pl.multiple_of(at * size, SUB), size), :] = value

    outs = [rows_of(2 * sum(sizes), cols)] if merged else [rows_of(2 * s, cols) for s in sizes]
    return list(step_call(body, "widen", index, ins, specs, outs))


def blank(shape):
    return pl.pallas_call(
        lambda ref: None, out_shape=jax.ShapeDtypeStruct(shape, F32),
        out_specs=pl.BlockSpec(memory_space=pltpu.HBM), name="blank",
        compiler_params=pltpu.CompilerParams(vmem_limit_bytes=16 * MIB), cost_estimate=CHEAP,
    )()


def put(targets, pieces, parts, sizes, flags):
    def spans(chunk, h):
        low = sum(sizes[:chunk]) + h * (sizes[chunk] // 2)
        return spans_of(parts, low, low + sizes[chunk] // 2)

    arrays = [p[0] for p in pieces]
    n = len(targets)
    sems = max(len(spans(p[1], h)) for p in pieces for h in range(2))

    def body(flag_ref, *refs):
        values = refs[n : n + len(arrays)]
        outs, sem = refs[n + len(arrays) : -1], refs[-1]

        def copies(k, h):
            _, chunk, _, at = pieces[k]
            made = []
            for q, (first, rows, target, row, per, col) in enumerate(spans(chunk, h)):
                to = outs[target].at[
                    pl.ds(pl.multiple_of(flag_ref[at] * per + row, SUB), rows), pl.ds(col, arrays[k].shape[1])
                ]
                made.append(pltpu.make_async_copy(values[k].at[pl.ds(first, rows), :], to, sem.at[k * sems + q]))
            return made

        for act in ("start", "wait"):
            for k in range(len(arrays)):
                for h in range(2):
                    @pl.when(flag_ref[pieces[k][2]] == h)
                    def _():
                        for copy in copies(k, h):
                            getattr(copy, act)()

    return pl.pallas_call(
        body,
        out_shape=[jax.ShapeDtypeStruct(t.shape, F32) for t in targets],
        grid_spec=pltpu.PrefetchScalarGridSpec(
            num_scalar_prefetch=1, grid=(1,),
            in_specs=[pl.BlockSpec(memory_space=pltpu.HBM)] * n
            + [pl.BlockSpec(a.shape, lambda i, ix: (0, 0)) for a in arrays],
            out_specs=[pl.BlockSpec(memory_space=pltpu.HBM)] * n,
            scratch_shapes=[pltpu.SemaphoreType.DMA((len(arrays) * sems,))],
        ),
        input_output_aliases={1 + k: k for k in range(n)},
        compiler_params=pltpu.CompilerParams(vmem_limit_bytes=20 * MIB),
        cost_estimate=CHEAP,
        name="put",
    )(flags, *targets, *arrays)


def bits_of(axis):
    return lax.axis_size(axis).bit_length() - 1


def bit(step):
    return (lax.axis_index(step[0]) >> step[1]) & 1


def swap(value, step):
    axis, place = step
    size = lax.axis_size(axis)
    return lax.ppermute(value, axis, [(i, i ^ (1 << place)) for i in range(size)])


CORE = ("rep", 0)


def orders(*heads):
    axes = {"x": ("dp", 0), "y": ("rep", 1), "z": ("dp", 1)}
    rest = [("dp", b) for b in range(2, bits_of("dp"))] + [("rep", b) for b in range(2, bits_of("rep"))]
    return [[axes[a] for a in head] + rest for head in heads]


class Order:
    def __init__(self):
        self.last = None

    def tie(self, *values):
        if self.last is None:
            return values
        return lax.optimization_barrier((values, self.last))[0]

    def done(self, value):
        self.last = value


class Reduced:
    def __init__(self, order, steps):
        self.order = order
        self.steps = steps
        self.count = len(steps[0])
        self.share = None

    def index(self, k):
        return jnp.stack([bit(s[k]) for s in self.steps]).astype(jnp.int32)

    def same(self, k):
        return all(s[k] == self.steps[0][k] for s in self.steps)

    def send(self, k, values):
        if len(values) == 1:
            return [swap(values[0], self.steps[0][k])]
        return [swap(v, s[k]) for v, s in zip(values, self.steps)]

    def begin(self, sends, keeps):
        self.k = 0
        self.kept = keeps
        self.got = self.send(0, sends)

    def fold(self):
        k = self.k + 1
        kept, got = self.order.tie(self.kept, self.got)
        if k == self.count:
            self.share = [last_call(self.index(0), kept, got)]
            self.sizes = [v.shape[0] for v in kept]
            if any(v % SUB for v in self.sizes):
                cut = [sum(self.sizes[:c]) for c in range(len(kept))]
                self.share = [lax.slice_in_dim(self.share[0], a, a + n) for a, n in zip(cut, self.sizes)]
            self.order.done(self.share[0])
            self.k = k - 1
            return
        equal = len({v.shape[0] for v in kept}) == 1
        merged = self.same(k) and (equal or k == self.count - 1)
        if any(v.shape[0] % (2 * SUB) for v in kept):
            if len(got) < len(kept):
                size = kept[0].shape[0]
                got = [lax.slice_in_dim(got[0], c * size, (c + 1) * size) for c in range(len(kept))]
            total = [a + b for a, b in zip(kept, got)]
            index = [bit(s[k]) for s in self.steps]
            half = lambda v, i: lax.dynamic_slice_in_dim(v, i * (v.shape[0] // 2), v.shape[0] // 2, 0)
            sends = [half(v, 1 - i) for v, i in zip(total, index)]
            self.kept = [half(v, i) for v, i in zip(total, index)]
        else:
            sends, self.kept = fold_call(self.index(k), kept, got, merged)
        self.order.done(self.kept[0])
        self.k = k
        self.got = self.send(k, sends)

    def finish(self):
        while self.share is None:
            self.fold()

    def back(self):
        self.got = self.send(self.k, self.share)
        while self.k > 3:
            self.widen()

    def widen(self):
        k = self.k
        share, got = self.order.tie(self.share, self.got)
        if any(v % SUB for v in self.sizes):
            pick = [bit(s[k]) == 0 for s in self.steps]
            self.share = [
                jnp.where(p, jnp.concatenate([v, g]), jnp.concatenate([g, v])) for p, v, g in zip(pick, share, got)
            ]
        else:
            self.share = widen_call(self.index(k), self.sizes, share, got, self.same(k - 1))
        self.sizes = [2 * v for v in self.sizes]
        self.order.done(self.share[0])
        self.k = k - 1
        self.got = self.send(k - 1, self.share)

    def own(self):
        n = len(self.steps)
        share = self.order.tie(*self.share)
        return [(v, c, c, 2 * n) for c, v in enumerate(share)] + [
            (swap(v, CORE), c, c, 2 * n + 1) for c, v in enumerate(share)
        ]

    def arrived(self):
        n = len(self.steps)
        got = self.order.tie(*self.got)
        return [(v, c, n + c, 2 * n) for c, v in enumerate(got)] + [
            (swap(v, CORE), c, n + c, 2 * n + 1) for c, v in enumerate(got)
        ]

    def flags(self):
        mine = [bit(s[0]) for s in self.steps]
        core = bit(CORE)
        return jnp.stack(mine + [1 - i for i in mine] + [core, 1 - core]).astype(jnp.int32)


def spans_of(parts, low, high):
    found, start = [], 0
    for rows, target, row, col in parts:
        a, b = max(low, start), min(high, start + rows)
        if a < b:
            found.append((a - low, b - a, target, row + a - start, rows, col))
        start += rows
    return found


SEQUENCE = (
    "front", "scan0", "out0", "scan1", "mixed", "p0.f", "out1", "p0.f", "back01", "p0.f", "back00", "p0.e", "p0.b", "p1.f",
    "back11", "p1.f", "p0.w", "back10", "p1.f", "p0.w", "post0", "p1.e", "p1.b", "p0.w", "post1", "out2", "p0.own", "p0.got",
    "p1.w", "p2.f", "p2.f", "p2.f", "p1.w", "gn", "p2.e", "p2.b", "p1.w", "p1.own", "p2.w", "p2.w", "p1.got", "p2.w",
    "p2.own", "p2.got",
)
PARTS = 2


def shards(
    tokens, cotangent, lengths, norm_gain, in_weight, conv_weight, conv_bias, xproj_weight,
    dt_weight, dt_bias, decay_log, skip_gain, out_weight,
):
    tok, cot = tokens[0], cotangent[0]
    length, model = tok.shape
    taps, width = conv_weight.shape
    states = decay_log.shape[0]
    rank = dt_weight.shape[0]
    cols = xproj_weight.shape[1]
    row = lambda v: v.reshape(1, -1)
    core = bit(CORE).astype(jnp.int32)[None]
    dlog3 = decay_log.reshape(states, width // LANES, LANES)
    turned = xproj_weight.T
    sizes = [cols, rank, states, 2, taps + 1]
    used = -(-sum(sizes) // SUB) * SUB
    gain_rows = model // 2 // (WIDE // LANES)
    order = Order()
    tie, done = order.tie, order.done
    sets = [Reduced(order, orders(*heads)) for heads in (("xyz", "yxz"), ("xyz", "yxz"), ("xyz", "zxy", "yzx"))]
    low = model // 2
    third = 3 * model // 8
    heights = [[low, low]] * 2 + [[third, third, low]]
    parts = [[(WIDE // 2, 1, b * WIDE, 0), (low, 0, 0, width + b * WIDE)] for b in range(2)]
    parts.append([(low, 0, 0, 0), (low, 0, 0, WIDE), (used + gain_rows, 2, 0, 0)])
    state = {"targets": [blank((model, 2 * width)), blank((width, model)), blank((2 * (used + gain_rows), WIDE))]}
    scans, backs, posts, others, gains = {}, {}, {}, {}, {}

    def op_front():
        state["front"] = front(
            tok, cot, jnp.concatenate([lengths, core]), row(norm_gain), in_weight, conv_weight, row(conv_bias), turned
        )
        _, send, og, _, _, mp = state["front"]
        state["og"] = swap(og, CORE)
        state["normed"] = swap(send, CORE)
        done(mp)

    def op_scan(b):
        normed, _, og, _, act, mp = state["front"]
        mp, = tie(mp)
        scans[b] = scan(
            b, core, mp, normed, og, act, in_weight, out_weight, dt_weight, row(dt_bias), dlog3, row(skip_gain)
        )
        done(scans[b][0])
        others[b] = (swap(scans[b][2], CORE), swap(scans[b][3], CORE))

    def op_out(b):
        normed, _, og, _, _, _ = state["front"]
        if b < 2:
            own = [(scans[b][0], og), (normed, scans[b][1])]
            one, two = others[b]
            low = model // 2
            other = [
                ([(one, 0, low)], [(state["og"], 0, model)]),
                ([(state["normed"], 0, low)], [(one, low, one.shape[1] - low), (two, 0, two.shape[1])]),
            ]
            small = ()
        else:
            own = [(normed, posts[q][0]) for q in range(2)]
            other = [([(state["normed"], 0, model // 2)], [(others[2 + q], 0, WIDE)]) for q in range(2)]
            small = (posts[0][1], posts[1][1], others["small"])
        own, arrays, small = tie(own, [[[p[0] for p in pieces] for pieces in pair] for pair in other], small)
        other = [
            [[(a, *p[1:]) for a, p in zip(array, pieces)] for array, pieces in zip(pair, cut)]
            for pair, cut in zip(arrays, other)
        ]
        flags = jnp.concatenate([sets[b].index(0), core])
        if b < 2:
            got = outer(core, own, other, heights[b], flags, in_weight, ((1, width + b * WIDE),))
            gains[b] = got[-1]
        else:
            got = outer(
                core, own, other, heights[b], flags, in_weight, ((0, 0), (1, WIDE)), (gains[0], gains[1]), small
            )
        done(got[1])
        chunks = len(heights[b])
        sets[b].begin(got[0 : 2 * chunks : 2], got[1 : 2 * chunks : 2])

    def op_back(b, part):
        _, _, _, _, act, mp = state["front"]
        mp, = tie(mp)
        carry = backs[b, part + 1][4] if part < PARTS - 1 else None
        backs[b, part] = back(
            b, part, PARTS, mp, act, scans[b][5], scans[b][4], scans[b][6], dt_weight, dlog3, carry
        )
        done(backs[b, part][0])

    def op_post(b):
        _, _, _, inner, act, _ = state["front"]
        parts, every = tie([backs[b, k] for k in range(PARTS)], [backs[q, k][1:4:2] for q in range(2) for k in range(PARTS)])
        posts[b] = post(
            b, used, scans[b][4], act, inner, turned, conv_weight, row(conv_bias), row(skip_gain), parts[0][4], decay_log,
            [p[0] for p in parts], [p[2] for p in parts], [p[5] for p in parts], [v[0] for v in every], [v[1] for v in every],
        )
        done(posts[b][0])
        others[2 + b] = swap(posts[b][0], CORE)
        if b == 1:
            others["small"] = swap(jnp.where(core[0] == 0, posts[1][1], posts[0][1]), CORE)

    def op_gn():
        parts = tie(posts[0][0], posts[1][0], scans[0][1], scans[1][1])
        grad_projected = jnp.concatenate([v.astype(BF16) for v in parts], axis=1)
        grad_normed = dot(grad_projected, in_weight, ((1,), (1,)))
        x = tok.astype(F32)
        inv = lax.rsqrt(jnp.mean(x * x, axis=1, keepdims=True) + EPS)
        unit = x * inv
        grad_unit = grad_normed * norm_gain
        state["grad_tokens"] = cot.astype(F32) + inv * (
            grad_unit - unit * jnp.mean(grad_unit * unit, axis=1, keepdims=True)
        )
        done(state["grad_tokens"])

    def op_mixed():
        b0, b1 = tie(scans[0][0], scans[1][0])
        live = (jnp.arange(length) < lengths[0])[:, None]
        total = dot(jnp.concatenate([b0, b1], axis=1), out_weight)
        state["mixed"] = (tok.astype(F32) + jnp.where(live, total, 0.0)).astype(BF16)
        done(state["mixed"])

    def op_put(p, pieces):
        arrays, targets = tie([v[0] for v in pieces], state["targets"])
        pieces = [(a,) + v[1:] for a, v in zip(arrays, pieces)]
        state["targets"] = put(targets, pieces, parts[p], heights[p], sets[p].flags())
        done(state["targets"][0])

    for name in SEQUENCE:
        if name[0] == "p" and name[2] == ".":
            p, what = int(name[1]), name[3:]
            if what == "f":
                sets[p].fold()
            elif what == "e":
                sets[p].finish()
            elif what == "b":
                sets[p].back()
            elif what == "w":
                sets[p].widen()
            else:
                op_put(p, sets[p].own() if what == "own" else sets[p].arrived())
        elif name[:4] == "back":
            op_back(int(name[4]), int(name[5]))
        elif name[-1] in "012":
            {"scan": op_scan, "out": op_out, "post": op_post}[name[:-1]](int(name[-1]))
        else:
            {"front": op_front, "gn": op_gn, "mixed": op_mixed}[name]()

    grad_in, grad_out, small = state["targets"]
    lines = small.reshape(2, used + gain_rows, WIDE)
    grad_gain = jnp.sum(lines[:, used:].reshape(2, gain_rows, WIDE // LANES, LANES), axis=3)
    grad_gain = jnp.swapaxes(grad_gain, 1, 2).reshape(-1) / norm_gain
    small = jnp.concatenate([lines[0, :used], lines[1, :used]], axis=1)
    ends = [sum(sizes[: i + 1]) for i in range(len(sizes))]
    cut = [small[e - n : e] for e, n in zip(ends, sizes)]
    return (
        state["mixed"][None], state["grad_tokens"][None],
        grad_gain, grad_in, cut[4][:taps], cut[4][taps], cut[0].T, cut[1], cut[3][0],
        cut[2], cut[3][1], grad_out,
    )


def solution(mesh):
    rows = P(("dp", "rep"), None, None)
    return jax.shard_map(
        shards,
        mesh=mesh,
        in_specs=(rows, rows, P(("dp", "rep"))) + (P(),) * 10,
        out_specs=(rows, rows) + (P(),) * 10,
        check_vma=False,
    )
```

```python
import functools
import math
import jax
import jax.numpy as jnp
from jax import lax
from jax.experimental import pallas as pl
from jax.experimental.pallas import tpu as pltpu
from jax.sharding import PartitionSpec as P

F32 = jnp.float32
BF16 = jnp.bfloat16
EPS = 1e-05
LANES = 128
SUB = 8
WIDE = 1024
SEG = 16
MIB = 1024 * 1024
LOG2E = math.log2(math.e)
CHEAP = pl.CostEstimate(flops=1, bytes_accessed=1, transcendentals=0)


def dot(a, b, dims=((1,), (0,))):
    return lax.dot_general(a, b, (dims, ((), ())), preferred_element_type=F32)


def shifted(value, rows):
    if rows == 0:
        return value
    length = value.shape[0]
    index = lax.broadcasted_iota(jnp.int32, value.shape, 0)
    moved = pltpu.roll(value, rows % length, 0)
    keep = index >= rows if rows > 0 else index < length + rows
    return jnp.where(keep, moved, 0.0)


def conv_of(inner, cw_ref, cb_ref):
    taps = cw_ref.shape[0]
    total = cb_ref[...] + cw_ref[taps - 1 : taps, :] * inner
    for k in range(taps - 1):
        total = total + cw_ref[k : k + 1, :] * shifted(inner, taps - 1 - k)
    return total


def front_kernel(
    len_ref, tok_ref, cot_ref, gain_ref, w_ref, cw_ref, cb_ref, xp_ref,
    normed_ref, send_ref, og_ref, inner_ref, act_ref, mp_ref,
):
    @pl.when(pl.program_id(0) == 0)
    def _():
        x = tok_ref[...].astype(F32)
        inv = lax.rsqrt(jnp.mean(x * x, axis=1, keepdims=True) + EPS)
        normed = (x * inv * gain_ref[...]).astype(BF16)
        normed_ref[...] = normed
        low = x.shape[1] // 2
        send_ref[...] = jnp.where(len_ref[1] == 0, normed[:, low:], normed[:, :low]).astype(F32)
        row = lax.broadcasted_iota(jnp.int32, x.shape, 0)
        og_ref[...] = jnp.where(row < len_ref[0], cot_ref[...].astype(F32), 0.0)
        mp_ref[...] = jnp.zeros_like(mp_ref)

    inner = dot(normed_ref[...], w_ref[...])
    inner_ref[...] = inner
    conv = conv_of(inner, cw_ref, cb_ref)
    act = (conv * jax.nn.sigmoid(conv)).astype(BF16)
    act_ref[...] = act
    mp_ref[...] += dot(act, xp_ref[...], ((1,), (1,)))


def front(tokens, cot, lengths, gain, in_weight, cw, cb, xproj):
    length, model = tokens.shape
    width = cw.shape[1]
    cols = xproj.shape[0]
    blk = 512
    whole = lambda shape: pl.BlockSpec(shape, lambda j: (0, 0))
    part = lambda rows: pl.BlockSpec((rows, blk), lambda j: (0, j))
    return pl.pallas_call(
        front_kernel,
        grid=(width // blk,),
        in_specs=[
            pl.BlockSpec(memory_space=pltpu.SMEM),
            whole((length, model)), whole((length, model)), whole((1, model)),
            part(model), part(cw.shape[0]), part(1),
            part(cols),
        ],
        out_specs=[
            whole((length, model)), whole((length, model // 2)), whole((length, model)),
            part(length), part(length), whole((length, cols)),
        ],
        out_shape=[
            jax.ShapeDtypeStruct((length, model), BF16),
            jax.ShapeDtypeStruct((length, model // 2), F32),
            jax.ShapeDtypeStruct((length, model), F32),
            jax.ShapeDtypeStruct((length, width), F32),
            jax.ShapeDtypeStruct((length, width), BF16),
            jax.ShapeDtypeStruct((length, cols), F32),
        ],
        compiler_params=pltpu.CompilerParams(vmem_limit_bytes=60 * MIB),
        cost_estimate=CHEAP,
        name="front",
    )(lengths, tokens, cot, gain, in_weight, cw, cb, xproj)


def splat_rows(length, count):
    return -(-length // LANES) * count * LANES


def fill_splats(mp_ref, splat_ref, first, count):
    length, cols = mp_ref.shape
    for g in range(-(-length // LANES)):
        size = min(LANES, length - g * LANES)
        rows = mp_ref[pl.ds(g * LANES, size), :]
        rows = jnp.concatenate([rows, jnp.zeros((size, LANES - cols), F32)], axis=1)
        if size < LANES:
            rows = jnp.concatenate([rows, jnp.zeros((LANES - size, LANES), F32)], axis=0)
        turned = rows.T
        for n in range(count):
            line = jnp.broadcast_to(turned[first + n : first + n + 1, :], (LANES, LANES))
            splat_ref[pl.ds((g * count + n) * LANES, size), :] = line.T[:size]


def splat(splat_ref, tb, count, n, s):
    per = LANES // SUB
    row = tb // per * (count * LANES) + tb % per * SUB + (n * LANES + s)
    return jnp.broadcast_to(splat_ref[pl.ds(row, 1), :], (SUB, LANES))


def tile_rows(tb, s):
    return pl.ds(pl.multiple_of(tb * SUB * SUB, SUB * SUB) + s, SUB, stride=SUB)


def put_tiles(ref, j, value):
    for tb in range(value.shape[0] // SUB):
        ref[pl.ds(tb * SUB * SUB + j * SUB, SUB), :] = value[tb * SUB : (tb + 1) * SUB, :]


def get_tiles(ref, j, length):
    return jnp.concatenate(
        [ref[pl.ds(tb * SUB * SUB + j * SUB, SUB), :] for tb in range(length // SUB)], axis=0
    )


def scan_kernel(
    block, core_ref, mp_ref, act_ref, dtw_ref, dtb_ref, dlog_ref, skip_ref, normed_hbm, og_hbm, win_hbm, wout_hbm,
    branch_ref, ggp_ref, send_ref, more_ref, gs_ref, step_out, mark_out,
    splat_ref, u_ref, y_ref, a_ref, gate_ref, gb_ref, normed_ref, og_ref, wg_ref, wo_ref, step_ref, mark_ref, sems,
):
    length = mp_ref.shape[0]
    rank = dtw_ref.shape[0]
    states = a_ref.shape[0]
    both = 2 * states
    width = win_hbm.shape[1] // 2
    loads = [
        pltpu.make_async_copy(src, dst, sems.at[k])
        for k, (src, dst) in enumerate((
            (normed_hbm, normed_ref), (win_hbm.at[:, pl.ds(width + block * WIDE, WIDE)], wg_ref),
            (og_hbm, og_ref), (wout_hbm.at[pl.ds(block * WIDE, WIDE), :], wo_ref),
        ))
    ]
    for load in loads:
        load.start()
    fill_splats(mp_ref, splat_ref, rank, both)
    a_ref[...] = -jnp.exp(dlog_ref[...]) * LOG2E
    delta_in = mp_ref[:, :rank].astype(BF16)
    for j in range(WIDE // LANES):
        cols = pl.ds(j * LANES, LANES)
        pre = dot(delta_in, dtw_ref[:, cols]) + dtb_ref[:, cols]
        step = jnp.maximum(pre, 0.0) + jnp.log1p(jnp.exp(-jnp.abs(pre)))
        put_tiles(step_ref, j, step)
        put_tiles(u_ref, j, step * act_ref[:, cols].astype(F32))
    stores = [
        pltpu.make_async_copy(step_ref, step_out, sems.at[4]), pltpu.make_async_copy(mark_ref, mark_out, sems.at[5])
    ]
    stores[0].start()

    def body(seg, carry):
        h = list(carry)
        base = pl.multiple_of(seg * states * SUB, states * SUB)
        for n in range(states):
            mark_ref[pl.ds(base + n * SUB, SUB), :] = h[n]

        def eight(k, h):
            h = list(h)
            tb = seg * (SEG // SUB) + k
            for s in range(SUB):
                step = step_ref[tile_rows(tb, s), :]
                u = u_ref[tile_rows(tb, s), :]
                y = None
                for n in range(states):
                    f = jnp.exp2(step * a_ref[n])
                    h[n] = f * h[n] + u * splat(splat_ref, tb, both, n, s)
                    q = h[n] * splat(splat_ref, tb, both, states + n, s)
                    y = q if y is None else y + q
                y_ref[tile_rows(tb, s), :] = y
            return tuple(h)

        return lax.fori_loop(0, SEG // SUB, eight, tuple(h))

    zero = jnp.zeros((SUB, LANES), F32)
    lax.fori_loop(0, length // SEG, body, (zero,) * states)
    stores[1].start()

    for load in loads:
        load.wait()
    og = og_ref[...].astype(BF16)
    for k in range(WIDE // 256):
        cols = pl.ds(k * 256, 256)
        gate_ref[:, cols] = dot(normed_ref[...], wg_ref[:, cols])
        gb_ref[:, cols] = dot(og, wo_ref[cols, :], ((1,), (1,)))
    for j in range(WIDE // LANES):
        cols = pl.ds(j * LANES, LANES)
        gate = gate_ref[:, cols]
        gb = gb_ref[:, cols]
        summed = get_tiles(y_ref, j, length) + skip_ref[:, cols] * act_ref[:, cols].astype(F32)
        sig = jax.nn.sigmoid(gate)
        gate_act = gate * sig
        branch = (summed * gate_act).astype(BF16)
        branch_ref[:, cols] = branch
        into = pl.ds(j * LANES % (WIDE // 2), LANES)

        @pl.when((core_ref[1] == 0) == (j * LANES >= WIDE // 2))
        def _():
            send_ref[:, into] = branch.astype(F32)
        put_tiles(gs_ref, j, gb * gate_act)
        ggp = (gb * summed * (sig * (1.0 + gate * (1.0 - sig)))).astype(BF16)
        ggp_ref[:, cols] = ggp
        to = WIDE // 2 + j * LANES
        if to < 3 * WIDE // 4:
            send_ref[:, to : to + LANES] = ggp.astype(F32)
        else:
            to = to - 3 * WIDE // 4
            more_ref[:, to : to + LANES] = ggp.astype(F32)
    for store in stores:
        store.wait()


def scan(block, core, mp, normed, og, act, in_weight, out_weight, dtw, dtb, dlog, skip):
    length, model = normed.shape
    rank = dtw.shape[0]
    states = dlog.shape[0]
    whole = lambda shape: pl.BlockSpec(shape, lambda i: (0,) * len(shape))
    col = lambda rows: pl.BlockSpec((rows, WIDE), lambda i: (0, block))
    hbm = pl.BlockSpec(memory_space=pltpu.HBM)
    tiles = (length * SUB, LANES)
    marks = (length // SEG * states * SUB, LANES)
    flat = (length, WIDE)
    send = (length, 3 * WIDE // 4)
    shape = jax.ShapeDtypeStruct
    return pl.pallas_call(
        functools.partial(scan_kernel, block),
        grid=(1,),
        in_specs=[
            pl.BlockSpec(memory_space=pltpu.SMEM), whole(mp.shape), col(length), col(rank), col(1),
            pl.BlockSpec((states, SUB, LANES), lambda i: (0, block, 0)), col(1), hbm, hbm, hbm, hbm,
        ],
        out_specs=[whole(flat)] * 2 + [whole(send)] * 2 + [whole(tiles), hbm, hbm],
        out_shape=[shape(flat, BF16)] * 2 + [shape(send, F32)] * 2 + [shape(tiles, F32)] * 2 + [shape(marks, F32)],
        scratch_shapes=[
            pltpu.VMEM((splat_rows(length, 2 * states), LANES), F32),
            pltpu.VMEM(tiles, F32),
            pltpu.VMEM(tiles, F32),
            pltpu.VMEM((states, SUB, LANES), F32),
            pltpu.VMEM(flat, F32),
            pltpu.VMEM(flat, F32),
            pltpu.VMEM(normed.shape, BF16),
            pltpu.VMEM(og.shape, F32),
            pltpu.VMEM((model, WIDE), BF16),
            pltpu.VMEM((WIDE, model), BF16),
            pltpu.VMEM(tiles, F32),
            pltpu.VMEM(marks, F32),
            pltpu.SemaphoreType.DMA((6,)),
        ],
        compiler_params=pltpu.CompilerParams(vmem_limit_bytes=60 * MIB),
        cost_estimate=CHEAP,
        name=f"scan{block}",
    )(core, mp, act, dtw, dtb, dlog, skip, normed, og, in_weight, out_weight)


def back_kernel(
    first, mp_ref, act_ref, step_ref, gs_ref, mark_ref, dtw_ref, dlog_ref, *rest,
):
    if not first:
        carry_in, rest = rest[0], rest[1:]
    (
        gact_ref, gdelta_ref, gdtw_ref, gwr_ref, carry_ref, rows_ref, glin_ref,
        splat_ref, act_t_ref, gd_ref, gu_ref, a_ref, f_ref, h_ref, turn_ref, part_ref,
    ) = rest
    length = mp_ref.shape[0]
    rank = dtw_ref.shape[0]
    states = a_ref.shape[0]
    both = 2 * states
    fill_splats(mp_ref, splat_ref, rank, both)
    a_ref[...] = -jnp.exp(dlog_ref[...])
    for j in range(WIDE // LANES):
        put_tiles(act_t_ref, j, act_ref[:, pl.ds(j * LANES, LANES)].astype(F32))
    per = SEG // SUB

    groups = states // SUB
    if first:
        carry_ref[...] = jnp.zeros_like(carry_ref)
    else:
        carry_ref[...] = carry_in[...]

    def segment(i, _):
        seg = length // SEG - 1 - i
        for q in range(groups):
            mine = range(q * SUB, (q + 1) * SUB)
            rates = [a_ref[n] for n in mine]
            base = pl.multiple_of(seg * states * SUB, states * SUB)
            start = [mark_ref[pl.ds(base + n * SUB, SUB), :] for n in mine]
            for j in range(SUB):
                h_ref[0, j] = start[j]

            def again(k, hs):
                hs = list(hs)
                tb = seg * per + k
                for s in range(SUB):
                    step = step_ref[tile_rows(tb, s), :]
                    u = step * act_t_ref[tile_rows(tb, s), :]
                    step2 = step * LOG2E
                    for j, n in enumerate(mine):
                        f = jnp.exp2(step2 * rates[j])
                        f_ref[k * SUB + s, j] = f
                        hs[j] = f * hs[j] + u * splat(splat_ref, tb, both, n, s)
                        h_ref[k * SUB + s + 1, j] = hs[j]
                return tuple(hs)

            last = lax.fori_loop(0, per, again, tuple(start))

            def reverse(k2, carry):
                dhs, gas, now = (list(c) for c in carry)
                k = per - 1 - k2
                tb = seg * per + k
                for s in reversed(range(SUB)):
                    g = gs_ref[tile_rows(tb, s), :]
                    step = step_ref[tile_rows(tb, s), :]
                    u = step * act_t_ref[tile_rows(tb, s), :]
                    gd = gu = None
                    ws, rs = [], []
                    for j, n in enumerate(mine):
                        dh = dhs[j] + g * splat(splat_ref, tb, both, states + n, s)
                        before = h_ref[k * SUB + s, j]
                        rs.append(now[j] * g)
                        ws.append(dh * u)
                        t = dh * splat(splat_ref, tb, both, n, s)
                        gu = t if gu is None else gu + t
                        dhs[j] = dh * f_ref[k * SUB + s, j]
                        ga = dhs[j] * before
                        t = ga * rates[j]
                        gd = t if gd is None else gd + t
                        gas[j] = gas[j] + ga * step
                        now[j] = before
                    if q == 0:
                        gd_ref[tile_rows(tb, s), :] = gd
                        gu_ref[tile_rows(tb, s), :] = gu
                    else:
                        gd_ref[tile_rows(tb, s), :] = gd_ref[tile_rows(tb, s), :] + gd
                        gu_ref[tile_rows(tb, s), :] = gu_ref[tile_rows(tb, s), :] + gu
                    for slot, values in ((0, ws), (1, rs)):
                        at = (s * 2 + slot) * SUB * SUB
                        for j in range(SUB):
                            turn_ref[pl.ds(at + j * SUB, SUB), :] = values[j]
                        total = turn_ref[pl.ds(at, SUB, stride=SUB), :]
                        for j in range(1, SUB):
                            total = total + turn_ref[pl.ds(at + j, SUB, stride=SUB), :]
                        row = tb * (both * SUB) + (slot * states + q * SUB) * SUB + s
                        part_ref[pl.ds(row, SUB, stride=SUB), :] = total
                return (tuple(dhs), tuple(gas), tuple(now))

            begin = (
                tuple(carry_ref[0, n] for n in mine), tuple(carry_ref[1, n] for n in mine), last
            )
            dhs, gas, _ = lax.fori_loop(0, per, reverse, begin)
            for j, n in enumerate(mine):
                carry_ref[0, n] = dhs[j]
                carry_ref[1, n] = gas[j]
        return 0

    lax.fori_loop(0, length // SEG, segment, 0)
    row = lax.broadcasted_iota(jnp.int32, (2 * LANES, LANES), 0)
    lane = lax.broadcasted_iota(jnp.int32, (2 * LANES, LANES), 1)
    gwr = None
    for n in range(0, both, 2):
        pieces = []
        for k in range(2):
            pieces.append(jnp.concatenate(
                [part_ref[pl.ds((tb * both + n + k) * SUB, SUB), :] for tb in range(length // SUB)], axis=0
            ).astype(BF16))
        into = jnp.where(lane == rank + n + row // LANES, 1.0, 0.0).astype(BF16)
        term = dot(jnp.concatenate(pieces, axis=1), into)
        gwr = term if gwr is None else gwr + term
    gwr_ref[...] = gwr

    for j in range(WIDE // LANES):
        cols = pl.ds(j * LANES, LANES)
        act = act_ref[:, cols].astype(F32)
        step = get_tiles(step_ref, j, length)
        gs = get_tiles(gs_ref, j, length)
        gu = get_tiles(gu_ref, j, length)
        gstep = get_tiles(gd_ref, j, length) + gu * act
        gpre = gstep * (1.0 - jnp.exp(-step))
        glin_ref[:, cols] = gpre.astype(BF16)
        rows_ref[0:1, cols] = jnp.sum(gpre, axis=0, keepdims=True)
        rows_ref[1:2, cols] = jnp.sum(gs * act, axis=0, keepdims=True)
        gact_ref[:, cols] = gu * step
    delta_in = mp_ref[:, :rank].astype(BF16)
    gdtw_ref[...] = dot(delta_in, glin_ref[...], ((0,), (0,)))
    gdelta_ref[...] = dot(glin_ref[...], dtw_ref[...], ((1,), (1,)))


def back(block, part, parts, mp, act, step, gs, marks, dtw, dlog, carry=None):
    length = act.shape[0] // parts
    rank = dtw.shape[0]
    states = dlog.shape[0]
    first = carry is None
    whole = lambda shape: pl.BlockSpec(shape, lambda i: (0,) * len(shape))
    mine = lambda v: pl.BlockSpec((v.shape[0] // parts, v.shape[1]), lambda i: (part, 0))
    flat = jax.ShapeDtypeStruct((length, WIDE), F32)
    outs = [
        flat,
        jax.ShapeDtypeStruct((length, rank), F32),
        jax.ShapeDtypeStruct((rank, WIDE), F32),
        jax.ShapeDtypeStruct((length, LANES), F32),
        jax.ShapeDtypeStruct((2, states, SUB, LANES), F32),
        jax.ShapeDtypeStruct((2, WIDE), F32),
    ]
    tiles = pltpu.VMEM((length * SUB, LANES), F32)
    return pl.pallas_call(
        functools.partial(back_kernel, first),
        grid=(1,),
        in_specs=[
            mine(mp), pl.BlockSpec((length, WIDE), lambda i: (part, block)), mine(step), mine(gs), mine(marks),
            pl.BlockSpec((rank, WIDE), lambda i: (0, block)),
            pl.BlockSpec((states, SUB, LANES), lambda i: (0, block, 0)),
        ] + ([] if first else [whole(carry.shape)]),
        out_specs=[whole(o.shape) for o in outs],
        out_shape=outs,
        scratch_shapes=[
            pltpu.VMEM((length, WIDE), BF16),
            pltpu.VMEM((splat_rows(length, 2 * states), LANES), F32),
            tiles, tiles, tiles,
            pltpu.VMEM((states, SUB, LANES), F32),
            pltpu.VMEM((SEG, SUB, SUB, LANES), F32),
            pltpu.VMEM((SEG + 1, SUB, SUB, LANES), F32),
            pltpu.VMEM((2 * SUB * SUB * SUB, LANES), F32),
            pltpu.VMEM((length * 2 * states, LANES), F32),
        ],
        compiler_params=pltpu.CompilerParams(vmem_limit_bytes=36 * MIB),
        cost_estimate=CHEAP,
        name=f"back{block}{part}",
    )(mp, act, step, gs, marks, dtw, dlog, *([] if first else [carry]))


def post_kernel(
    parts, gs_ref, act_ref, inner_ref, xp_ref, cw_ref, cb_ref, skip_ref, carry_ref, dlog_ref, *rest,
):
    gact_refs, gdtw_refs, two_refs = rest[:parts], rest[parts : 2 * parts], rest[2 * parts : 3 * parts]
    gdelta_refs, gwr_refs = rest[3 * parts : 5 * parts], rest[5 * parts : 7 * parts]
    gi_ref, small_ref = rest[7 * parts :]
    total_of = lambda refs: sum([ref[...] for ref in refs[1:]], refs[0][...])
    length = act_ref.shape[0]
    taps = cw_ref.shape[0]
    states = dlog_ref.shape[0]
    lines = []
    for k in range(parts):
        delta = gdelta_refs[k][...] + gdelta_refs[parts + k][...]
        rest_of = (gwr_refs[k][...] + gwr_refs[parts + k][...])[:, : xp_ref.shape[0]]
        room = jnp.zeros((delta.shape[0], xp_ref.shape[0] - delta.shape[1]), F32)
        lines.append(jnp.concatenate([delta, room], axis=1) + rest_of)
    gmix = jnp.concatenate(lines, axis=0).astype(BF16)
    share = dot(gmix, xp_ref[...])
    sizes = [xp_ref.shape[0], gdtw_refs[0].shape[0], states, two_refs[0].shape[0]]
    ends = [sum(sizes[: i + 1]) for i in range(4)]
    small_ref[: ends[0], :] = dot(gmix, act_ref[...], ((0,), (0,)))
    small_ref[ends[0] : ends[1], :] = total_of(gdtw_refs)
    for n in range(states):
        for j in range(SUB):
            small_ref[ends[1] + n : ends[1] + n + 1, j * LANES : (j + 1) * LANES] = carry_ref[1, n, j : j + 1, :]
    small_ref[ends[1] : ends[2], :] = small_ref[ends[1] : ends[2], :] * -jnp.exp(dlog_ref[...])
    small_ref[ends[2] : ends[3], :] = total_of(two_refs)
    small_ref[ends[3] + taps + 1 :, :] = jnp.zeros((small_ref.shape[0] - ends[3] - taps - 1, WIDE), F32)
    for j in range(WIDE // LANES):
        cols = pl.ds(j * LANES, LANES)
        inner = inner_ref[:, cols]
        cw = cw_ref[:, cols]
        conv = conv_of(inner, cw, cb_ref[:, cols])
        sig = jax.nn.sigmoid(conv)
        gact = (
            get_tiles(gs_ref, j, length) * skip_ref[:, cols]
            + jnp.concatenate([ref[:, cols] for ref in gact_refs], axis=0)
            + share[:, j * LANES : (j + 1) * LANES]
        )
        gconv = gact * (sig * (1.0 + conv * (1.0 - sig)))
        at = ends[3]
        small_ref[at + taps : at + taps + 1, cols] = jnp.sum(gconv, axis=0, keepdims=True)
        total = None
        for k in range(taps):
            small_ref[at + k : at + k + 1, cols] = jnp.sum(
                gconv * shifted(inner, taps - 1 - k), axis=0, keepdims=True
            )
            term = cw[k : k + 1, :] * shifted(gconv, k + 1 - taps)
            total = term if total is None else total + term
        gi_ref[:, cols] = total


def post(block, lines, gs, act, inner, xproj, cw, cb, skip, carry, dlog, gact, gdtw, two, gdelta, gwr):
    length = act.shape[0]
    cols = xproj.shape[0]
    taps = cw.shape[0]
    whole = lambda shape: pl.BlockSpec(shape, lambda i: (0,) * len(shape))
    col = lambda rows, at: pl.BlockSpec((rows, WIDE), lambda i: (0, at))
    outs = [jax.ShapeDtypeStruct((length, WIDE), F32), jax.ShapeDtypeStruct((lines, WIDE), F32)]
    return pl.pallas_call(
        functools.partial(post_kernel, len(gact)),
        grid=(1,),
        in_specs=[
            whole(gs.shape), col(length, block), col(length, block),
            col(cols, block), col(taps, block), col(1, block), col(1, block),
            whole(carry.shape), col(dlog.shape[0], block),
        ] + [whole(v.shape) for v in [*gact, *gdtw, *two, *gdelta, *gwr]],
        out_specs=[whole(o.shape) for o in outs],
        out_shape=outs,
        compiler_params=pltpu.CompilerParams(vmem_limit_bytes=60 * MIB),
        cost_estimate=CHEAP,
        name=f"post{block}",
    )(gs, act, inner, xproj, cw, cb, skip, carry, dlog, *gact, *gdtw, *two, *gdelta, *gwr)


def outer(own, other, sizes, flags, bits, weight=None, cols=(), gains=(), small=()):
    length = own[0][0].shape[0]
    low, wide = own[0][0].shape[1] // 2, own[0][1].shape[1]
    halves = [v // 2 for v in sizes for _ in range(2)]
    starts = [sum(halves[:k]) for k in range(len(halves))]
    blk = 256
    total = sum(sizes)
    at_core = 1
    big, moves = [], []
    for c in range(2):
        for k, pieces in enumerate(([(own[c][0], None, low)], other[c][0], [(own[c][1], 0, wide)], other[c][1])):
            to = 0
            for array, col, count in pieces:
                moves.append((len(big), 4 * c + k, col, to, count))
                big.append(array)
                to += count
    n_big = len(big)
    n_buf = 8
    with_gain = weight is not None
    extra = ([weight] if with_gain else []) + list(gains) + list(small)

    def body(flag_ref, *refs):
        ins, refs = refs[: n_big + len(extra)], refs[n_big + len(extra) :]
        outs, refs = refs[: len(halves) + with_gain], refs[len(halves) + with_gain :]
        bufs, refs = refs[:n_buf], refs[n_buf:]
        w_bufs, refs = (refs[: len(cols)], refs[len(cols) :])
        lefts, rights, result, sem_in, sem_w, sem_out = refs
        loads = []
        for k, buf, col, to, count in moves:
            col = pl.multiple_of(flag_ref[at_core] * low, LANES) if col is None else col
            loads.append(pltpu.make_async_copy(
                ins[k].at[:, pl.ds(col, count)], bufs[buf].at[:, pl.ds(to, count)], sem_in.at[k]
            ))
            loads[-1].start()
        w_loads = []
        for q, (c, col) in enumerate(cols):
            src = ins[n_big].at[pl.ds(pl.multiple_of(flag_ref[at_core] * low, SUB), low), pl.ds(col, wide)]
            w_loads.append(pltpu.make_async_copy(src, w_bufs[q], sem_w.at[q]))
            w_loads[-1].start()

        def copy(k, flip):
            c, h = k // 2, k % 2
            return pltpu.make_async_copy(
                result.at[pl.ds(starts[k], halves[k]), :], outs[2 * c + flip], sem_out.at[k]
            )

        def each(k, act):
            c, h = k // 2, k % 2
            for flip in range(2):
                @pl.when((flag_ref[bits[c]] == h) == bool(flip))
                def _():
                    getattr(copy(k, flip), act)()

        ready, sent = 0, 0
        gain = None
        for c in range(2):
            for k, buf, _, _, _ in moves:
                if buf // 4 == c:
                    loads[k].wait()
            lefts[:length] = bufs[4 * c][...].astype(BF16)
            lefts[length:] = bufs[4 * c + 1][...].astype(BF16)
            rights[:length] = bufs[4 * c + 2][...].astype(BF16)
            rights[length:] = bufs[4 * c + 3][...].astype(BF16)
            for m in range(0, low, blk):
                result[c * low + m : c * low + m + blk, :] = dot(lefts[:, m : m + blk], rights[...], ((0,), (0,)))
                ready = c * low + m + blk
                while sent < len(halves) and starts[sent] + halves[sent] <= ready:
                    each(sent, "start")
                    sent += 1
            for q, (pair, _) in enumerate(cols):
                if pair == c:
                    w_loads[q].wait()
                    for j in range(0, wide, LANES):
                        term = result[c * low : (c + 1) * low, j : j + LANES] * w_bufs[q][:, j : j + LANES].astype(F32)
                        gain = term if gain is None else gain + term
        if small:
            a, b, got = ins[-3:]
            lines = got.shape[0]
            result[2 * low : 2 * low + lines, :] = jnp.where(flag_ref[at_core] == 0, a[...], b[...]) + got[...]
            for ref in ins[n_big + 1 : n_big + 1 + len(gains)]:
                gain = gain + ref[...]
            rows = low // (wide // LANES)
            for j in range(wide // LANES):
                result[2 * low + lines : 2 * low + lines + rows, j * LANES : (j + 1) * LANES] = gain[j * rows : (j + 1) * rows]
            if 2 * low + lines + rows < total:
                result[2 * low + lines + rows :, :] = jnp.zeros((total - 2 * low - lines - rows, wide), F32)
        elif 2 * low < total:
            result[2 * low :, :] = jnp.zeros((total - 2 * low, wide), F32)
        if with_gain:
            outs[-1][...] = gain
        while sent < len(halves):
            each(sent, "start")
            sent += 1
        for k in range(len(halves)):
            each(k, "wait")

    hbm = pl.BlockSpec(memory_space=pltpu.HBM)
    vmem = lambda v: pl.BlockSpec(v.shape, lambda i, ix: (0, 0))
    out_shape = [jax.ShapeDtypeStruct((v // 2, wide), F32) for v in sizes for _ in range(2)]
    out_specs = [hbm] * len(out_shape)
    if with_gain:
        out_shape.append(jax.ShapeDtypeStruct((low, LANES), F32))
        out_specs.append(pl.BlockSpec((low, LANES), lambda i, ix: (0, 0)))
    buffers = [
        pltpu.VMEM((length, low if k % 4 < 2 else wide), own[k // 4][k % 4 // 2].dtype if k % 2 == 0 else F32) for k in range(n_buf)
    ] + [pltpu.VMEM((low, wide), BF16) for _ in cols]
    return pl.pallas_call(
        body,
        out_shape=out_shape,
        grid_spec=pltpu.PrefetchScalarGridSpec(
            num_scalar_prefetch=1, grid=(1,),
            in_specs=[hbm] * n_big + ([hbm] if with_gain else []) + [vmem(v) for v in [*gains, *small]],
            out_specs=out_specs,
            scratch_shapes=buffers + [
                pltpu.VMEM((2 * length, low), BF16), pltpu.VMEM((2 * length, wide), BF16), pltpu.VMEM((total, wide), F32),
                pltpu.SemaphoreType.DMA((n_big,)), pltpu.SemaphoreType.DMA((max(len(cols), 1),)),
                pltpu.SemaphoreType.DMA((len(halves),)),
            ],
        ),
        compiler_params=pltpu.CompilerParams(vmem_limit_bytes=60 * MIB),
        cost_estimate=CHEAP,
        name="outer",
    )(flags, *big, *extra)


def step_call(body, name, index, ins, in_specs, outs):
    return pl.pallas_call(
        body,
        out_shape=outs,
        grid_spec=pltpu.PrefetchScalarGridSpec(
            num_scalar_prefetch=1, grid=(1,), in_specs=in_specs,
            out_specs=[pl.BlockSpec(o.shape, lambda i, ix: (0, 0)) for o in outs],
        ),
        compiler_params=pltpu.CompilerParams(vmem_limit_bytes=20 * MIB),
        cost_estimate=CHEAP,
        name=name,
    )(index, *ins)


def rows_of(rows, cols):
    return jax.ShapeDtypeStruct((rows, cols), F32)


def fold_call(flags, at, kept, got, merged):
    n = len(kept)
    ins, specs, sends, keeps = [], [], [], []
    for c in range(n):
        size, cols = kept[c].shape[0] // 2, kept[c].shape[1]
        base = 2 * c if len(got) < n else 0
        for flip in (0, 1):
            block = lambda i, ix, p=at[c], flip=flip, base=0: (base + (ix[p] if flip else 1 - ix[p]), 0)
            ins += [kept[c], got[c % len(got)]]
            specs += [pl.BlockSpec((size, cols), block), pl.BlockSpec((size, cols), functools.partial(block, base=base))]
        sends.append(rows_of(size, cols))
        keeps.append(rows_of(size, cols))
    sizes = [v.shape[0] for v in sends]
    if merged:
        sends = [rows_of(sum(sizes), cols)]

    def body(ix, *refs):
        outs = refs[4 * n :]
        for c in range(n):
            for flip in (0, 1):
                a, b = refs[4 * c + 2 * flip : 4 * c + 2 * flip + 2]
                if flip:
                    outs[len(sends) + c][...] = a[...] + b[...]
                elif merged:
                    outs[0][sum(sizes[:c]) : sum(sizes[: c + 1]), :] = a[...] + b[...]
                else:
                    outs[c][...] = a[...] + b[...]

    out = step_call(body, "fold", flags, ins, specs, sends + keeps)
    return list(out[: len(sends)]), list(out[len(sends) :])


def last_call(flags, kept, got):
    n = len(kept)
    sizes = [v.shape[0] for v in kept]
    cols = kept[0].shape[1]
    specs = [pl.BlockSpec(v.shape, lambda i, ix: (0, 0)) for v in [*kept, *got]]

    def body(ix, *refs):
        for c in range(n):
            at = slice(sum(sizes[:c]), sum(sizes[: c + 1]))
            refs[-1][at, :] = refs[c][...] + (refs[n + c][...] if len(got) == n else refs[n][at, :])

    return step_call(body, "last", flags, [*kept, *got], specs, [rows_of(sum(sizes), cols)])[0]


def widen_call(flags, bits, sizes, share, got, merged):
    cols = share[0].shape[1]
    ins = [*share, *got]
    specs = [pl.BlockSpec(v.shape, lambda i, ix: (0, 0)) for v in ins]
    n = len(share)

    def body(ix, *refs):
        outs = refs[n + len(got) :]
        for c, size in enumerate(sizes):
            low = sum(sizes[:c])
            for side, at in ((refs[:n], ix[bits[c]]), (refs[n : n + len(got)], 1 - ix[bits[c]])):
                value = side[c][...] if len(side) == len(sizes) else side[0][low : low + size, :]
                if merged:
                    outs[0][pl.ds(pl.multiple_of(2 * low + at * size, SUB), size), :] = value
                else:
                    outs[c][pl.ds(pl.multiple_of(at * size, SUB), size), :] = value

    outs = [rows_of(2 * sum(sizes), cols)] if merged else [rows_of(2 * s, cols) for s in sizes]
    return list(step_call(body, "widen", flags, ins, specs, outs))


def blank(shape):
    return pl.pallas_call(
        lambda ref: None, out_shape=jax.ShapeDtypeStruct(shape, F32),
        out_specs=pl.BlockSpec(memory_space=pltpu.HBM), name="blank",
        compiler_params=pltpu.CompilerParams(vmem_limit_bytes=16 * MIB), cost_estimate=CHEAP,
    )()


def put(targets, pieces, parts, sizes, flags):
    def spans(chunk, h):
        low = sum(sizes[:chunk]) + h * (sizes[chunk] // 2)
        return spans_of(parts, low, low + sizes[chunk] // 2)

    arrays = [p[0] for p in pieces]
    n = len(targets)
    sems = max(len(spans(p[1], h)) for p in pieces for h in range(2))

    def body(flag_ref, *refs):
        values = refs[n : n + len(arrays)]
        outs, sem = refs[n + len(arrays) : -1], refs[-1]

        def copies(k, h):
            _, chunk, _, at = pieces[k]
            made = []
            for q, (first, rows, target, row, per, col) in enumerate(spans(chunk, h)):
                to = outs[target].at[
                    pl.ds(pl.multiple_of(flag_ref[at] * per + row, SUB), rows), pl.ds(col, arrays[k].shape[1])
                ]
                made.append(pltpu.make_async_copy(values[k].at[pl.ds(first, rows), :], to, sem.at[k * sems + q]))
            return made

        for act in ("start", "wait"):
            for k in range(len(arrays)):
                for h in range(2):
                    @pl.when(flag_ref[pieces[k][2]] == h)
                    def _():
                        for copy in copies(k, h):
                            getattr(copy, act)()

    return pl.pallas_call(
        body,
        out_shape=[jax.ShapeDtypeStruct(t.shape, F32) for t in targets],
        grid_spec=pltpu.PrefetchScalarGridSpec(
            num_scalar_prefetch=1, grid=(1,),
            in_specs=[pl.BlockSpec(memory_space=pltpu.HBM)] * n
            + [pl.BlockSpec(a.shape, lambda i, ix: (0, 0)) for a in arrays],
            out_specs=[pl.BlockSpec(memory_space=pltpu.HBM)] * n,
            scratch_shapes=[pltpu.SemaphoreType.DMA((len(arrays) * sems,))],
        ),
        input_output_aliases={1 + k: k for k in range(n)},
        compiler_params=pltpu.CompilerParams(vmem_limit_bytes=20 * MIB),
        cost_estimate=CHEAP,
        name="put",
    )(flags, *targets, *arrays)


def bits_of(axis):
    return lax.axis_size(axis).bit_length() - 1


def bit(step):
    return (lax.axis_index(step[0]) >> step[1]) & 1


def swap(value, step):
    axis, place = step
    size = lax.axis_size(axis)
    return lax.ppermute(value, axis, [(i, i ^ (1 << place)) for i in range(size)])


CORE = ("rep", 0)


def orders(*heads):
    axes = {"x": ("dp", 0), "y": ("rep", 1), "z": ("dp", 1)}
    rest = [("dp", b) for b in range(2, bits_of("dp"))] + [("rep", b) for b in range(2, bits_of("rep"))]
    return [[axes[a] for a in head] + rest for head in heads]


class Order:
    def __init__(self):
        self.last = None

    def tie(self, *values):
        if self.last is None:
            return values
        return lax.optimization_barrier((values, self.last))[0]

    def done(self, value):
        self.last = value


class Reduced:
    def __init__(self, order, steps, flags, where):
        self.order = order
        self.steps = steps
        self.flags = flags
        self.where = where
        self.count = len(steps[0])
        self.share = None

    def places(self, k):
        return [self.where[s[k]] for s in self.steps]

    def same(self, k):
        return all(s[k] == self.steps[0][k] for s in self.steps)

    def send(self, k, values):
        if len(values) == 1:
            return [swap(values[0], self.steps[0][k])]
        return [swap(v, s[k]) for v, s in zip(values, self.steps)]

    def begin(self, sends, keeps):
        self.k = 0
        self.kept = keeps
        self.got = self.send(0, sends)

    def fold(self):
        k = self.k + 1
        kept, got = self.order.tie(self.kept, self.got)
        if k == self.count:
            self.share = [last_call(self.flags, kept, got)]
            self.sizes = [v.shape[0] for v in kept]
            if any(v % SUB for v in self.sizes):
                cut = [sum(self.sizes[:c]) for c in range(len(kept))]
                self.share = [lax.slice_in_dim(self.share[0], a, a + n) for a, n in zip(cut, self.sizes)]
            self.order.done(self.share[0])
            self.k = k - 1
            return
        equal = len({v.shape[0] for v in kept}) == 1
        merged = self.same(k) and (equal or k == self.count - 1)
        if any(v.shape[0] % (2 * SUB) for v in kept):
            if len(got) < len(kept):
                size = kept[0].shape[0]
                got = [lax.slice_in_dim(got[0], c * size, (c + 1) * size) for c in range(len(kept))]
            total = [a + b for a, b in zip(kept, got)]
            index = [bit(s[k]) for s in self.steps]
            half = lambda v, i: lax.dynamic_slice_in_dim(v, i * (v.shape[0] // 2), v.shape[0] // 2, 0)
            sends = [half(v, 1 - i) for v, i in zip(total, index)]
            self.kept = [half(v, i) for v, i in zip(total, index)]
        else:
            sends, self.kept = fold_call(self.flags, self.places(k), kept, got, merged)
        self.order.done(self.kept[0])
        self.k = k
        self.got = self.send(k, sends)

    def finish(self):
        while self.share is None:
            self.fold()

    def back(self):
        self.got = self.send(self.k, self.share)
        while self.k > 3:
            self.widen()

    def widen(self):
        k = self.k
        share, got = self.order.tie(self.share, self.got)
        if any(v % SUB for v in self.sizes):
            pick = [bit(s[k]) == 0 for s in self.steps]
            self.share = [
                jnp.where(p, jnp.concatenate([v, g]), jnp.concatenate([g, v])) for p, v, g in zip(pick, share, got)
            ]
        else:
            self.share = widen_call(self.flags, self.places(k), self.sizes, share, got, self.same(k - 1))
        self.sizes = [2 * v for v in self.sizes]
        self.order.done(self.share[0])
        self.k = k - 1
        self.got = self.send(k - 1, self.share)

    def pieces(self, values, side):
        halves = [p + side for p in self.places(0)]
        values = self.order.tie(*values)
        return [(v, c, halves[c], 1) for c, v in enumerate(values)] + [
            (swap(v, CORE), c, halves[c], 2) for c, v in enumerate(values)
        ]

    def own(self):
        return self.pieces(self.share, 0)

    def arrived(self):
        return self.pieces(self.got, 1)


def spans_of(parts, low, high):
    found, start = [], 0
    for rows, target, row, col in parts:
        a, b = max(low, start), min(high, start + rows)
        if a < b:
            found.append((a - low, b - a, target, row + a - start, rows, col))
        start += rows
    return found


SEQUENCE = (
    "front", "scan0", "out0", "scan1", "mixed", "p0.f", "out1", "p0.f", "back01", "p0.f", "back00", "p0.e", "p0.b", "p1.f",
    "back11", "p1.f", "p0.w", "back10", "p1.f", "p0.w", "post0", "p1.e", "p1.b", "p0.w", "post1", "out2", "p0.own", "p0.got",
    "p1.w", "p2.f", "p2.f", "p2.f", "p1.w", "gn", "p2.e", "p2.b", "p1.w", "p1.own", "p2.w", "p2.w", "p1.got", "p2.w",
    "p2.own", "p2.got",
)
PARTS = 2


def shards(
    tokens, cotangent, lengths, norm_gain, in_weight, conv_weight, conv_bias, xproj_weight,
    dt_weight, dt_bias, decay_log, skip_gain, out_weight,
):
    tok, cot = tokens[0], cotangent[0]
    length, model = tok.shape
    taps, width = conv_weight.shape
    states = decay_log.shape[0]
    rank = dt_weight.shape[0]
    cols = xproj_weight.shape[1]
    row = lambda v: v.reshape(1, -1)
    core = bit(CORE).astype(jnp.int32)[None]
    dlog3 = decay_log.reshape(states, width // LANES, LANES)
    turned = xproj_weight.T
    sizes = [cols, rank, states, 2, taps + 1]
    used = -(-sum(sizes) // SUB) * SUB
    gain_rows = model // 2 // (WIDE // LANES)
    every = orders("xyz")[0]
    where = {s: 3 + 2 * k for k, s in enumerate(every)}
    marks = [lengths[0], core[0], 1 - core[0]]
    for s in every:
        marks += [bit(s), 1 - bit(s)]
    flags = jnp.stack([v.astype(jnp.int32) for v in marks])
    order = Order()
    tie, done = order.tie, order.done
    sets = [Reduced(order, orders(*heads), flags, where) for heads in (("xyz", "yxz"), ("xyz", "yxz"), ("xyz", "zxy", "yzx"))]
    low = model // 2
    third = 3 * model // 8
    heights = [[low, low]] * 2 + [[third, third, low]]
    parts = [[(WIDE // 2, 1, b * WIDE, 0), (low, 0, 0, width + b * WIDE)] for b in range(2)]
    parts.append([(low, 0, 0, 0), (low, 0, 0, WIDE), (used + gain_rows, 2, 0, 0)])
    state = {"targets": [blank((model, 2 * width)), blank((width, model)), blank((2 * (used + gain_rows), WIDE))]}
    scans, backs, posts, others, gains = {}, {}, {}, {}, {}

    def op_front():
        state["front"] = front(
            tok, cot, flags, row(norm_gain), in_weight, conv_weight, row(conv_bias), turned
        )
        _, send, og, _, _, mp = state["front"]
        state["og"] = swap(og, CORE)
        state["normed"] = swap(send, CORE)
        done(mp)

    def op_scan(b):
        normed, _, og, _, act, mp = state["front"]
        mp, = tie(mp)
        scans[b] = scan(
            b, flags, mp, normed, og, act, in_weight, out_weight, dt_weight, row(dt_bias), dlog3, row(skip_gain)
        )
        done(scans[b][0])
        others[b] = (swap(scans[b][2], CORE), swap(scans[b][3], CORE))

    def op_out(b):
        normed, _, og, _, _, _ = state["front"]
        if b < 2:
            own = [(scans[b][0], og), (normed, scans[b][1])]
            one, two = others[b]
            low = model // 2
            other = [
                ([(one, 0, low)], [(state["og"], 0, model)]),
                ([(state["normed"], 0, low)], [(one, low, one.shape[1] - low), (two, 0, two.shape[1])]),
            ]
            small = ()
        else:
            own = [(normed, posts[q][0]) for q in range(2)]
            other = [([(state["normed"], 0, model // 2)], [(others[2 + q], 0, WIDE)]) for q in range(2)]
            small = (posts[0][1], posts[1][1], others["small"])
        own, arrays, small = tie(own, [[[p[0] for p in pieces] for pieces in pair] for pair in other], small)
        other = [
            [[(a, *p[1:]) for a, p in zip(array, pieces)] for array, pieces in zip(pair, cut)]
            for pair, cut in zip(arrays, other)
        ]
        bits = sets[b].places(0)
        if b < 2:
            got = outer(own, other, heights[b], flags, bits, in_weight, ((1, width + b * WIDE),))
            gains[b] = got[-1]
        else:
            got = outer(
                own, other, heights[b], flags, bits, in_weight, ((0, 0), (1, WIDE)), (gains[0], gains[1]), small
            )
        done(got[1])
        chunks = len(heights[b])
        sets[b].begin(got[0 : 2 * chunks : 2], got[1 : 2 * chunks : 2])

    def op_back(b, part):
        _, _, _, _, act, mp = state["front"]
        mp, = tie(mp)
        carry = backs[b, part + 1][4] if part < PARTS - 1 else None
        backs[b, part] = back(
            b, part, PARTS, mp, act, scans[b][5], scans[b][4], scans[b][6], dt_weight, dlog3, carry
        )
        done(backs[b, part][0])

    def op_post(b):
        _, _, _, inner, act, _ = state["front"]
        parts, every = tie([backs[b, k] for k in range(PARTS)], [backs[q, k][1:4:2] for q in range(2) for k in range(PARTS)])
        posts[b] = post(
            b, used, scans[b][4], act, inner, turned, conv_weight, row(conv_bias), row(skip_gain), parts[0][4], decay_log,
            [p[0] for p in parts], [p[2] for p in parts], [p[5] for p in parts], [v[0] for v in every], [v[1] for v in every],
        )
        done(posts[b][0])
        others[2 + b] = swap(posts[b][0], CORE)
        if b == 1:
            others["small"] = swap(jnp.where(core[0] == 0, posts[1][1], posts[0][1]), CORE)

    def op_gn():
        parts = tie(posts[0][0], posts[1][0], scans[0][1], scans[1][1])
        grad_projected = jnp.concatenate([v.astype(BF16) for v in parts], axis=1)
        grad_normed = dot(grad_projected, in_weight, ((1,), (1,)))
        x = tok.astype(F32)
        inv = lax.rsqrt(jnp.mean(x * x, axis=1, keepdims=True) + EPS)
        unit = x * inv
        grad_unit = grad_normed * norm_gain
        state["grad_tokens"] = cot.astype(F32) + inv * (
            grad_unit - unit * jnp.mean(grad_unit * unit, axis=1, keepdims=True)
        )
        done(state["grad_tokens"])

    def op_mixed():
        b0, b1 = tie(scans[0][0], scans[1][0])
        live = (jnp.arange(length) < lengths[0])[:, None]
        total = dot(jnp.concatenate([b0, b1], axis=1), out_weight)
        state["mixed"] = (tok.astype(F32) + jnp.where(live, total, 0.0)).astype(BF16)
        done(state["mixed"])

    def op_put(p, pieces):
        arrays, targets = tie([v[0] for v in pieces], state["targets"])
        pieces = [(a,) + v[1:] for a, v in zip(arrays, pieces)]
        state["targets"] = put(targets, pieces, parts[p], heights[p], flags)
        done(state["targets"][0])

    for name in SEQUENCE:
        if name[0] == "p" and name[2] == ".":
            p, what = int(name[1]), name[3:]
            if what == "f":
                sets[p].fold()
            elif what == "e":
                sets[p].finish()
            elif what == "b":
                sets[p].back()
            elif what == "w":
                sets[p].widen()
            else:
                op_put(p, sets[p].own() if what == "own" else sets[p].arrived())
        elif name[:4] == "back":
            op_back(int(name[4]), int(name[5]))
        elif name[-1] in "012":
            {"scan": op_scan, "out": op_out, "post": op_post}[name[:-1]](int(name[-1]))
        else:
            {"front": op_front, "gn": op_gn, "mixed": op_mixed}[name]()

    grad_in, grad_out, small = state["targets"]
    lines = small.reshape(2, used + gain_rows, WIDE)
    grad_gain = jnp.sum(lines[:, used:].reshape(2, gain_rows, WIDE // LANES, LANES), axis=3)
    grad_gain = jnp.swapaxes(grad_gain, 1, 2).reshape(-1) / norm_gain
    small = jnp.concatenate([lines[0, :used], lines[1, :used]], axis=1)
    ends = [sum(sizes[: i + 1]) for i in range(len(sizes))]
    cut = [small[e - n : e] for e, n in zip(ends, sizes)]
    return (
        state["mixed"][None], state["grad_tokens"][None],
        grad_gain, grad_in, cut[4][:taps], cut[4][taps], cut[0].T, cut[1], cut[3][0],
        cut[2], cut[3][1], grad_out,
    )


def solution(mesh):
    rows = P(("dp", "rep"), None, None)
    return jax.shard_map(
        shards,
        mesh=mesh,
        in_specs=(rows, rows, P(("dp", "rep"))) + (P(),) * 10,
        out_specs=(rows, rows) + (P(),) * 10,
        check_vma=False,
    )
```

```python
import functools
import math
import jax
import jax.numpy as jnp
from jax import lax
from jax.experimental import pallas as pl
from jax.experimental.pallas import tpu as pltpu
from jax.sharding import PartitionSpec as P

F32 = jnp.float32
BF16 = jnp.bfloat16
EPS = 1e-05
LANES = 128
SUB = 8
WIDE = 1024
SEG = 16
MIB = 1024 * 1024
LOG2E = math.log2(math.e)
CHEAP = pl.CostEstimate(flops=1, bytes_accessed=1, transcendentals=0)


def dot(a, b, dims=((1,), (0,))):
    return lax.dot_general(a, b, (dims, ((), ())), preferred_element_type=F32)


def shifted(value, rows):
    if rows == 0:
        return value
    length = value.shape[0]
    index = lax.broadcasted_iota(jnp.int32, value.shape, 0)
    moved = pltpu.roll(value, rows % length, 0)
    keep = index >= rows if rows > 0 else index < length + rows
    return jnp.where(keep, moved, 0.0)


def conv_of(inner, cw_ref, cb_ref):
    taps = cw_ref.shape[0]
    total = cb_ref[...] + cw_ref[taps - 1 : taps, :] * inner
    for k in range(taps - 1):
        total = total + cw_ref[k : k + 1, :] * shifted(inner, taps - 1 - k)
    return total


def front_kernel(
    len_ref, tok_ref, cot_ref, gain_ref, w_ref, cw_ref, cb_ref, xp_ref,
    normed_ref, send_ref, og_ref, inner_ref, act_ref, mp_ref,
):
    @pl.when(pl.program_id(0) == 0)
    def _():
        x = tok_ref[...].astype(F32)
        inv = lax.rsqrt(jnp.mean(x * x, axis=1, keepdims=True) + EPS)
        normed = (x * inv * gain_ref[...]).astype(BF16)
        normed_ref[...] = normed
        low = x.shape[1] // 2
        send_ref[...] = jnp.where(len_ref[1] == 0, normed[:, low:], normed[:, :low]).astype(F32)
        row = lax.broadcasted_iota(jnp.int32, x.shape, 0)
        og_ref[...] = jnp.where(row < len_ref[0], cot_ref[...].astype(F32), 0.0)
        mp_ref[...] = jnp.zeros_like(mp_ref)

    inner = dot(normed_ref[...], w_ref[...])
    inner_ref[...] = inner
    conv = conv_of(inner, cw_ref, cb_ref)
    act = (conv * jax.nn.sigmoid(conv)).astype(BF16)
    act_ref[...] = act
    mp_ref[...] += dot(act, xp_ref[...], ((1,), (1,)))


def front(tokens, cot, lengths, gain, in_weight, cw, cb, xproj):
    length, model = tokens.shape
    width = cw.shape[1]
    cols = xproj.shape[0]
    blk = 512
    whole = lambda shape: pl.BlockSpec(shape, lambda j: (0, 0))
    part = lambda rows: pl.BlockSpec((rows, blk), lambda j: (0, j))
    return pl.pallas_call(
        front_kernel,
        grid=(width // blk,),
        in_specs=[
            pl.BlockSpec(memory_space=pltpu.SMEM),
            whole((length, model)), whole((length, model)), whole((1, model)),
            part(model), part(cw.shape[0]), part(1),
            part(cols),
        ],
        out_specs=[
            whole((length, model)), whole((length, model // 2)), whole((length, model)),
            part(length), part(length), whole((length, cols)),
        ],
        out_shape=[
            jax.ShapeDtypeStruct((length, model), BF16),
            jax.ShapeDtypeStruct((length, model // 2), F32),
            jax.ShapeDtypeStruct((length, model), F32),
            jax.ShapeDtypeStruct((length, width), F32),
            jax.ShapeDtypeStruct((length, width), BF16),
            jax.ShapeDtypeStruct((length, cols), F32),
        ],
        compiler_params=pltpu.CompilerParams(vmem_limit_bytes=60 * MIB),
        cost_estimate=CHEAP,
        name="front",
    )(lengths, tokens, cot, gain, in_weight, cw, cb, xproj)


def splat_rows(length, count):
    return -(-length // LANES) * count * LANES


def fill_splats(mp_ref, splat_ref, first, count):
    length, cols = mp_ref.shape
    for g in range(-(-length // LANES)):
        size = min(LANES, length - g * LANES)
        rows = mp_ref[pl.ds(g * LANES, size), :]
        rows = jnp.concatenate([rows, jnp.zeros((size, LANES - cols), F32)], axis=1)
        if size < LANES:
            rows = jnp.concatenate([rows, jnp.zeros((LANES - size, LANES), F32)], axis=0)
        turned = rows.T
        for n in range(count):
            line = jnp.broadcast_to(turned[first + n : first + n + 1, :], (LANES, LANES))
            splat_ref[pl.ds((g * count + n) * LANES, size), :] = line.T[:size]


def splat(splat_ref, tb, count, n, s):
    per = LANES // SUB
    row = tb // per * (count * LANES) + tb % per * SUB + (n * LANES + s)
    return jnp.broadcast_to(splat_ref[pl.ds(row, 1), :], (SUB, LANES))


def tile_rows(tb, s):
    return pl.ds(pl.multiple_of(tb * SUB * SUB, SUB * SUB) + s, SUB, stride=SUB)


def put_tiles(ref, j, value):
    for tb in range(value.shape[0] // SUB):
        ref[pl.ds(tb * SUB * SUB + j * SUB, SUB), :] = value[tb * SUB : (tb + 1) * SUB, :]


def get_tiles(ref, j, length):
    return jnp.concatenate(
        [ref[pl.ds(tb * SUB * SUB + j * SUB, SUB), :] for tb in range(length // SUB)], axis=0
    )


def scan_kernel(
    block, core_ref, mp_ref, act_ref, dtw_ref, dtb_ref, dlog_ref, skip_ref, normed_hbm, og_hbm, win_hbm, wout_hbm,
    branch_ref, ggp_ref, send_ref, more_ref, gs_ref, step_out, mark_out,
    splat_ref, u_ref, y_ref, a_ref, gate_ref, gb_ref, normed_ref, og_ref, wg_ref, wo_ref, step_ref, mark_ref, sems,
):
    length = mp_ref.shape[0]
    rank = dtw_ref.shape[0]
    states = a_ref.shape[0]
    both = 2 * states
    width = win_hbm.shape[1] // 2
    loads = [
        pltpu.make_async_copy(src, dst, sems.at[k])
        for k, (src, dst) in enumerate((
            (normed_hbm, normed_ref), (win_hbm.at[:, pl.ds(width + block * WIDE, WIDE)], wg_ref),
            (og_hbm, og_ref), (wout_hbm.at[pl.ds(block * WIDE, WIDE), :], wo_ref),
        ))
    ]
    for load in loads:
        load.start()
    fill_splats(mp_ref, splat_ref, rank, both)
    a_ref[...] = -jnp.exp(dlog_ref[...]) * LOG2E
    delta_in = mp_ref[:, :rank].astype(BF16)
    for j in range(WIDE // LANES):
        cols = pl.ds(j * LANES, LANES)
        pre = dot(delta_in, dtw_ref[:, cols]) + dtb_ref[:, cols]
        step = jnp.maximum(pre, 0.0) + jnp.log1p(jnp.exp(-jnp.abs(pre)))
        put_tiles(step_ref, j, step)
        put_tiles(u_ref, j, step * act_ref[:, cols].astype(F32))
    stores = [
        pltpu.make_async_copy(step_ref, step_out, sems.at[4]), pltpu.make_async_copy(mark_ref, mark_out, sems.at[5])
    ]
    stores[0].start()

    def body(seg, carry):
        h = list(carry)
        base = pl.multiple_of(seg * states * SUB, states * SUB)
        for n in range(states):
            mark_ref[pl.ds(base + n * SUB, SUB), :] = h[n]

        def eight(k, h):
            h = list(h)
            tb = seg * (SEG // SUB) + k
            for s in range(SUB):
                step = step_ref[tile_rows(tb, s), :]
                u = u_ref[tile_rows(tb, s), :]
                y = None
                for n in range(states):
                    f = jnp.exp2(step * a_ref[n])
                    h[n] = f * h[n] + u * splat(splat_ref, tb, both, n, s)
                    q = h[n] * splat(splat_ref, tb, both, states + n, s)
                    y = q if y is None else y + q
                y_ref[tile_rows(tb, s), :] = y
            return tuple(h)

        return lax.fori_loop(0, SEG // SUB, eight, tuple(h))

    zero = jnp.zeros((SUB, LANES), F32)
    lax.fori_loop(0, length // SEG, body, (zero,) * states)
    stores[1].start()

    for load in loads:
        load.wait()
    og = og_ref[...].astype(BF16)
    for k in range(WIDE // 256):
        cols = pl.ds(k * 256, 256)
        gate_ref[:, cols] = dot(normed_ref[...], wg_ref[:, cols])
        gb_ref[:, cols] = dot(og, wo_ref[cols, :], ((1,), (1,)))
    for j in range(WIDE // LANES):
        cols = pl.ds(j * LANES, LANES)
        gate = gate_ref[:, cols]
        gb = gb_ref[:, cols]
        summed = get_tiles(y_ref, j, length) + skip_ref[:, cols] * act_ref[:, cols].astype(F32)
        sig = jax.nn.sigmoid(gate)
        gate_act = gate * sig
        branch = (summed * gate_act).astype(BF16)
        branch_ref[:, cols] = branch
        into = pl.ds(j * LANES % (WIDE // 2), LANES)

        @pl.when((core_ref[1] == 0) == (j * LANES >= WIDE // 2))
        def _():
            send_ref[:, into] = branch.astype(F32)
        put_tiles(gs_ref, j, gb * gate_act)
        ggp = (gb * summed * (sig * (1.0 + gate * (1.0 - sig)))).astype(BF16)
        ggp_ref[:, cols] = ggp
        to = WIDE // 2 + j * LANES
        if to < 3 * WIDE // 4:
            send_ref[:, to : to + LANES] = ggp.astype(F32)
        else:
            to = to - 3 * WIDE // 4
            more_ref[:, to : to + LANES] = ggp.astype(F32)
    for store in stores:
        store.wait()


def scan(block, core, mp, normed, og, act, in_weight, out_weight, dtw, dtb, dlog, skip):
    length, model = normed.shape
    rank = dtw.shape[0]
    states = dlog.shape[0]
    whole = lambda shape: pl.BlockSpec(shape, lambda i: (0,) * len(shape))
    col = lambda rows: pl.BlockSpec((rows, WIDE), lambda i: (0, block))
    hbm = pl.BlockSpec(memory_space=pltpu.HBM)
    tiles = (length * SUB, LANES)
    marks = (length // SEG * states * SUB, LANES)
    flat = (length, WIDE)
    send = (length, 3 * WIDE // 4)
    shape = jax.ShapeDtypeStruct
    return pl.pallas_call(
        functools.partial(scan_kernel, block),
        grid=(1,),
        in_specs=[
            pl.BlockSpec(memory_space=pltpu.SMEM), whole(mp.shape), col(length), col(rank), col(1),
            pl.BlockSpec((states, SUB, LANES), lambda i: (0, block, 0)), col(1), hbm, hbm, hbm, hbm,
        ],
        out_specs=[whole(flat)] * 2 + [whole(send)] * 2 + [whole(tiles), hbm, hbm],
        out_shape=[shape(flat, BF16)] * 2 + [shape(send, F32)] * 2 + [shape(tiles, F32)] * 2 + [shape(marks, F32)],
        scratch_shapes=[
            pltpu.VMEM((splat_rows(length, 2 * states), LANES), F32),
            pltpu.VMEM(tiles, F32),
            pltpu.VMEM(tiles, F32),
            pltpu.VMEM((states, SUB, LANES), F32),
            pltpu.VMEM(flat, F32),
            pltpu.VMEM(flat, F32),
            pltpu.VMEM(normed.shape, BF16),
            pltpu.VMEM(og.shape, F32),
            pltpu.VMEM((model, WIDE), BF16),
            pltpu.VMEM((WIDE, model), BF16),
            pltpu.VMEM(tiles, F32),
            pltpu.VMEM(marks, F32),
            pltpu.SemaphoreType.DMA((6,)),
        ],
        compiler_params=pltpu.CompilerParams(vmem_limit_bytes=60 * MIB),
        cost_estimate=CHEAP,
        name=f"scan{block}",
    )(core, mp, act, dtw, dtb, dlog, skip, normed, og, in_weight, out_weight)


def back_kernel(
    first, mp_ref, act_ref, step_ref, gs_ref, mark_ref, dtw_ref, dlog_ref, *rest,
):
    if not first:
        carry_in, rest = rest[0], rest[1:]
    (
        gact_ref, gdelta_ref, gdtw_ref, gwr_ref, carry_ref, rows_ref, glin_ref,
        splat_ref, act_t_ref, gd_ref, gu_ref, a_ref, f_ref, h_ref, turn_ref, part_ref,
    ) = rest
    length = mp_ref.shape[0]
    rank = dtw_ref.shape[0]
    states = a_ref.shape[0]
    both = 2 * states
    fill_splats(mp_ref, splat_ref, rank, both)
    a_ref[...] = -jnp.exp(dlog_ref[...])
    for j in range(WIDE // LANES):
        put_tiles(act_t_ref, j, act_ref[:, pl.ds(j * LANES, LANES)].astype(F32))
    per = SEG // SUB

    groups = states // SUB
    if first:
        carry_ref[...] = jnp.zeros_like(carry_ref)
    else:
        carry_ref[...] = carry_in[...]

    def segment(i, _):
        seg = length // SEG - 1 - i
        for q in range(groups):
            mine = range(q * SUB, (q + 1) * SUB)
            rates = [a_ref[n] for n in mine]
            base = pl.multiple_of(seg * states * SUB, states * SUB)
            start = [mark_ref[pl.ds(base + n * SUB, SUB), :] for n in mine]
            for j in range(SUB):
                h_ref[0, j] = start[j]

            def again(k, hs):
                hs = list(hs)
                tb = seg * per + k
                for s in range(SUB):
                    step = step_ref[tile_rows(tb, s), :]
                    u = step * act_t_ref[tile_rows(tb, s), :]
                    step2 = step * LOG2E
                    for j, n in enumerate(mine):
                        f = jnp.exp2(step2 * rates[j])
                        f_ref[k * SUB + s, j] = f
                        hs[j] = f * hs[j] + u * splat(splat_ref, tb, both, n, s)
                        h_ref[k * SUB + s + 1, j] = hs[j]
                return tuple(hs)

            last = lax.fori_loop(0, per, again, tuple(start))

            def reverse(k2, carry):
                dhs, gas, now = (list(c) for c in carry)
                k = per - 1 - k2
                tb = seg * per + k
                for s in reversed(range(SUB)):
                    g = gs_ref[tile_rows(tb, s), :]
                    step = step_ref[tile_rows(tb, s), :]
                    u = step * act_t_ref[tile_rows(tb, s), :]
                    gd = gu = None
                    ws, rs = [], []
                    for j, n in enumerate(mine):
                        dh = dhs[j] + g * splat(splat_ref, tb, both, states + n, s)
                        before = h_ref[k * SUB + s, j]
                        rs.append(now[j] * g)
                        ws.append(dh * u)
                        t = dh * splat(splat_ref, tb, both, n, s)
                        gu = t if gu is None else gu + t
                        dhs[j] = dh * f_ref[k * SUB + s, j]
                        ga = dhs[j] * before
                        t = ga * rates[j]
                        gd = t if gd is None else gd + t
                        gas[j] = gas[j] + ga * step
                        now[j] = before
                    if q == 0:
                        gd_ref[tile_rows(tb, s), :] = gd
                        gu_ref[tile_rows(tb, s), :] = gu
                    else:
                        gd_ref[tile_rows(tb, s), :] = gd_ref[tile_rows(tb, s), :] + gd
                        gu_ref[tile_rows(tb, s), :] = gu_ref[tile_rows(tb, s), :] + gu
                    for slot, values in ((0, ws), (1, rs)):
                        at = (s * 2 + slot) * SUB * SUB
                        for j in range(SUB):
                            turn_ref[pl.ds(at + j * SUB, SUB), :] = values[j]
                        total = turn_ref[pl.ds(at, SUB, stride=SUB), :]
                        for j in range(1, SUB):
                            total = total + turn_ref[pl.ds(at + j, SUB, stride=SUB), :]
                        row = tb * (both * SUB) + (slot * states + q * SUB) * SUB + s
                        part_ref[pl.ds(row, SUB, stride=SUB), :] = total
                return (tuple(dhs), tuple(gas), tuple(now))

            begin = (
                tuple(carry_ref[0, n] for n in mine), tuple(carry_ref[1, n] for n in mine), last
            )
            dhs, gas, _ = lax.fori_loop(0, per, reverse, begin)
            for j, n in enumerate(mine):
                carry_ref[0, n] = dhs[j]
                carry_ref[1, n] = gas[j]
        return 0

    lax.fori_loop(0, length // SEG, segment, 0)
    row = lax.broadcasted_iota(jnp.int32, (2 * LANES, LANES), 0)
    lane = lax.broadcasted_iota(jnp.int32, (2 * LANES, LANES), 1)
    gwr = None
    for n in range(0, both, 2):
        pieces = []
        for k in range(2):
            pieces.append(jnp.concatenate(
                [part_ref[pl.ds((tb * both + n + k) * SUB, SUB), :] for tb in range(length // SUB)], axis=0
            ).astype(BF16))
        into = jnp.where(lane == rank + n + row // LANES, 1.0, 0.0).astype(BF16)
        term = dot(jnp.concatenate(pieces, axis=1), into)
        gwr = term if gwr is None else gwr + term
    gwr_ref[...] = gwr

    for j in range(WIDE // LANES):
        cols = pl.ds(j * LANES, LANES)
        act = act_ref[:, cols].astype(F32)
        step = get_tiles(step_ref, j, length)
        gs = get_tiles(gs_ref, j, length)
        gu = get_tiles(gu_ref, j, length)
        gstep = get_tiles(gd_ref, j, length) + gu * act
        gpre = gstep * (1.0 - jnp.exp(-step))
        glin_ref[:, cols] = gpre.astype(BF16)
        rows_ref[0:1, cols] = jnp.sum(gpre, axis=0, keepdims=True)
        rows_ref[1:2, cols] = jnp.sum(gs * act, axis=0, keepdims=True)
        gact_ref[:, cols] = gu * step
    delta_in = mp_ref[:, :rank].astype(BF16)
    gdtw_ref[...] = dot(delta_in, glin_ref[...], ((0,), (0,)))
    gdelta_ref[...] = dot(glin_ref[...], dtw_ref[...], ((1,), (1,)))


def back(block, part, parts, mp, act, step, gs, marks, dtw, dlog, carry=None):
    length = act.shape[0] // parts
    rank = dtw.shape[0]
    states = dlog.shape[0]
    first = carry is None
    whole = lambda shape: pl.BlockSpec(shape, lambda i: (0,) * len(shape))
    mine = lambda v: pl.BlockSpec((v.shape[0] // parts, v.shape[1]), lambda i: (part, 0))
    flat = jax.ShapeDtypeStruct((length, WIDE), F32)
    outs = [
        flat,
        jax.ShapeDtypeStruct((length, rank), F32),
        jax.ShapeDtypeStruct((rank, WIDE), F32),
        jax.ShapeDtypeStruct((length, LANES), F32),
        jax.ShapeDtypeStruct((2, states, SUB, LANES), F32),
        jax.ShapeDtypeStruct((2, WIDE), F32),
    ]
    tiles = pltpu.VMEM((length * SUB, LANES), F32)
    return pl.pallas_call(
        functools.partial(back_kernel, first),
        grid=(1,),
        in_specs=[
            mine(mp), pl.BlockSpec((length, WIDE), lambda i: (part, block)), mine(step), mine(gs), mine(marks),
            pl.BlockSpec((rank, WIDE), lambda i: (0, block)),
            pl.BlockSpec((states, SUB, LANES), lambda i: (0, block, 0)),
        ] + ([] if first else [whole(carry.shape)]),
        out_specs=[whole(o.shape) for o in outs],
        out_shape=outs,
        scratch_shapes=[
            pltpu.VMEM((length, WIDE), BF16),
            pltpu.VMEM((splat_rows(length, 2 * states), LANES), F32),
            tiles, tiles, tiles,
            pltpu.VMEM((states, SUB, LANES), F32),
            pltpu.VMEM((SEG, SUB, SUB, LANES), F32),
            pltpu.VMEM((SEG + 1, SUB, SUB, LANES), F32),
            pltpu.VMEM((2 * SUB * SUB * SUB, LANES), F32),
            pltpu.VMEM((length * 2 * states, LANES), F32),
        ],
        compiler_params=pltpu.CompilerParams(vmem_limit_bytes=36 * MIB),
        cost_estimate=CHEAP,
        name=f"back{block}{part}",
    )(mp, act, step, gs, marks, dtw, dlog, *([] if first else [carry]))


def post_kernel(
    parts, gs_ref, act_ref, inner_ref, xp_ref, cw_ref, cb_ref, skip_ref, carry_ref, dlog_ref, *rest,
):
    gact_refs, gdtw_refs, two_refs = rest[:parts], rest[parts : 2 * parts], rest[2 * parts : 3 * parts]
    gdelta_refs, gwr_refs = rest[3 * parts : 5 * parts], rest[5 * parts : 7 * parts]
    gi_ref, small_ref = rest[7 * parts :]
    total_of = lambda refs: sum([ref[...] for ref in refs[1:]], refs[0][...])
    length = act_ref.shape[0]
    taps = cw_ref.shape[0]
    states = dlog_ref.shape[0]
    lines = []
    for k in range(parts):
        delta = gdelta_refs[k][...] + gdelta_refs[parts + k][...]
        rest_of = (gwr_refs[k][...] + gwr_refs[parts + k][...])[:, : xp_ref.shape[0]]
        room = jnp.zeros((delta.shape[0], xp_ref.shape[0] - delta.shape[1]), F32)
        lines.append(jnp.concatenate([delta, room], axis=1) + rest_of)
    gmix = jnp.concatenate(lines, axis=0).astype(BF16)
    share = dot(gmix, xp_ref[...])
    sizes = [xp_ref.shape[0], gdtw_refs[0].shape[0], states, two_refs[0].shape[0]]
    ends = [sum(sizes[: i + 1]) for i in range(4)]
    small_ref[: ends[0], :] = dot(gmix, act_ref[...], ((0,), (0,)))
    small_ref[ends[0] : ends[1], :] = total_of(gdtw_refs)
    for n in range(states):
        for j in range(SUB):
            small_ref[ends[1] + n : ends[1] + n + 1, j * LANES : (j + 1) * LANES] = carry_ref[1, n, j : j + 1, :]
    small_ref[ends[1] : ends[2], :] = small_ref[ends[1] : ends[2], :] * -jnp.exp(dlog_ref[...])
    small_ref[ends[2] : ends[3], :] = total_of(two_refs)
    small_ref[ends[3] + taps + 1 :, :] = jnp.zeros((small_ref.shape[0] - ends[3] - taps - 1, WIDE), F32)
    for j in range(WIDE // LANES):
        cols = pl.ds(j * LANES, LANES)
        inner = inner_ref[:, cols]
        cw = cw_ref[:, cols]
        conv = conv_of(inner, cw, cb_ref[:, cols])
        sig = jax.nn.sigmoid(conv)
        gact = (
            get_tiles(gs_ref, j, length) * skip_ref[:, cols]
            + jnp.concatenate([ref[:, cols] for ref in gact_refs], axis=0)
            + share[:, j * LANES : (j + 1) * LANES]
        )
        gconv = gact * (sig * (1.0 + conv * (1.0 - sig)))
        at = ends[3]
        small_ref[at + taps : at + taps + 1, cols] = jnp.sum(gconv, axis=0, keepdims=True)
        total = None
        for k in range(taps):
            small_ref[at + k : at + k + 1, cols] = jnp.sum(
                gconv * shifted(inner, taps - 1 - k), axis=0, keepdims=True
            )
            term = cw[k : k + 1, :] * shifted(gconv, k + 1 - taps)
            total = term if total is None else total + term
        gi_ref[:, cols] = total


def post(block, lines, gs, act, inner, xproj, cw, cb, skip, carry, dlog, gact, gdtw, two, gdelta, gwr):
    length = act.shape[0]
    cols = xproj.shape[0]
    taps = cw.shape[0]
    whole = lambda shape: pl.BlockSpec(shape, lambda i: (0,) * len(shape))
    col = lambda rows, at: pl.BlockSpec((rows, WIDE), lambda i: (0, at))
    outs = [jax.ShapeDtypeStruct((length, WIDE), F32), jax.ShapeDtypeStruct((lines, WIDE), F32)]
    return pl.pallas_call(
        functools.partial(post_kernel, len(gact)),
        grid=(1,),
        in_specs=[
            whole(gs.shape), col(length, block), col(length, block),
            col(cols, block), col(taps, block), col(1, block), col(1, block),
            whole(carry.shape), col(dlog.shape[0], block),
        ] + [whole(v.shape) for v in [*gact, *gdtw, *two, *gdelta, *gwr]],
        out_specs=[whole(o.shape) for o in outs],
        out_shape=outs,
        compiler_params=pltpu.CompilerParams(vmem_limit_bytes=60 * MIB),
        cost_estimate=CHEAP,
        name=f"post{block}",
    )(gs, act, inner, xproj, cw, cb, skip, carry, dlog, *gact, *gdtw, *two, *gdelta, *gwr)


def outer(own, other, sizes, flags, bits, weight=None, cols=(), gains=(), small=()):
    length = own[0][0].shape[0]
    low, wide = own[0][0].shape[1] // 2, own[0][1].shape[1]
    halves = [v // 2 for v in sizes for _ in range(2)]
    starts = [sum(halves[:k]) for k in range(len(halves))]
    blk = 256
    total = sum(sizes)
    at_core = 1
    big, moves = [], []
    for c in range(2):
        for k, pieces in enumerate(([(own[c][0], None, low)], other[c][0], [(own[c][1], 0, wide)], other[c][1])):
            to = 0
            for array, col, count in pieces:
                moves.append((len(big), 4 * c + k, col, to, count))
                big.append(array)
                to += count
    n_big = len(big)
    n_buf = 8
    with_gain = weight is not None
    extra = ([weight] if with_gain else []) + list(gains) + list(small)

    def body(flag_ref, *refs):
        ins, refs = refs[: n_big + len(extra)], refs[n_big + len(extra) :]
        outs, refs = refs[: len(halves) + with_gain], refs[len(halves) + with_gain :]
        bufs, refs = refs[:n_buf], refs[n_buf:]
        w_bufs, refs = (refs[: len(cols)], refs[len(cols) :])
        lefts, rights, result, sem_in, sem_w, sem_out = refs
        loads = []
        for k, buf, col, to, count in moves:
            col = pl.multiple_of(flag_ref[at_core] * low, LANES) if col is None else col
            loads.append(pltpu.make_async_copy(
                ins[k].at[:, pl.ds(col, count)], bufs[buf].at[:, pl.ds(to, count)], sem_in.at[k]
            ))
            loads[-1].start()
        w_loads = []
        for q, (c, col) in enumerate(cols):
            src = ins[n_big].at[pl.ds(pl.multiple_of(flag_ref[at_core] * low, SUB), low), pl.ds(col, wide)]
            w_loads.append(pltpu.make_async_copy(src, w_bufs[q], sem_w.at[q]))
            w_loads[-1].start()

        def copy(k, flip):
            c, h = k // 2, k % 2
            return pltpu.make_async_copy(
                result.at[pl.ds(starts[k], halves[k]), :], outs[2 * c + flip], sem_out.at[k]
            )

        def each(k, act):
            c, h = k // 2, k % 2
            for flip in range(2):
                @pl.when((flag_ref[bits[c]] == h) == bool(flip))
                def _():
                    getattr(copy(k, flip), act)()

        ready, sent = 0, 0
        gain = None
        for c in range(2):
            for k, buf, _, _, _ in moves:
                if buf // 4 == c:
                    loads[k].wait()
            lefts[:length] = bufs[4 * c][...].astype(BF16)
            lefts[length:] = bufs[4 * c + 1][...].astype(BF16)
            rights[:length] = bufs[4 * c + 2][...].astype(BF16)
            rights[length:] = bufs[4 * c + 3][...].astype(BF16)
            for m in range(0, low, blk):
                result[c * low + m : c * low + m + blk, :] = dot(lefts[:, m : m + blk], rights[...], ((0,), (0,)))
                ready = c * low + m + blk
                while sent < len(halves) and starts[sent] + halves[sent] <= ready:
                    each(sent, "start")
                    sent += 1
            for q, (pair, _) in enumerate(cols):
                if pair == c:
                    w_loads[q].wait()
                    for j in range(0, wide, LANES):
                        term = result[c * low : (c + 1) * low, j : j + LANES] * w_bufs[q][:, j : j + LANES].astype(F32)
                        gain = term if gain is None else gain + term
        if small:
            a, b, got = ins[-3:]
            lines = got.shape[0]
            result[2 * low : 2 * low + lines, :] = jnp.where(flag_ref[at_core] == 0, a[...], b[...]) + got[...]
            for ref in ins[n_big + 1 : n_big + 1 + len(gains)]:
                gain = gain + ref[...]
            rows = low // (wide // LANES)
            for j in range(wide // LANES):
                result[2 * low + lines : 2 * low + lines + rows, j * LANES : (j + 1) * LANES] = gain[j * rows : (j + 1) * rows]
            if 2 * low + lines + rows < total:
                result[2 * low + lines + rows :, :] = jnp.zeros((total - 2 * low - lines - rows, wide), F32)
        elif 2 * low < total:
            result[2 * low :, :] = jnp.zeros((total - 2 * low, wide), F32)
        if with_gain:
            outs[-1][...] = gain
        while sent < len(halves):
            each(sent, "start")
            sent += 1
        for k in range(len(halves)):
            each(k, "wait")

    hbm = pl.BlockSpec(memory_space=pltpu.HBM)
    vmem = lambda v: pl.BlockSpec(v.shape, lambda i, ix: (0, 0))
    out_shape = [jax.ShapeDtypeStruct((v // 2, wide), F32) for v in sizes for _ in range(2)]
    out_specs = [hbm] * len(out_shape)
    if with_gain:
        out_shape.append(jax.ShapeDtypeStruct((low, LANES), F32))
        out_specs.append(pl.BlockSpec((low, LANES), lambda i, ix: (0, 0)))
    buffers = [
        pltpu.VMEM((length, low if k % 4 < 2 else wide), own[k // 4][k % 4 // 2].dtype if k % 2 == 0 else F32) for k in range(n_buf)
    ] + [pltpu.VMEM((low, wide), BF16) for _ in cols]
    return pl.pallas_call(
        body,
        out_shape=out_shape,
        grid_spec=pltpu.PrefetchScalarGridSpec(
            num_scalar_prefetch=1, grid=(1,),
            in_specs=[hbm] * n_big + ([hbm] if with_gain else []) + [vmem(v) for v in [*gains, *small]],
            out_specs=out_specs,
            scratch_shapes=buffers + [
                pltpu.VMEM((2 * length, low), BF16), pltpu.VMEM((2 * length, wide), BF16), pltpu.VMEM((total, wide), F32),
                pltpu.SemaphoreType.DMA((n_big,)), pltpu.SemaphoreType.DMA((max(len(cols), 1),)),
                pltpu.SemaphoreType.DMA((len(halves),)),
            ],
        ),
        compiler_params=pltpu.CompilerParams(vmem_limit_bytes=60 * MIB),
        cost_estimate=CHEAP,
        name="outer",
    )(flags, *big, *extra)


def step_call(body, name, index, ins, in_specs, outs):
    return pl.pallas_call(
        body,
        out_shape=outs,
        grid_spec=pltpu.PrefetchScalarGridSpec(
            num_scalar_prefetch=1, grid=(1,), in_specs=in_specs,
            out_specs=[pl.BlockSpec(o.shape, lambda i, ix: (0, 0)) for o in outs],
        ),
        compiler_params=pltpu.CompilerParams(vmem_limit_bytes=20 * MIB),
        cost_estimate=CHEAP,
        name=name,
    )(index, *ins)


def rows_of(rows, cols):
    return jax.ShapeDtypeStruct((rows, cols), F32)


def fold_call(flags, at, kept, got, merged):
    n = len(kept)
    ins, specs, sends, keeps = [], [], [], []
    for c in range(n):
        size, cols = kept[c].shape[0] // 2, kept[c].shape[1]
        base = 2 * c if len(got) < n else 0
        for flip in (0, 1):
            block = lambda i, ix, p=at[c], flip=flip, base=0: (base + (ix[p] if flip else 1 - ix[p]), 0)
            ins += [kept[c], got[c % len(got)]]
            specs += [pl.BlockSpec((size, cols), block), pl.BlockSpec((size, cols), functools.partial(block, base=base))]
        sends.append(rows_of(size, cols))
        keeps.append(rows_of(size, cols))
    sizes = [v.shape[0] for v in sends]
    if merged:
        sends = [rows_of(sum(sizes), cols)]

    def body(ix, *refs):
        outs = refs[4 * n :]
        for c in range(n):
            for flip in (0, 1):
                a, b = refs[4 * c + 2 * flip : 4 * c + 2 * flip + 2]
                if flip:
                    outs[len(sends) + c][...] = a[...] + b[...]
                elif merged:
                    outs[0][sum(sizes[:c]) : sum(sizes[: c + 1]), :] = a[...] + b[...]
                else:
                    outs[c][...] = a[...] + b[...]

    out = step_call(body, "fold", flags, ins, specs, sends + keeps)
    return list(out[: len(sends)]), list(out[len(sends) :])


def last_call(flags, kept, got):
    n = len(kept)
    sizes = [v.shape[0] for v in kept]
    cols = kept[0].shape[1]
    specs = [pl.BlockSpec(v.shape, lambda i, ix: (0, 0)) for v in [*kept, *got]]

    def body(ix, *refs):
        for c in range(n):
            at = slice(sum(sizes[:c]), sum(sizes[: c + 1]))
            refs[-1][at, :] = refs[c][...] + (refs[n + c][...] if len(got) == n else refs[n][at, :])

    return step_call(body, "last", flags, [*kept, *got], specs, [rows_of(sum(sizes), cols)])[0]


def widen_call(flags, bits, sizes, share, got, merged):
    cols = share[0].shape[1]
    ins = [*share, *got]
    specs = [pl.BlockSpec(v.shape, lambda i, ix: (0, 0)) for v in ins]
    n = len(share)

    def body(ix, *refs):
        outs = refs[n + len(got) :]
        for c, size in enumerate(sizes):
            low = sum(sizes[:c])
            for side, at in ((refs[:n], ix[bits[c]]), (refs[n : n + len(got)], 1 - ix[bits[c]])):
                value = side[c][...] if len(side) == len(sizes) else side[0][low : low + size, :]
                if merged:
                    outs[0][pl.ds(pl.multiple_of(2 * low + at * size, SUB), size), :] = value
                else:
                    outs[c][pl.ds(pl.multiple_of(at * size, SUB), size), :] = value

    outs = [rows_of(2 * sum(sizes), cols)] if merged else [rows_of(2 * s, cols) for s in sizes]
    return list(step_call(body, "widen", flags, ins, specs, outs))


def blank(shape):
    return pl.pallas_call(
        lambda ref: None, out_shape=jax.ShapeDtypeStruct(shape, F32),
        out_specs=pl.BlockSpec(memory_space=pltpu.HBM), name="blank",
        compiler_params=pltpu.CompilerParams(vmem_limit_bytes=16 * MIB), cost_estimate=CHEAP,
    )()


def put(targets, pieces, parts, sizes, flags):
    def spans(chunk, h):
        low = sum(sizes[:chunk]) + h * (sizes[chunk] // 2)
        return spans_of(parts, low, low + sizes[chunk] // 2)

    arrays = [p[0] for p in pieces]
    n = len(targets)
    sems = max(len(spans(p[1], h)) for p in pieces for h in range(2))

    def body(flag_ref, *refs):
        values = refs[n : n + len(arrays)]
        outs, sem = refs[n + len(arrays) : -1], refs[-1]

        def copies(k, h):
            _, chunk, _, at = pieces[k]
            made = []
            for q, (first, rows, target, row, per, col) in enumerate(spans(chunk, h)):
                to = outs[target].at[
                    pl.ds(pl.multiple_of(flag_ref[at] * per + row, SUB), rows), pl.ds(col, arrays[k].shape[1])
                ]
                made.append(pltpu.make_async_copy(values[k].at[pl.ds(first, rows), :], to, sem.at[k * sems + q]))
            return made

        for act in ("start", "wait"):
            for k in range(len(arrays)):
                for h in range(2):
                    @pl.when(flag_ref[pieces[k][2]] == h)
                    def _():
                        for copy in copies(k, h):
                            getattr(copy, act)()

    return pl.pallas_call(
        body,
        out_shape=[jax.ShapeDtypeStruct(t.shape, F32) for t in targets],
        grid_spec=pltpu.PrefetchScalarGridSpec(
            num_scalar_prefetch=1, grid=(1,),
            in_specs=[pl.BlockSpec(memory_space=pltpu.HBM)] * n
            + [pl.BlockSpec(a.shape, lambda i, ix: (0, 0)) for a in arrays],
            out_specs=[pl.BlockSpec(memory_space=pltpu.HBM)] * n,
            scratch_shapes=[pltpu.SemaphoreType.DMA((len(arrays) * sems,))],
        ),
        input_output_aliases={1 + k: k for k in range(n)},
        compiler_params=pltpu.CompilerParams(vmem_limit_bytes=20 * MIB),
        cost_estimate=CHEAP,
        name="put",
    )(flags, *targets, *arrays)


def bits_of(axis):
    return lax.axis_size(axis).bit_length() - 1


def bit(step):
    return (lax.axis_index(step[0]) >> step[1]) & 1


def swap(value, step):
    axis, place = step
    size = lax.axis_size(axis)
    return lax.ppermute(value, axis, [(i, i ^ (1 << place)) for i in range(size)])


CORE = ("rep", 0)


def orders(*heads):
    axes = {"x": ("dp", 0), "y": ("rep", 1), "z": ("dp", 1)}
    rest = [("dp", b) for b in range(2, bits_of("dp"))] + [("rep", b) for b in range(2, bits_of("rep"))]
    return [[axes[a] for a in head] + rest for head in heads]


class Order:
    def __init__(self):
        self.last = None

    def tie(self, *values):
        if self.last is None:
            return values
        return lax.optimization_barrier((values, self.last))[0]

    def done(self, value):
        self.last = value


class Reduced:
    def __init__(self, order, steps, flags, where):
        self.order = order
        self.steps = steps
        self.flags = flags
        self.where = where
        self.count = len(steps[0])
        self.share = None

    def places(self, k):
        return [self.where[s[k]] for s in self.steps]

    def same(self, k):
        return all(s[k] == self.steps[0][k] for s in self.steps)

    def send(self, k, values):
        if len(values) == 1:
            return [swap(values[0], self.steps[0][k])]
        return [swap(v, s[k]) for v, s in zip(values, self.steps)]

    def begin(self, sends, keeps):
        self.k = 0
        self.kept = keeps
        self.got = self.send(0, sends)

    def fold(self):
        k = self.k + 1
        kept, got = self.order.tie(self.kept, self.got)
        if k == self.count:
            self.share = [last_call(self.flags, kept, got)]
            self.sizes = [v.shape[0] for v in kept]
            if any(v % SUB for v in self.sizes):
                cut = [sum(self.sizes[:c]) for c in range(len(kept))]
                self.share = [lax.slice_in_dim(self.share[0], a, a + n) for a, n in zip(cut, self.sizes)]
            self.order.done(self.share[0])
            self.k = k - 1
            return
        equal = len({v.shape[0] for v in kept}) == 1
        merged = self.same(k) and (equal or k == self.count - 1)
        if any(v.shape[0] % (2 * SUB) for v in kept):
            if len(got) < len(kept):
                size = kept[0].shape[0]
                got = [lax.slice_in_dim(got[0], c * size, (c + 1) * size) for c in range(len(kept))]
            total = [a + b for a, b in zip(kept, got)]
            index = [bit(s[k]) for s in self.steps]
            half = lambda v, i: lax.dynamic_slice_in_dim(v, i * (v.shape[0] // 2), v.shape[0] // 2, 0)
            sends = [half(v, 1 - i) for v, i in zip(total, index)]
            self.kept = [half(v, i) for v, i in zip(total, index)]
        else:
            sends, self.kept = fold_call(self.flags, self.places(k), kept, got, merged)
        self.order.done(self.kept[0])
        self.k = k
        self.got = self.send(k, sends)

    def finish(self):
        while self.share is None:
            self.fold()

    def back(self):
        self.got = self.send(self.k, self.share)
        while self.k > 3:
            self.widen()

    def wait(self):
        self.got = self.order.tie(*self.got)
        self.order.done(self.got)

    def widen(self):
        k = self.k
        share, got = self.order.tie(self.share, self.got)
        if any(v % SUB for v in self.sizes):
            pick = [bit(s[k]) == 0 for s in self.steps]
            self.share = [
                jnp.where(p, jnp.concatenate([v, g]), jnp.concatenate([g, v])) for p, v, g in zip(pick, share, got)
            ]
        else:
            self.share = widen_call(self.flags, self.places(k), self.sizes, share, got, self.same(k - 1))
        self.sizes = [2 * v for v in self.sizes]
        self.order.done(self.share[0])
        self.k = k - 1
        self.got = self.send(k - 1, self.share)

    def pieces(self, values, side):
        halves = [p + side for p in self.places(0)]
        values = self.order.tie(*values)
        return [(v, c, halves[c], 1) for c, v in enumerate(values)] + [
            (swap(v, CORE), c, halves[c], 2) for c, v in enumerate(values)
        ]

    def own(self):
        return self.pieces(self.share, 0)

    def arrived(self):
        return self.pieces(self.got, 1)


def spans_of(parts, low, high):
    found, start = [], 0
    for rows, target, row, col in parts:
        a, b = max(low, start), min(high, start + rows)
        if a < b:
            found.append((a - low, b - a, target, row + a - start, rows, col))
        start += rows
    return found


SEQUENCE = (
    "front", "scan0", "out0", "scan1", "mixed", "p0.f", "out1", "p0.f", "back01", "p0.f", "back00", "p0.e", "p0.b", "p1.f",
    "back11", "p1.f", "p0.w", "back10", "p1.f", "p0.w", "post0", "p1.e", "p1.b", "p0.w", "post1", "out2", "gn", "p0.d", "p0.own",
    "p1.w", "p2.f", "p2.f", "p2.f", "p1.w", "p0.got", "p2.e", "p2.b", "p1.w", "p1.own", "p2.w", "p2.w", "p1.got", "p2.w",
    "p2.own", "p2.got",
)
PARTS = 2


def shards(
    tokens, cotangent, lengths, norm_gain, in_weight, conv_weight, conv_bias, xproj_weight,
    dt_weight, dt_bias, decay_log, skip_gain, out_weight,
):
    tok, cot = tokens[0], cotangent[0]
    length, model = tok.shape
    taps, width = conv_weight.shape
    states = decay_log.shape[0]
    rank = dt_weight.shape[0]
    cols = xproj_weight.shape[1]
    row = lambda v: v.reshape(1, -1)
    core = bit(CORE).astype(jnp.int32)[None]
    dlog3 = decay_log.reshape(states, width // LANES, LANES)
    turned = xproj_weight.T
    sizes = [cols, rank, states, 2, taps + 1]
    used = -(-sum(sizes) // SUB) * SUB
    gain_rows = model // 2 // (WIDE // LANES)
    every = orders("xyz")[0]
    where = {s: 3 + 2 * k for k, s in enumerate(every)}
    marks = [lengths[0], core[0], 1 - core[0]]
    for s in every:
        marks += [bit(s), 1 - bit(s)]
    flags = jnp.stack([v.astype(jnp.int32) for v in marks])
    order = Order()
    tie, done = order.tie, order.done
    sets = [Reduced(order, orders(*heads), flags, where) for heads in (("xyz", "yxz"), ("xyz", "yxz"), ("xyz", "zxy", "yzx"))]
    low = model // 2
    third = 3 * model // 8
    heights = [[low, low]] * 2 + [[third, third, low]]
    parts = [[(WIDE // 2, 1, b * WIDE, 0), (low, 0, 0, width + b * WIDE)] for b in range(2)]
    parts.append([(low, 0, 0, 0), (low, 0, 0, WIDE), (used + gain_rows, 2, 0, 0)])
    state = {"targets": [blank((model, 2 * width)), blank((width, model)), blank((2 * (used + gain_rows), WIDE))]}
    scans, backs, posts, others, gains = {}, {}, {}, {}, {}

    def op_front():
        state["front"] = front(
            tok, cot, flags, row(norm_gain), in_weight, conv_weight, row(conv_bias), turned
        )
        _, send, og, _, _, mp = state["front"]
        state["og"] = swap(og, CORE)
        state["normed"] = swap(send, CORE)
        done(mp)

    def op_scan(b):
        normed, _, og, _, act, mp = state["front"]
        mp, = tie(mp)
        scans[b] = scan(
            b, flags, mp, normed, og, act, in_weight, out_weight, dt_weight, row(dt_bias), dlog3, row(skip_gain)
        )
        done(scans[b][0])
        others[b] = (swap(scans[b][2], CORE), swap(scans[b][3], CORE))

    def op_out(b):
        normed, _, og, _, _, _ = state["front"]
        if b < 2:
            own = [(scans[b][0], og), (normed, scans[b][1])]
            one, two = others[b]
            low = model // 2
            other = [
                ([(one, 0, low)], [(state["og"], 0, model)]),
                ([(state["normed"], 0, low)], [(one, low, one.shape[1] - low), (two, 0, two.shape[1])]),
            ]
            small = ()
        else:
            own = [(normed, posts[q][0]) for q in range(2)]
            other = [([(state["normed"], 0, model // 2)], [(others[2 + q], 0, WIDE)]) for q in range(2)]
            small = (posts[0][1], posts[1][1], others["small"])
        own, arrays, small = tie(own, [[[p[0] for p in pieces] for pieces in pair] for pair in other], small)
        other = [
            [[(a, *p[1:]) for a, p in zip(array, pieces)] for array, pieces in zip(pair, cut)]
            for pair, cut in zip(arrays, other)
        ]
        bits = sets[b].places(0)
        if b < 2:
            got = outer(own, other, heights[b], flags, bits, in_weight, ((1, width + b * WIDE),))
            gains[b] = got[-1]
        else:
            got = outer(
                own, other, heights[b], flags, bits, in_weight, ((0, 0), (1, WIDE)), (gains[0], gains[1]), small
            )
        done(got[1])
        chunks = len(heights[b])
        sets[b].begin(got[0 : 2 * chunks : 2], got[1 : 2 * chunks : 2])

    def op_back(b, part):
        _, _, _, _, act, mp = state["front"]
        mp, = tie(mp)
        carry = backs[b, part + 1][4] if part < PARTS - 1 else None
        backs[b, part] = back(
            b, part, PARTS, mp, act, scans[b][5], scans[b][4], scans[b][6], dt_weight, dlog3, carry
        )
        done(backs[b, part][0])

    def op_post(b):
        _, _, _, inner, act, _ = state["front"]
        parts, every = tie([backs[b, k] for k in range(PARTS)], [backs[q, k][1:4:2] for q in range(2) for k in range(PARTS)])
        posts[b] = post(
            b, used, scans[b][4], act, inner, turned, conv_weight, row(conv_bias), row(skip_gain), parts[0][4], decay_log,
            [p[0] for p in parts], [p[2] for p in parts], [p[5] for p in parts], [v[0] for v in every], [v[1] for v in every],
        )
        done(posts[b][0])
        others[2 + b] = swap(posts[b][0], CORE)
        if b == 1:
            others["small"] = swap(jnp.where(core[0] == 0, posts[1][1], posts[0][1]), CORE)

    def op_gn():
        parts = tie(posts[0][0], posts[1][0], scans[0][1], scans[1][1])
        grad_projected = jnp.concatenate([v.astype(BF16) for v in parts], axis=1)
        grad_normed = dot(grad_projected, in_weight, ((1,), (1,)))
        x = tok.astype(F32)
        inv = lax.rsqrt(jnp.mean(x * x, axis=1, keepdims=True) + EPS)
        unit = x * inv
        grad_unit = grad_normed * norm_gain
        state["grad_tokens"] = cot.astype(F32) + inv * (
            grad_unit - unit * jnp.mean(grad_unit * unit, axis=1, keepdims=True)
        )
        done(state["grad_tokens"])

    def op_mixed():
        b0, b1 = tie(scans[0][0], scans[1][0])
        live = (jnp.arange(length) < lengths[0])[:, None]
        total = dot(jnp.concatenate([b0, b1], axis=1), out_weight)
        state["mixed"] = (tok.astype(F32) + jnp.where(live, total, 0.0)).astype(BF16)
        done(state["mixed"])

    def op_put(p, pieces):
        arrays, targets = tie([v[0] for v in pieces], state["targets"])
        pieces = [(a,) + v[1:] for a, v in zip(arrays, pieces)]
        state["targets"] = put(targets, pieces, parts[p], heights[p], flags)
        done(state["targets"][0])

    for name in SEQUENCE:
        if name[0] == "p" and name[2] == ".":
            p, what = int(name[1]), name[3:]
            if what == "f":
                sets[p].fold()
            elif what == "e":
                sets[p].finish()
            elif what == "b":
                sets[p].back()
            elif what == "w":
                sets[p].widen()
            elif what == "d":
                sets[p].wait()
            else:
                op_put(p, sets[p].own() if what == "own" else sets[p].arrived())
        elif name[:4] == "back":
            op_back(int(name[4]), int(name[5]))
        elif name[-1] in "012":
            {"scan": op_scan, "out": op_out, "post": op_post}[name[:-1]](int(name[-1]))
        else:
            {"front": op_front, "gn": op_gn, "mixed": op_mixed}[name]()

    grad_in, grad_out, small = state["targets"]
    lines = small.reshape(2, used + gain_rows, WIDE)
    grad_gain = jnp.sum(lines[:, used:].reshape(2, gain_rows, WIDE // LANES, LANES), axis=3)
    grad_gain = jnp.swapaxes(grad_gain, 1, 2).reshape(-1) / norm_gain
    small = jnp.concatenate([lines[0, :used], lines[1, :used]], axis=1)
    ends = [sum(sizes[: i + 1]) for i in range(len(sizes))]
    cut = [small[e - n : e] for e, n in zip(ends, sizes)]
    return (
        state["mixed"][None], state["grad_tokens"][None],
        grad_gain, grad_in, cut[4][:taps], cut[4][taps], cut[0].T, cut[1], cut[3][0],
        cut[2], cut[3][1], grad_out,
    )


def solution(mesh):
    rows = P(("dp", "rep"), None, None)
    return jax.shard_map(
        shards,
        mesh=mesh,
        in_specs=(rows, rows, P(("dp", "rep"))) + (P(),) * 10,
        out_specs=(rows, rows) + (P(),) * 10,
        check_vma=False,
    )
```
